32 devices in a mesh: dp: 8 (over z, core), fsdp: 4 (over y, x).
Axes of the slice: x: 2, y: 2, z: 4, core: 2. Of those that a mesh axis runs over, the one named last changes fastest.
Arguments:
- tokens: bfloat16 [16384, 768], P(('dp', 'fsdp')), may hold values from -8 to 8
- qkv_weight: bfloat16 [768, 2304], P(('dp', 'fsdp')), may hold values from -0.21875 to 0.21875
- proj_weight: bfloat16 [768, 768], P(('dp', 'fsdp')), may hold values from -0.4375 to 0.4375
- ffn_in_weight: bfloat16 [768, 3072], P(('dp', 'fsdp')), may hold values from -0.21875 to 0.21875
- ffn_out_weight: bfloat16 [3072, 768], P(('dp', 'fsdp')), may hold values from -0.109375 to 0.109375
- bias_rows: bfloat16 [6, 768], P(None, ('dp', 'fsdp')), may hold values from -1.796875 to 1.796875
- ffn_bias: bfloat16 [3072], P(('dp', 'fsdp')), may hold values from -1.796875 to 1.796875
- norm_gains: bfloat16 [2, 768], P(None, ('dp', 'fsdp')), may hold values from 0.5 to 1.5
- buckets: int32 [32, 8], P(('dp', 'fsdp')), may hold values from 0 to 512, as said below
- padding: int32 [16384], P(('dp', 'fsdp')), may hold values from 0 to 1, as said below
- dropout: int32 [2, 2, 16384, 768], P(None, None, ('dp', 'fsdp')), may hold values 0 or 1
Outputs:
- hidden_out: bfloat16 [2, 16384, 768], P(None, ('dp', 'fsdp'))
- loss_mean: float32 [], replicated
- grad_tokens: float32 [16384, 768], P(('dp', 'fsdp'))
- grad_qkv_weight: float32 [768, 2304], P(('dp', 'fsdp'))
- grad_proj_weight: float32 [768, 768], P(('dp', 'fsdp'))
- grad_ffn_in: float32 [768, 3072], P(('dp', 'fsdp'))
- grad_ffn_out: float32 [3072, 768], P(('dp', 'fsdp'))
- grad_bias_rows: float32 [6, 768], P(None, ('dp', 'fsdp'))
- grad_ffn_bias: float32 [3072], P(('dp', 'fsdp'))
- grad_norm_gains: float32 [2, 768], P(None, ('dp', 'fsdp'))
The draws below stay inside these ranges and needn't reach their ends.
Inputs may be any that keep to these rules, and one draw needn't show every extreme that they name: `buckets`: row g lists device g's sentences in the order of their rows, then zeros. Each length is 512 // 8 times 1, 2, 4 or 8, a sentence starts at a multiple of its own length, and a row's lengths add up to 512. One device holds a single sentence of 512 rows and another holds 8 sentences of 64 rows. `padding`: within each sentence the ones form a prefix longer than half its bucket length; a sentence's first row is always 1.
All inputs are finite; a program needn't handle non-finite values. No bound on the sum of `dropout` on one device may be relied on, other than what follows from the above.
Results may differ from the reference program's by a relative error of at most 0.012.
The reference program's roundings to bfloat16 on the way count: a program that leaves them out, or rounds other values in their place, can miss the bound.
Values may be sent and summed in bfloat16 or wider, within the bound.
A program may use at most 256 MiB of HBM per device.

```python
import jax
import jax.numpy as jnp
import numpy as np
from jax import lax

D = 768
H = 12
HD = 64
FF = 3072
ROWS = 512
SLOTS = 8
GROUPS = 32
TOKENS = 16384


def sentence_draw(key):
    split_key = jax.random.fold_in(key, 11)
    length_key = jax.random.fold_in(key, 12)
    unit_rows = ROWS // SLOTS
    split_bits = jax.random.randint(split_key, (GROUPS, 7), 0, 2)
    device_ids = jnp.arange(GROUPS, dtype=jnp.int32)[:, None]
    split_bits = jnp.where(device_ids == 0, 0, jnp.where(device_ids == 1, 1, split_bits))
    unit_table = np.arange(8)
    top_bit = split_bits[:, np.zeros(8, np.int32)]
    half_bit = split_bits[:, 1 + unit_table // 4]
    quarter_bit = split_bits[:, 3 + unit_table // 2]
    span_units = jnp.where(top_bit == 0, 8, jnp.where(half_bit == 0, 4, jnp.where(quarter_bit == 0, 2, 1))).astype(jnp.int32)
    unit_index = jnp.broadcast_to(jnp.arange(8, dtype=jnp.int32)[None, :], (GROUPS, 8))
    begins = (unit_index % span_units == 0).astype(jnp.int32)
    ordering = jnp.argsort((1 - begins) * 8 + unit_index, axis=1)
    buckets = jnp.take_along_axis(span_units * begins * unit_rows, ordering, axis=1)
    first_unit = unit_index - unit_index % span_units
    extent = span_units * unit_rows
    length_draws = jax.random.randint(length_key, (GROUPS, 8), 0, 1 << 20)
    start_draw = jnp.take_along_axis(length_draws, first_unit, axis=1)
    real_length = extent // 2 + 1 + start_draw % (extent - extent // 2)
    row_offset = jnp.broadcast_to(jnp.arange(ROWS, dtype=jnp.int32)[None, :], (GROUPS, ROWS))
    row_unit = row_offset // unit_rows
    row_real = jnp.take_along_axis(real_length, row_unit, axis=1)
    row_first = jnp.take_along_axis(first_unit, row_unit, axis=1)
    padding = (row_offset - row_first * unit_rows < row_real).astype(jnp.int32).reshape(GROUPS * ROWS)
    return (buckets.astype(jnp.int32), padding)


def draw_buckets(key, part):
    layout = sentence_draw(key)
    return layout[0]


def draw_padding(key, part):
    layout = sentence_draw(key)
    return layout[1]


def draw_tokens(key, part):
    key = jax.random.fold_in(key, 3)
    keys = jax.random.split(key, 4)
    common = jax.random.normal(keys[0], (D,), jnp.float32)
    directions = jax.random.normal(keys[1], (4, D), jnp.float32)
    mixing = 0.35 * jax.random.normal(keys[2], (TOKENS, 4), jnp.float32)
    noise = 0.6 * jax.random.normal(keys[3], (TOKENS, D), jnp.float32)
    values = common[None, :] + noise
    values = values + mixing[:, 0:1] * directions[0][None, :] + mixing[:, 1:2] * directions[1][None, :]
    values = values + mixing[:, 2:3] * directions[2][None, :] + mixing[:, 3:4] * directions[3][None, :]
    return jnp.clip(values, -8.0, 8.0).astype(jnp.bfloat16)


def plant(drawn, stream_key, low, high):
    longest = drawn.shape.index(max(drawn.shape))
    spots = []
    for shift in (0, 1):
        where = [jax.random.randint(jax.random.fold_in(stream_key, axis), (), 0, length) for axis, length in enumerate(drawn.shape)]
        where[longest] = (where[longest] + shift) % drawn.shape[longest]
        spots.append(tuple(where))
    return drawn.at[spots[0]].set(low).at[spots[1]].set(high)


def steps_of(rng, dims, cuts, least, high):
    gain = 1.0
    for axis_at, blocks in cuts:
        draws = jax.random.uniform(jax.random.fold_in(jax.random.fold_in(rng, 6), axis_at), (blocks,), jnp.float32, least / len(cuts), high / len(cuts))
        gain = gain * jnp.repeat(jnp.exp(draws), dims[axis_at] // blocks).reshape((-1,) + (1,) * (len(dims) - 1 - axis_at))
    return gain


def centred(rng, shape, scale, most, shards=(), kind=jnp.bfloat16):
    values = scale * jax.random.normal(rng, shape, jnp.float32)
    if shards:
        values = values * steps_of(rng, shape, shards, -0.22, 0.18)
    return jnp.clip(values, -most, most).astype(kind)


def setup_inputs(seed: int = 0) -> dict:
    streams_of = jax.random.split(jax.random.key(seed), 12)
    tokens = draw_tokens(jax.random.fold_in(streams_of[11], 71), 0)
    qkv_weight = centred(streams_of[1], (D, 3 * D), D ** -0.5, 0.21875, ((0, 32),))
    proj_weight = centred(streams_of[2], (D, D), (D // 4) ** -0.5, 0.4375, ((0, 32),))
    ffn_in_weight = centred(streams_of[3], (D, FF), D ** -0.5, 0.21875, ((0, 32),))
    ffn_out_weight = centred(streams_of[4], (FF, D), FF ** -0.5, 0.109375, ((0, 32),))
    bias_rows = centred(streams_of[5], (6, D), 0.3, 1.796875, ((1, 32),))
    ffn_bias = centred(streams_of[6], (FF,), 0.3, 1.796875, ((0, 32),))
    norm_gains = jnp.clip(1.0 + 0.1 * jax.random.normal(streams_of[7], (2, D), jnp.float32), 0.5, 1.5).astype(jnp.bfloat16)
    buckets = draw_buckets(jax.random.fold_in(streams_of[11], 71), 0)
    padding = draw_padding(jax.random.fold_in(streams_of[11], 71), 0)
    dropout = plant((jax.random.randint(streams_of[10], (2, 2, TOKENS, D), 0, 10) < 9).astype(jnp.int32), jax.random.fold_in(streams_of[10], 1), 0, 1)
    return dict(tokens=tokens, qkv_weight=qkv_weight, proj_weight=proj_weight, ffn_in_weight=ffn_in_weight, ffn_out_weight=ffn_out_weight, bias_rows=bias_rows, ffn_bias=ffn_bias, norm_gains=norm_gains, buckets=buckets, padding=padding, dropout=dropout)


NEGATIVE = -1e+30
NORM_EPSILON = 1e-12
UNIT_EPSILON = 1e-06
SOFTMAX_TEMP = 0.05
KEEP_SCALE = 1.0 / 0.9
FULL_PRECISION = lax.Precision.HIGHEST

@jax.custom_vjp
def low(v):
    return lax.optimization_barrier(v.astype(jnp.bfloat16)).astype(jnp.float32)

@jax.custom_vjp
def reduced_backward(v):
    return v

def low_keep(v):
    return (low(v), None)

def low_pass(kept, grad):
    return (grad,)

def back_keep(v):
    return (v, None)

def back_low(kept, grad):
    return (low(grad),)
low.defvjp(low_keep, low_pass)
reduced_backward.defvjp(back_keep, back_low)

def layer_norm(inputs, gain_vec, shift_vec):
    centre = inputs - lax.optimization_barrier(jnp.mean(inputs, axis=-1, keepdims=True))
    spread = lax.optimization_barrier(jnp.mean(centre * centre, axis=-1, keepdims=True))
    return centre * lax.rsqrt(spread + NORM_EPSILON) * gain_vec + shift_vec

def normalize(inputs):
    return inputs * lax.rsqrt(lax.optimization_barrier(jnp.sum(inputs * inputs, axis=-1, keepdims=True)) + UNIT_EPSILON)

def sentence_layout(bucket_row, pad_row):
    row_ids = jnp.arange(ROWS, dtype=jnp.int32)
    starts = (jnp.cumsum(bucket_row) - bucket_row).astype(jnp.int32)
    used = bucket_row > 0
    member = (row_ids[:, None] >= starts[None, :]) & used[None, :]
    sentence = lax.optimization_barrier(jnp.sum(member.astype(jnp.int32), axis=1))
    allowed = (sentence[:, None] == sentence[None, :]) & (pad_row[None, :] > 0)
    select = ((row_ids[None, :] == starts[:, None]) & used[:, None]).astype(jnp.float32)
    return (allowed, select)

def block_forward(params, token_rows, keep_block, bucket_row, pad_row):
    qkv_weight, proj_weight, ffn_in_weight, ffn_out_weight, bias_rows, ffn_bias, norm_gains = params
    allowed, select = sentence_layout(bucket_row, pad_row)
    projected = jnp.dot(token_rows, qkv_weight, precision=FULL_PRECISION)
    zero_row = jnp.zeros_like(bias_rows[0])
    qkv = low(reduced_backward(projected + jnp.concatenate([bias_rows[0], zero_row, bias_rows[1]])))
    head_view = qkv.reshape(ROWS, 3, H, HD)
    queries, key_rows, value_rows = (head_view[:, 0], head_view[:, 1], head_view[:, 2])
    scores = jnp.einsum('qhd,khd->hqk', queries, key_rows, precision=FULL_PRECISION) * HD ** (-0.5)
    scores = reduced_backward(scores)
    scores = jnp.where(allowed[None], scores, NEGATIVE)
    peak = lax.optimization_barrier(jnp.max(scores, axis=-1, keepdims=True))
    exp_scores = jnp.exp(scores - peak)
    probability = low(exp_scores / lax.optimization_barrier(jnp.sum(exp_scores, axis=-1, keepdims=True)))
    context = jnp.einsum('hqk,khd->qhd', probability, value_rows, precision=FULL_PRECISION).reshape(ROWS, D)
    context = low(reduced_backward(context))
    branch = reduced_backward(jnp.dot(context, proj_weight, precision=FULL_PRECISION) + bias_rows[2])
    keep_mask = keep_block.astype(jnp.float32)
    mixed_one = token_rows[None] + branch[None] * keep_mask[:, 0] * KEEP_SCALE
    normed = layer_norm(mixed_one, norm_gains[0], bias_rows[3])
    preact = reduced_backward(jnp.einsum('vrd,df->vrf', low(normed), ffn_in_weight, precision=FULL_PRECISION) + ffn_bias)
    activation = low(jax.nn.gelu(preact, approximate=False))
    ffn_out = reduced_backward(jnp.einsum('vrf,fd->vrd', activation, ffn_out_weight, precision=FULL_PRECISION) + bias_rows[4])
    final_rows = layer_norm(normed + ffn_out * keep_mask[:, 1] * KEEP_SCALE, norm_gains[1], bias_rows[5])
    cls_rows = jnp.einsum('sr,vrd->vsd', select, final_rows, precision=FULL_PRECISION)
    return (final_rows, cls_rows)

def forward(params, tokens_f, dropout, buckets, padding):
    checked = jax.checkpoint(block_forward)

    def scan_step(carried, group_id):
        token_rows = lax.dynamic_slice_in_dim(tokens_f, group_id * ROWS, ROWS, 0)
        keep_block = lax.dynamic_slice_in_dim(dropout, group_id * ROWS, ROWS, 2)
        pad_row = lax.dynamic_slice_in_dim(padding, group_id * ROWS, ROWS, 0)
        bucket_row = buckets[group_id]
        final_rows, cls_rows = checked(params, token_rows, keep_block, bucket_row, pad_row)
        return (carried, (final_rows, cls_rows))
    _, (finals, classes) = lax.scan(scan_step, jnp.zeros((), jnp.float32), jnp.arange(GROUPS, dtype=jnp.int32))
    hidden_out = finals.transpose(1, 0, 2, 3).reshape(2, TOKENS, D)
    used_slot = (buckets > 0).reshape(GROUPS * SLOTS).astype(jnp.float32)
    first_view = classes[:, 0].reshape(GROUPS * SLOTS, D)
    second_view = classes[:, 1].reshape(GROUPS * SLOTS, D)
    first_normalized = low(normalize(first_view))
    second_normalized = low(normalize(second_view))
    similarity_logits = reduced_backward(jnp.dot(first_normalized, second_normalized.T, precision=FULL_PRECISION) / SOFTMAX_TEMP)
    similarity_logits = jnp.where(used_slot[None, :] > 0, similarity_logits, NEGATIVE)
    peak = lax.optimization_barrier(jnp.max(similarity_logits, axis=-1, keepdims=True))
    log_total = peak[:, 0] + jnp.log(lax.optimization_barrier(jnp.sum(jnp.exp(similarity_logits - peak), axis=-1)))
    positive = jnp.diagonal(similarity_logits)
    loss_sum = jnp.sum((log_total - positive) * used_slot)
    return (loss_sum, (hidden_out, loss_sum / jnp.sum(used_slot)))

def reference(tokens, qkv_weight, proj_weight, ffn_in_weight, ffn_out_weight, bias_rows, ffn_bias, norm_gains, buckets, padding, dropout):
    params = (qkv_weight.astype(jnp.float32), proj_weight.astype(jnp.float32), ffn_in_weight.astype(jnp.float32), ffn_out_weight.astype(jnp.float32), bias_rows.astype(jnp.float32), ffn_bias.astype(jnp.float32), norm_gains.astype(jnp.float32))
    tokens_f = tokens.astype(jnp.float32)

    def objective(weights_in, tokens_in):
        return forward(weights_in, tokens_in, dropout, buckets, padding)
    loss_sum, pullback, (hidden_full, loss_mean) = jax.vjp(objective, params, tokens_f, has_aux=True)
    grad_params, grad_tokens = pullback(jnp.ones((), jnp.float32))
    hidden_out = hidden_full.astype(jnp.bfloat16)
    return (hidden_out, loss_mean, grad_tokens, grad_params[0], grad_params[1], grad_params[2], grad_params[3], grad_params[4], grad_params[5], grad_params[6])
```

```python
import jax
import jax.numpy as jnp
from jax import lax
from jax.sharding import PartitionSpec as P

H = 12
HD = 64

NEGATIVE = -1e30
NORM_EPSILON = 1e-12
UNIT_EPSILON = 1e-06
SOFTMAX_TEMP = 0.05
KEEP_SCALE = 1.0 / 0.9
FULL_PRECISION = lax.Precision.HIGHEST
AXES = ("dp", "fsdp")
BF = jnp.bfloat16
F32 = jnp.float32


def dot(a, b, dims=((1,), (0,))):
    return lax.dot_general(a, b, (dims, ((), ())), preferred_element_type=F32)


def layer_norm(inputs, gain_vec, shift_vec):
    centre = inputs - jnp.mean(inputs, axis=-1, keepdims=True)
    spread = jnp.mean(centre * centre, axis=-1, keepdims=True)
    return centre * lax.rsqrt(spread + NORM_EPSILON) * gain_vec + shift_vec


def normalize(inputs):
    return inputs * lax.rsqrt(jnp.sum(inputs * inputs, axis=-1, keepdims=True) + UNIT_EPSILON)


def exact_gelu(inputs):
    return jax.nn.gelu(inputs, approximate=False)


def sentence_layout(bucket_row, pad_row, rows_here):
    row_ids = jnp.arange(rows_here, dtype=jnp.int32)
    starts = jnp.cumsum(bucket_row) - bucket_row
    used = bucket_row > 0
    member = (row_ids[:, None] >= starts[None, :]) & used[None, :]
    sentence = jnp.sum(member.astype(jnp.int32), axis=1)
    allowed = (sentence[:, None] == sentence[None, :]) & (pad_row[None, :] > 0)
    select = ((row_ids[None, :] == starts[:, None]) & used[:, None]).astype(jnp.float32)
    slot_allowed = (
        (sentence[None, :] == jnp.arange(1, bucket_row.shape[0] + 1)[:, None])
        & used[:, None]
        & (pad_row[None, :] > 0)
    )
    return (allowed, select, slot_allowed)


def gather(x, axis=0):
    return lax.all_gather(x, AXES, axis=axis, tiled=True)


def all_to_all(x):
    return lax.all_to_all(x, AXES, split_axis=0, concat_axis=0, tiled=True)


def per_device(
    tokens,
    qkv_weight,
    proj_weight,
    ffn_in_weight,
    ffn_out_weight,
    bias_rows,
    ffn_bias,
    norm_gains,
    buckets,
    padding,
    dropout,
):
    rows_here, width = tokens.shape
    slots = buckets.shape[1]
    hidden = ffn_in_weight.shape[1]
    small = bias_rows.shape[1]
    devices = width // small
    hidden_small = hidden // devices
    me = lax.axis_index(AXES)
    score_scale = HD ** (-0.5)
    used_slot = (buckets[0] > 0).astype(BF)

    params = jnp.concatenate(
        [bias_rows.reshape(-1), norm_gains.reshape(-1), ffn_bias, used_slot]
    )
    params_all = gather(params[None])
    qp = gather(jnp.concatenate([qkv_weight, proj_weight], axis=1))
    qkv_full, proj_full = qp[:, : 3 * width], qp[:, 3 * width :]
    in_full = gather(ffn_in_weight)
    out_full = gather(ffn_out_weight)
    rows8 = params_all[:, : 8 * small].reshape(devices, 8, small).transpose(1, 0, 2)
    rows8 = rows8.reshape(8, width).astype(F32)
    bias_f, gain_f = rows8[:6], rows8[6:]
    ffn_bias_f = params_all[:, 8 * small : 8 * small + hidden_small].reshape(-1).astype(F32)
    used_all = params_all[:, 8 * small + hidden_small :].reshape(-1)

    allowed, select, slot_allowed = sentence_layout(buckets[0], padding, rows_here)
    select_low = select.astype(BF)
    zero_row = jnp.zeros((width,), F32)
    qkv = (dot(tokens, qkv_full) + jnp.concatenate([bias_f[0], zero_row, bias_f[1]])).astype(BF)
    head_view = qkv.reshape(rows_here, 3, H, HD)
    queries, key_rows, value_rows = (head_view[:, 0], head_view[:, 1], head_view[:, 2])

    scores = (
        jnp.einsum("qhd,khd->hqk", queries, key_rows, preferred_element_type=F32) * score_scale
    )
    scores = jnp.where(allowed[None], scores, NEGATIVE)
    exp_scores = jnp.exp(scores - jnp.max(scores, axis=-1, keepdims=True))
    probability = (exp_scores / jnp.sum(exp_scores, axis=-1, keepdims=True)).astype(BF)
    context = jnp.einsum("hqk,khd->qhd", probability, value_rows, preferred_element_type=F32)
    context = context.reshape(rows_here, width).astype(BF)
    branch = dot(context, proj_full) + bias_f[2]
    keep_mask = dropout.astype(F32)
    mixed_one = tokens.astype(F32)[None] + branch[None] * keep_mask[:, 0] * KEEP_SCALE
    normed = layer_norm(mixed_one, gain_f[0], bias_f[3])
    normed_low = normed.astype(BF)
    preact = dot(normed_low.reshape(-1, width), in_full) + ffn_bias_f
    activation = exact_gelu(preact).astype(BF)
    ffn_out = (dot(activation, out_full) + bias_f[4]).reshape(normed.shape)
    mixed_two = normed + ffn_out * keep_mask[:, 1] * KEEP_SCALE
    hidden_out = layer_norm(mixed_two, gain_f[1], bias_f[5]).astype(BF)

    tokens_s = dot(select_low, tokens)
    qkv_s = dot(select_low, qkv).astype(BF)
    queries_s = qkv_s[:, :width].reshape(slots, H, HD)
    scores_s = (
        jnp.einsum("shd,khd->hsk", queries_s, key_rows, preferred_element_type=F32) * score_scale
    )
    scores_s = jnp.where(slot_allowed[None], scores_s, NEGATIVE)
    peak_s = jnp.max(scores_s, axis=-1, keepdims=True)
    exp_s = jnp.exp(scores_s - peak_s) * slot_allowed[None].astype(F32)
    probability_f = exp_s / jnp.maximum(jnp.sum(exp_s, axis=-1, keepdims=True), 1e-30)
    probability_s = probability_f.astype(BF)
    context_s = dot(select_low, context).astype(BF)
    branch_s = dot(context_s, proj_full) + bias_f[2]
    keep_s = jnp.einsum(
        "sr,vbrd->vbsd", select_low, dropout.astype(BF), preferred_element_type=F32
    )
    mixed_s = tokens_s[None] + branch_s[None] * keep_s[:, 0] * KEEP_SCALE
    normed_s, first_back = jax.vjp(layer_norm, mixed_s, gain_f[0], bias_f[3])
    normed_s_low = normed_s.astype(BF).reshape(2 * slots, width)
    preact_s = dot(normed_s_low, in_full) + ffn_bias_f
    activation_sf, gelu_back = jax.vjp(exact_gelu, preact_s)
    activation_s = activation_sf.astype(BF)
    ffn_out_s = (dot(activation_s, out_full) + bias_f[4]).reshape(normed_s.shape)
    mixed_two_s = normed_s + ffn_out_s * keep_s[:, 1] * KEEP_SCALE
    final_s, second_back = jax.vjp(layer_norm, mixed_two_s, gain_f[1], bias_f[5])
    used_f = used_slot.astype(F32)
    final_s = final_s * used_f[None, :, None]
    unit_s, unit_back = jax.vjp(normalize, final_s)
    unit_low = unit_s.astype(BF)

    unit_all = gather(unit_low.reshape(1, 2, slots, width))
    unit_0 = unit_all[:, 0].reshape(-1, width)
    unit_1 = unit_all[:, 1].reshape(-1, width)
    logits = dot(unit_0, unit_1, ((1,), (1,))) / SOFTMAX_TEMP
    logits = jnp.where(used_all[None, :] > 0, logits, NEGATIVE)
    total = unit_0.shape[0]
    ids = jnp.arange(total, dtype=jnp.int32)
    diagonal = ids[:, None] == ids[None, :]
    logit_peak = jnp.max(logits, axis=-1, keepdims=True)
    logit_total = logit_peak[:, 0] + jnp.log(jnp.sum(jnp.exp(logits - logit_peak), axis=-1))
    positive = jnp.sum(jnp.where(diagonal, logits, 0.0), axis=1)
    used_all_f = used_all.astype(F32)
    loss_mean = jnp.sum((logit_total - positive) * used_all_f) / jnp.sum(used_all_f)
    soft = jnp.exp(logits - logit_total[:, None])
    logit_gradient = ((soft - diagonal.astype(F32)) * used_all_f[:, None]).astype(BF)
    mine_rows = lax.dynamic_slice_in_dim(logit_gradient, me * slots, slots, 0)
    mine_columns = lax.dynamic_slice_in_dim(logit_gradient, me * slots, slots, 1)
    grad_unit = jnp.stack(
        [dot(mine_rows, unit_1), dot(mine_columns, unit_0, ((0,), (0,)))]
    ) / SOFTMAX_TEMP
    (grad_final,) = unit_back(grad_unit)
    grad_final = grad_final * used_f[None, :, None]
    grad_mixed_two, grad_gain_two, grad_shift_two = second_back(grad_final)
    grad_ffn = (grad_mixed_two * keep_s[:, 1] * KEEP_SCALE).astype(BF).reshape(-1, width)
    grad_shift_out = jnp.sum(grad_ffn.astype(F32), axis=0)
    grad_act = dot(grad_ffn, out_full, ((1,), (1,)))
    (grad_preact_f,) = gelu_back(grad_act)
    grad_preact = grad_preact_f.astype(BF)
    grad_hidden_bias = jnp.sum(grad_preact.astype(F32), axis=0)
    grad_normed = dot(grad_preact, in_full, ((1,), (1,))).reshape(normed_s.shape) + grad_mixed_two
    grad_mixed, grad_gain_one, grad_shift_one = first_back(grad_normed)
    grad_branch = jnp.sum(grad_mixed * keep_s[:, 0] * KEEP_SCALE, axis=0).astype(BF)
    grad_shift_proj = jnp.sum(grad_branch.astype(F32), axis=0)
    grad_context = dot(grad_branch, proj_full, ((1,), (1,))).astype(BF)
    grad_context_h = grad_context.reshape(slots, H, HD)
    grad_probs = jnp.einsum(
        "shd,khd->hsk", grad_context_h, value_rows, preferred_element_type=F32
    )
    inner = jnp.sum(probability_f * grad_probs, axis=-1, keepdims=True)
    grad_scores = (probability_f * (grad_probs - inner)).astype(BF)
    grad_queries = (
        (jnp.einsum("hsk,khd->shd", grad_scores, key_rows, preferred_element_type=F32) * score_scale)
        .reshape(slots, width)
        .astype(BF)
    )
    pairs = jnp.concatenate([grad_scores, probability_s], axis=0).reshape(2 * H * slots, rows_here)
    token_sums = dot(pairs, tokens).astype(BF)
    key_factor = (queries_s.astype(F32) * score_scale).astype(BF)
    back_w = qkv_full.reshape(width, 3, H, HD)
    through = jnp.concatenate(
        [
            jnp.einsum("shd,whd->hsw", key_factor, back_w[:, 1], preferred_element_type=F32),
            jnp.einsum("shd,whd->hsw", grad_context_h, back_w[:, 2], preferred_element_type=F32),
        ],
        axis=0,
    ).reshape(2 * H * slots, width)
    start_grad = jnp.sum(grad_mixed, axis=0) + dot(
        grad_queries, qkv_full[:, :width], ((1,), (1,))
    )
    grad_tokens = dot(pairs, through.astype(BF), ((0,), (0,))) + lax.dot_general(
        select, start_grad, (((0,), (0,)), ((), ())), precision=FULL_PRECISION
    )
    value_sum = jnp.sum(probability_s.astype(F32), axis=-1).T
    grad_shift_value = jnp.sum(value_sum[:, :, None] * grad_context_h.astype(F32), axis=0).reshape(-1)
    grad_shift_query = jnp.sum(grad_queries.astype(F32), axis=0)

    wide = gather(jnp.concatenate([grad_ffn, grad_preact], axis=1))
    gffn_all, gpre_all = wide[:, :width], wide[:, width:]
    narrow = gather(
        jnp.concatenate([grad_branch, key_factor.reshape(slots, width), grad_context, grad_queries], axis=1)
    )
    gbranch_all = narrow[:, :width]
    key_all = narrow[:, width : 2 * width].reshape(-1, H, HD)
    gctx_all = narrow[:, 2 * width : 3 * width].reshape(-1, H, HD)
    gq_all = narrow[:, 3 * width :]

    def cut(x, n):
        return x.reshape(x.shape[0], devices, n).transpose(1, 0, 2).reshape(devices, -1)

    bias_sums = jnp.concatenate(
        [
            jnp.stack(
                [
                    grad_shift_query,
                    grad_shift_value,
                    grad_shift_proj,
                    grad_shift_one,
                    grad_shift_out,
                    grad_shift_two,
                    grad_gain_one,
                    grad_gain_two,
                ]
            )
            .reshape(8, devices, small)
            .transpose(1, 0, 2)
            .reshape(devices, -1),
            grad_hidden_bias.reshape(devices, -1),
        ],
        axis=1,
    )
    high = bias_sums.astype(BF)
    lower = (bias_sums - high.astype(F32)).astype(BF)
    pieces = [
        cut(activation_s, hidden_small),
        cut(normed_s_low, small),
        cut(context_s, small),
        cut(tokens_s.astype(BF), small),
        cut(token_sums, small),
        high,
        lower,
    ]
    sizes = [p.shape[1] for p in pieces]
    received = all_to_all(jnp.concatenate(pieces, axis=1))
    ends = []
    at = 0
    for n in sizes:
        ends.append(received[:, at : at + n])
        at += n
    act_r = ends[0].reshape(-1, hidden_small)
    normed_r = ends[1].reshape(-1, small)
    ctx_r = ends[2].reshape(-1, small)
    tok_r = ends[3].reshape(-1, small)
    sums_r = ends[4].reshape(devices, 2, H, slots, small)
    bias_r = jnp.sum(ends[5].astype(F32) + ends[6].astype(F32), axis=0)

    grad_out_weight = dot(act_r, gffn_all, ((0,), (0,)))
    grad_in_weight = dot(normed_r, gpre_all, ((0,), (0,)))
    grad_proj = dot(ctx_r, gbranch_all, ((0,), (0,)))
    grad_q = dot(tok_r, gq_all, ((0,), (0,)))
    keys_r = sums_r[:, 0].transpose(1, 0, 2, 3).reshape(H, -1, small)
    values_r = sums_r[:, 1].transpose(1, 0, 2, 3).reshape(H, -1, small)
    grad_k = jnp.einsum("hnw,nhd->whd", keys_r, key_all, preferred_element_type=F32)
    grad_v = jnp.einsum("hnw,nhd->whd", values_r, gctx_all, preferred_element_type=F32)
    grad_qkv_weight = jnp.concatenate(
        [grad_q, grad_k.reshape(small, width), grad_v.reshape(small, width)], axis=1
    )
    bias8 = bias_r[: 8 * small].reshape(8, small)
    return (
        hidden_out,
        loss_mean,
        grad_tokens,
        grad_qkv_weight,
        grad_proj,
        grad_in_weight,
        grad_out_weight,
        bias8[:6],
        bias_r[8 * small :],
        bias8[6:],
    )


def solution(mesh):
    in_specs = (
        P(AXES, None),
        P(AXES, None),
        P(AXES, None),
        P(AXES, None),
        P(AXES, None),
        P(None, AXES),
        P(AXES),
        P(None, AXES),
        P(AXES, None),
        P(AXES),
        P(None, None, AXES, None),
    )
    out_specs = (
        P(None, AXES, None),
        P(),
        P(AXES, None),
        P(AXES, None),
        P(AXES, None),
        P(AXES, None),
        P(AXES, None),
        P(None, AXES),
        P(AXES),
        P(None, AXES),
    )
    return jax.shard_map(
        per_device, mesh=mesh, in_specs=in_specs, out_specs=out_specs, check_vma=False
    )
```

```python
import functools

import jax
import jax.numpy as jnp
from jax import lax
from jax.experimental import pallas as pl
from jax.experimental.pallas import tpu as pltpu
from jax.sharding import PartitionSpec as P

H = 12
HD = 64

NEGATIVE = -1e30
NORM_EPSILON = 1e-12
UNIT_EPSILON = 1e-06
SOFTMAX_TEMP = 0.05
KEEP_SCALE = 1.0 / 0.9
FULL_PRECISION = lax.Precision.HIGHEST
AXES = ("dp", "fsdp")
BF = jnp.bfloat16
F32 = jnp.float32


def dot(a, b, dims=((1,), (0,))):
    return lax.dot_general(a, b, (dims, ((), ())), preferred_element_type=F32)


def layer_norm(inputs, gain_vec, shift_vec):
    centre = inputs - jnp.mean(inputs, axis=-1, keepdims=True)
    spread = jnp.mean(centre * centre, axis=-1, keepdims=True)
    return centre * lax.rsqrt(spread + NORM_EPSILON) * gain_vec + shift_vec


def normalize(inputs):
    return inputs * lax.rsqrt(jnp.sum(inputs * inputs, axis=-1, keepdims=True) + UNIT_EPSILON)


def exact_gelu(inputs):
    return jax.nn.gelu(inputs, approximate=False)


def sentence_layout(bucket_row, pad_row, rows_here):
    row_ids = jnp.arange(rows_here, dtype=jnp.int32)
    starts = jnp.cumsum(bucket_row) - bucket_row
    used = bucket_row > 0
    member = (row_ids[:, None] >= starts[None, :]) & used[None, :]
    sentence = jnp.sum(member.astype(jnp.int32), axis=1)
    allowed = (sentence[:, None] == sentence[None, :]) & (pad_row[None, :] > 0)
    select = ((row_ids[None, :] == starts[:, None]) & used[:, None]).astype(jnp.float32)
    slot_allowed = (
        (sentence[None, :] == jnp.arange(1, bucket_row.shape[0] + 1)[:, None])
        & used[:, None]
        & (pad_row[None, :] > 0)
    )
    return (allowed, select, slot_allowed)


def gather(x, axis=0):
    return lax.all_gather(x, AXES, axis=axis, tiled=True)


def all_to_all(x):
    return lax.all_to_all(x, AXES, split_axis=0, concat_axis=0, tiled=True)


MESH = pl.DeviceIdType.MESH
PW, QW, SW = 3072, 1536, 256
WIDE = PW + QW
HALF = 2304

def place():
    dp = lax.axis_index("dp")
    fs = lax.axis_index("fsdp")
    return dp // 2, dp % 2, fs // 2, fs % 2

def peer_z(z, r):
    if r == 0:
        return z
    if r == 1:
        return z + 1 - 2 * (z % 2)
    if r == 2:
        return z + 2 - 4 * (z // 2)
    return 3 - z

def gather_kernel(qkv_ref, proj_ref, in_ref, out_ref, bias_ref, gain_ref, fbias_ref, used_ref,
                  wqp, win, wout, par, fpar,
                  l0, l1, l2, pb, stage, wpar,
                  sz, sx, sy, sa, sb, sc, scp, rz, rx, ry, ra, rb, rc, rcp):
    z, c, y, x = place()
    land = (l0, l1, l2)
    weights = (wqp, win, wout)

    def dev(z_, c_, y_, x_):
        return (2 * z_ + c_, 2 * y_ + x_)

    bar = pltpu.get_barrier_semaphore()
    partners = [dev(peer_z(z, 1), c, y, x), dev(peer_z(z, 2), c, y, x), dev(peer_z(z, 3), c, y, x),
                dev(z, c, y, 1 - x), dev(z, c, 1 - y, x), dev(z, 1 - c, y, x)]
    for p in partners:
        pl.semaphore_signal(bar, inc=1, device_id=p, device_id_type=MESH)

    def pack(ph, parts):
        dst = land[ph]
        at = 0
        qat = PW
        for ref in parts:
            v = ref[...].astype(F32)
            n = v.shape[1]
            even = x == 0
            p_rows = jnp.where(even, v[0:16], v[8:24])
            q_rows = jnp.where(even, v[16:24], v[0:8])
            dst[z, y, x, :, at:at + n] = p_rows.astype(BF)
            q = jnp.concatenate([q_rows[:, : n // 2], q_rows[:, n // 2:]], axis=0)
            dst[z, y, x, :, qat:qat + n // 2] = q.astype(BF)
            at += n
            qat += n // 2
    pack(0, (qkv_ref, proj_ref))
    d = 8 * z + 4 * c + 2 * y + x
    def put(ref, off):
        v = ref[...].astype(BF)
        n = v.shape[1]
        lane = lax.broadcasted_iota(jnp.int32, (n, SW), 1)
        row = lax.broadcasted_iota(jnp.int32, (n, SW), 0)
        hot = (lane == row + off).astype(BF)
        return jnp.dot(v, hot, preferred_element_type=F32)
    stage[...] = jnp.zeros_like(stage)
    stage[0:6, :] = put(bias_ref, (24 * d) % 128)
    stage[6:8, :] = put(gain_ref, (24 * d) % 128)
    stage[8:9, :] = put(fbias_ref, (96 * d) % 128)
    stage[9:10, :] = put(used_ref, (8 * d) % 128)
    l0[z, y, x, :, WIDE:] = stage[...].astype(BF)
    pl.semaphore_wait(bar, 6)

    def rcopy(src, dst, s, r, device):
        return pltpu.make_async_remote_copy(src_ref=src, dst_ref=dst, send_sem=s, recv_sem=r, device_id=device, device_id_type=MESH)

    def cp_z(ph, r):
        b = land[ph].at[z, y, x]
        return rcopy(b, b, sz.at[ph, r - 1], rz.at[ph, r - 1], dev(peer_z(z, r), c, y, x))

    def cp_x(ph, r):
        b = land[ph].at[peer_z(z, r), y, x]
        return rcopy(b, b, sx.at[ph, r], rx.at[ph, r], dev(z, c, y, 1 - x))

    def cp_y(ph, r):
        b = land[ph].at[peer_z(z, r), y, x]
        return rcopy(b, b, sy.at[ph, r], ry.at[ph, r], dev(z, c, 1 - y, x))

    def cp_a(ph, r):
        b = land[ph].at[peer_z(z, r), y, 1 - x, :, 0:HALF]
        return rcopy(b, b, sa.at[ph, r], ra.at[ph, r], dev(z, c, 1 - y, x))

    def cp_b(ph, r):
        b = land[ph].at[peer_z(z, r), 1 - y, x, :, HALF:]
        return rcopy(b, b, sb.at[ph, r], rb.at[ph, r], dev(z, c, y, 1 - x))

    def rows_of(ph, r):
        n = 384 if ph == 2 else 96
        return pl.ds(pl.multiple_of(n * (2 * peer_z(z, r) + c), n), n)

    def cp_c(ph, r):
        b = weights[ph].at[rows_of(ph, r)]
        return rcopy(b, b, sc.at[ph, r], rc.at[ph, r], dev(z, 1 - c, y, x))

    def cp_cp(r):
        b = pb.at[2 * peer_z(z, r) + c]
        return rcopy(b, b, scp.at[r], rcp.at[r], dev(z, 1 - c, y, x))

    def merge(ph, r):
        zz = peer_z(z, r)
        if ph == 2:
            for yy in range(2):
                for xx in range(2):
                    base = 384 * (2 * zz + c) + 96 * (2 * yy + xx)
                    for j in range(6):
                        wout[pl.ds(pl.multiple_of(base + 16 * j, 16), 16), :] = l2[zz, yy, xx, :, 768 * j:768 * (j + 1)]
        else:
            w = weights[ph]
            l = land[ph]
            for yy in range(2):
                base = 96 * (2 * zz + c) + 48 * yy
                w[pl.ds(pl.multiple_of(base, 16), 16), :] = l[zz, yy, 0, :, 0:PW]
                w[pl.ds(pl.multiple_of(base + 32, 16), 16), :] = l[zz, yy, 1, :, 0:PW]
                spans = [(0, 2304, PW), (2304, 768, PW + 1152)] if ph == 0 else [(0, 3072, PW)]
                mid = pl.ds(pl.multiple_of(base + 16, 16), 16)
                for at, n, qat in spans:
                    qe = l[zz, yy, 0, :, qat:qat + n // 2].astype(F32)
                    qo = l[zz, yy, 1, :, qat:qat + n // 2].astype(F32)
                    w[mid, at:at + n // 2] = jnp.concatenate([qe[0:8], qo[0:8]], axis=0).astype(BF)
                    w[mid, at + n // 2:at + n] = jnp.concatenate([qe[8:16], qo[8:16]], axis=0).astype(BF)
            if ph == 0:
                for yy in range(2):
                    for xx in range(2):
                        pb[2 * zz + c, 2 * yy + xx] = l0[zz, yy, xx, :, WIDE:]

    def finish(ph, r):
        if r > -1:
            merge(ph, r)
        cp_c(ph, r).start()
        if ph == 0:
            cp_cp(r).start()

    for r in (1, 2, 3):
        cp_z(0, r).start()
    cp_x(0, 0).start(); cp_y(0, 0).start()
    pack(1, (in_ref,))
    for j in range(6):
        l2[z, y, x, :, 768 * j:768 * (j + 1)] = out_ref[16 * j:16 * (j + 1), :]
    for r in (1, 2, 3):
        cp_z(0, r).wait_recv()
        cp_x(0, r).start(); cp_y(0, r).start()
        if r == 1:
            cp_x(0, 0).wait_recv(); cp_a(0, 0).start()
            cp_y(0, 0).wait_recv(); cp_b(0, 0).start()
    for ph in (1, 2):
        for r in (1, 2, 3):
            cp_z(ph, r).start()
    for r in (1, 2, 3):
        cp_x(0, r).wait_recv(); cp_a(0, r).start()
        cp_y(0, r).wait_recv(); cp_b(0, r).start()
    for r in range(4):
        if r:
            cp_z(1, r).wait_recv()
        cp_x(1, r).start(); cp_y(1, r).start()
    for r in range(4):
        cp_a(0, r).wait_recv(); cp_b(0, r).wait_recv()
        finish(0, r)
    for r in range(4):
        cp_c(0, r).wait_recv(); cp_cp(r).wait_recv()
    for r in range(4):
        cp_x(1, r).wait_recv(); cp_a(1, r).start()
        cp_y(1, r).wait_recv(); cp_b(1, r).start()
        if r:
            cp_z(2, r).wait_recv()
        cp_x(2, r).start(); cp_y(2, r).start()
    for r in range(4):
        cp_a(1, r).wait_recv(); cp_b(1, r).wait_recv()
        finish(1, r)
    for r in range(4):
        cp_c(1, r).wait_recv()
    for r in range(4):
        cp_x(2, r).wait_recv(); cp_a(2, r).start()
        cp_y(2, r).wait_recv(); cp_b(2, r).start()
    for r in range(4):
        cp_a(2, r).wait_recv(); cp_b(2, r).wait_recv()
        finish(2, r)
    for r in range(4):
        cp_c(2, r).wait_recv()
    wpar[...] = jnp.zeros_like(wpar)
    for dd in range(32):
        w = pb[dd // 4, dd % 4].astype(F32)
        t, t2, t3 = 24 * dd // 128, 96 * dd // 128, 8 * dd // 128
        wpar[0:8, 128 * t:128 * t + 256] += w[0:8]
        wpar[8:9, 128 * t2:128 * t2 + 256] += w[8:9]
        wpar[9:10, 128 * t3:128 * t3 + 256] += w[9:10]
    par[...] = wpar[0:8, 0:768]
    fpar[...] = wpar[8:16, 0:3072]
    for ph in range(3):
        for r in range(4):
            if r:
                cp_z(ph, r).wait_send()
            cp_x(ph, r).wait_send(); cp_y(ph, r).wait_send()
            cp_a(ph, r).wait_send(); cp_b(ph, r).wait_send()
            cp_c(ph, r).wait_send()
            if ph == 0:
                cp_cp(r).wait_send()

def gather_weights(qkv, proj, w_in, w_out, bias, gain, fbias, used):
    D = pltpu.SemaphoreType.DMA
    V = pl.BlockSpec(memory_space=pltpu.VMEM)
    sems = [D((3, 3)), D((3, 4)), D((3, 4)), D((3, 4)), D((3, 4)), D((3, 4)), D((4,))]
    return pl.pallas_call(
        gather_kernel,
        name="gather_weights",
        out_shape=[jax.ShapeDtypeStruct((768, PW), BF), jax.ShapeDtypeStruct((768, 3072), BF), jax.ShapeDtypeStruct((3072, 768), BF),
                   jax.ShapeDtypeStruct((8, 768), F32), jax.ShapeDtypeStruct((8, 3072), F32)],
        in_specs=[V] * 8, out_specs=[V] * 5,
        scratch_shapes=[pltpu.VMEM((4, 2, 2, 16, WIDE + SW), BF), pltpu.VMEM((4, 2, 2, 16, WIDE), BF), pltpu.VMEM((4, 2, 2, 16, WIDE), BF),
                        pltpu.VMEM((8, 4, 16, SW), BF), pltpu.VMEM((16, SW), F32), pltpu.VMEM((16, 3328), F32)] + sems + sems,
        compiler_params=pltpu.CompilerParams(collective_id=0, has_side_effects=True, vmem_limit_bytes=60 * 2**20),
    )(qkv, proj, w_in, w_out, bias, gain, fbias, used)


def per_device(
    grid_fits,
    tokens,
    qkv_weight,
    proj_weight,
    ffn_in_weight,
    ffn_out_weight,
    bias_rows,
    ffn_bias,
    norm_gains,
    buckets,
    padding,
    dropout,
):
    rows_here, width = tokens.shape
    slots = buckets.shape[1]
    hidden = ffn_in_weight.shape[1]
    small = bias_rows.shape[1]
    devices = width // small
    hidden_small = hidden // devices
    me = lax.axis_index(AXES)
    score_scale = HD ** (-0.5)
    used_slot = (buckets[0] > 0).astype(BF)

    if grid_fits:
        qp, in_full, out_full, rows8, extra = gather_weights(
            qkv_weight, proj_weight, ffn_in_weight, ffn_out_weight,
            bias_rows, norm_gains, ffn_bias[None], used_slot[None],
        )
        ffn_bias_f = extra[0]
        used_all = extra[1, : devices * slots]
    else:
        params = jnp.concatenate(
            [bias_rows.reshape(-1), norm_gains.reshape(-1), ffn_bias, used_slot]
        )
        params_all = gather(params[None])
        qp = gather(jnp.concatenate([qkv_weight, proj_weight], axis=1))
        in_full = gather(ffn_in_weight)
        out_full = gather(ffn_out_weight)
        rows8 = params_all[:, : 8 * small].reshape(devices, 8, small).transpose(1, 0, 2)
        rows8 = rows8.reshape(8, width).astype(F32)
        ffn_bias_f = params_all[:, 8 * small : 8 * small + hidden_small].reshape(-1).astype(F32)
        used_all = params_all[:, 8 * small + hidden_small :].reshape(-1)
    qkv_full, proj_full = qp[:, : 3 * width], qp[:, 3 * width :]
    bias_f, gain_f = rows8[:6], rows8[6:]

    allowed, select, slot_allowed = sentence_layout(buckets[0], padding, rows_here)
    select_low = select.astype(BF)
    zero_row = jnp.zeros((width,), F32)
    qkv = (dot(tokens, qkv_full) + jnp.concatenate([bias_f[0], zero_row, bias_f[1]])).astype(BF)
    head_view = qkv.reshape(rows_here, 3, H, HD)
    queries, key_rows, value_rows = (head_view[:, 0], head_view[:, 1], head_view[:, 2])

    scores = (
        jnp.einsum("qhd,khd->hqk", queries, key_rows, preferred_element_type=F32) * score_scale
    )
    scores = jnp.where(allowed[None], scores, NEGATIVE)
    exp_scores = jnp.exp(scores - jnp.max(scores, axis=-1, keepdims=True))
    probability = (exp_scores / jnp.sum(exp_scores, axis=-1, keepdims=True)).astype(BF)
    context = jnp.einsum("hqk,khd->qhd", probability, value_rows, preferred_element_type=F32)
    context = context.reshape(rows_here, width).astype(BF)
    branch = dot(context, proj_full) + bias_f[2]
    keep_mask = dropout.astype(F32)
    mixed_one = tokens.astype(F32)[None] + branch[None] * keep_mask[:, 0] * KEEP_SCALE
    normed = layer_norm(mixed_one, gain_f[0], bias_f[3])
    normed_low = normed.astype(BF)
    preact = dot(normed_low.reshape(-1, width), in_full) + ffn_bias_f
    activation = exact_gelu(preact).astype(BF)
    ffn_out = (dot(activation, out_full) + bias_f[4]).reshape(normed.shape)
    mixed_two = normed + ffn_out * keep_mask[:, 1] * KEEP_SCALE
    hidden_out = layer_norm(mixed_two, gain_f[1], bias_f[5]).astype(BF)

    tokens_s = dot(select_low, tokens)
    qkv_s = dot(select_low, qkv).astype(BF)
    queries_s = qkv_s[:, :width].reshape(slots, H, HD)
    scores_s = (
        jnp.einsum("shd,khd->hsk", queries_s, key_rows, preferred_element_type=F32) * score_scale
    )
    scores_s = jnp.where(slot_allowed[None], scores_s, NEGATIVE)
    peak_s = jnp.max(scores_s, axis=-1, keepdims=True)
    exp_s = jnp.exp(scores_s - peak_s) * slot_allowed[None].astype(F32)
    probability_f = exp_s / jnp.maximum(jnp.sum(exp_s, axis=-1, keepdims=True), 1e-30)
    probability_s = probability_f.astype(BF)
    context_s = dot(select_low, context).astype(BF)
    branch_s = dot(context_s, proj_full) + bias_f[2]
    keep_s = jnp.einsum(
        "sr,vbrd->vbsd", select_low, dropout.astype(BF), preferred_element_type=F32
    )
    mixed_s = tokens_s[None] + branch_s[None] * keep_s[:, 0] * KEEP_SCALE
    normed_s, first_back = jax.vjp(layer_norm, mixed_s, gain_f[0], bias_f[3])
    normed_s_low = normed_s.astype(BF).reshape(2 * slots, width)
    preact_s = dot(normed_s_low, in_full) + ffn_bias_f
    activation_sf, gelu_back = jax.vjp(exact_gelu, preact_s)
    activation_s = activation_sf.astype(BF)
    ffn_out_s = (dot(activation_s, out_full) + bias_f[4]).reshape(normed_s.shape)
    mixed_two_s = normed_s + ffn_out_s * keep_s[:, 1] * KEEP_SCALE
    final_s, second_back = jax.vjp(layer_norm, mixed_two_s, gain_f[1], bias_f[5])
    used_f = used_slot.astype(F32)
    final_s = final_s * used_f[None, :, None]
    unit_s, unit_back = jax.vjp(normalize, final_s)
    unit_low = unit_s.astype(BF)

    unit_all = gather(unit_low.reshape(1, 2, slots, width))
    unit_0 = unit_all[:, 0].reshape(-1, width)
    unit_1 = unit_all[:, 1].reshape(-1, width)
    logits = dot(unit_0, unit_1, ((1,), (1,))) / SOFTMAX_TEMP
    logits = jnp.where(used_all[None, :] > 0, logits, NEGATIVE)
    total = unit_0.shape[0]
    ids = jnp.arange(total, dtype=jnp.int32)
    diagonal = ids[:, None] == ids[None, :]
    logit_peak = jnp.max(logits, axis=-1, keepdims=True)
    logit_total = logit_peak[:, 0] + jnp.log(jnp.sum(jnp.exp(logits - logit_peak), axis=-1))
    positive = jnp.sum(jnp.where(diagonal, logits, 0.0), axis=1)
    used_all_f = used_all.astype(F32)
    loss_mean = jnp.sum((logit_total - positive) * used_all_f) / jnp.sum(used_all_f)
    soft = jnp.exp(logits - logit_total[:, None])
    logit_gradient = ((soft - diagonal.astype(F32)) * used_all_f[:, None]).astype(BF)
    mine_rows = lax.dynamic_slice_in_dim(logit_gradient, me * slots, slots, 0)
    mine_columns = lax.dynamic_slice_in_dim(logit_gradient, me * slots, slots, 1)
    grad_unit = jnp.stack(
        [dot(mine_rows, unit_1), dot(mine_columns, unit_0, ((0,), (0,)))]
    ) / SOFTMAX_TEMP
    (grad_final,) = unit_back(grad_unit)
    grad_final = grad_final * used_f[None, :, None]
    grad_mixed_two, grad_gain_two, grad_shift_two = second_back(grad_final)
    grad_ffn = (grad_mixed_two * keep_s[:, 1] * KEEP_SCALE).astype(BF).reshape(-1, width)
    grad_shift_out = jnp.sum(grad_ffn.astype(F32), axis=0)
    grad_act = dot(grad_ffn, out_full, ((1,), (1,)))
    (grad_preact_f,) = gelu_back(grad_act)
    grad_preact = grad_preact_f.astype(BF)
    grad_hidden_bias = jnp.sum(grad_preact.astype(F32), axis=0)
    grad_normed = dot(grad_preact, in_full, ((1,), (1,))).reshape(normed_s.shape) + grad_mixed_two
    grad_mixed, grad_gain_one, grad_shift_one = first_back(grad_normed)
    grad_branch = jnp.sum(grad_mixed * keep_s[:, 0] * KEEP_SCALE, axis=0).astype(BF)
    grad_shift_proj = jnp.sum(grad_branch.astype(F32), axis=0)
    grad_context = dot(grad_branch, proj_full, ((1,), (1,))).astype(BF)
    grad_context_h = grad_context.reshape(slots, H, HD)
    grad_probs = jnp.einsum(
        "shd,khd->hsk", grad_context_h, value_rows, preferred_element_type=F32
    )
    inner = jnp.sum(probability_f * grad_probs, axis=-1, keepdims=True)
    grad_scores = (probability_f * (grad_probs - inner)).astype(BF)
    grad_queries = (
        (jnp.einsum("hsk,khd->shd", grad_scores, key_rows, preferred_element_type=F32) * score_scale)
        .reshape(slots, width)
        .astype(BF)
    )
    pairs = jnp.concatenate([grad_scores, probability_s], axis=0).reshape(2 * H * slots, rows_here)
    token_sums = dot(pairs, tokens).astype(BF)
    key_factor = (queries_s.astype(F32) * score_scale).astype(BF)
    back_w = qkv_full.reshape(width, 3, H, HD)
    through = jnp.concatenate(
        [
            jnp.einsum("shd,whd->hsw", key_factor, back_w[:, 1], preferred_element_type=F32),
            jnp.einsum("shd,whd->hsw", grad_context_h, back_w[:, 2], preferred_element_type=F32),
        ],
        axis=0,
    ).reshape(2 * H * slots, width)
    start_grad = jnp.sum(grad_mixed, axis=0) + dot(
        grad_queries, qkv_full[:, :width], ((1,), (1,))
    )
    grad_tokens = dot(pairs, through.astype(BF), ((0,), (0,))) + lax.dot_general(
        select, start_grad, (((0,), (0,)), ((), ())), precision=FULL_PRECISION
    )
    value_sum = jnp.sum(probability_s.astype(F32), axis=-1).T
    grad_shift_value = jnp.sum(value_sum[:, :, None] * grad_context_h.astype(F32), axis=0).reshape(-1)
    grad_shift_query = jnp.sum(grad_queries.astype(F32), axis=0)

    wide = gather(jnp.concatenate([grad_ffn, grad_preact], axis=1))
    gffn_all, gpre_all = wide[:, :width], wide[:, width:]
    narrow = gather(
        jnp.concatenate([grad_branch, key_factor.reshape(slots, width), grad_context, grad_queries], axis=1)
    )
    gbranch_all = narrow[:, :width]
    key_all = narrow[:, width : 2 * width].reshape(-1, H, HD)
    gctx_all = narrow[:, 2 * width : 3 * width].reshape(-1, H, HD)
    gq_all = narrow[:, 3 * width :]

    def cut(x, n):
        return x.reshape(x.shape[0], devices, n).transpose(1, 0, 2).reshape(devices, -1)

    bias_sums = jnp.concatenate(
        [
            jnp.stack(
                [
                    grad_shift_query,
                    grad_shift_value,
                    grad_shift_proj,
                    grad_shift_one,
                    grad_shift_out,
                    grad_shift_two,
                    grad_gain_one,
                    grad_gain_two,
                ]
            )
            .reshape(8, devices, small)
            .transpose(1, 0, 2)
            .reshape(devices, -1),
            grad_hidden_bias.reshape(devices, -1),
        ],
        axis=1,
    )
    high = bias_sums.astype(BF)
    lower = (bias_sums - high.astype(F32)).astype(BF)
    pieces = [
        cut(activation_s, hidden_small),
        cut(normed_s_low, small),
        cut(context_s, small),
        cut(tokens_s.astype(BF), small),
        cut(token_sums, small),
        high,
        lower,
    ]
    sizes = [p.shape[1] for p in pieces]
    received = all_to_all(jnp.concatenate(pieces, axis=1))
    ends = []
    at = 0
    for n in sizes:
        ends.append(received[:, at : at + n])
        at += n
    act_r = ends[0].reshape(-1, hidden_small)
    normed_r = ends[1].reshape(-1, small)
    ctx_r = ends[2].reshape(-1, small)
    tok_r = ends[3].reshape(-1, small)
    sums_r = ends[4].reshape(devices, 2, H, slots, small)
    bias_r = jnp.sum(ends[5].astype(F32) + ends[6].astype(F32), axis=0)

    grad_out_weight = dot(act_r, gffn_all, ((0,), (0,)))
    grad_in_weight = dot(normed_r, gpre_all, ((0,), (0,)))
    grad_proj = dot(ctx_r, gbranch_all, ((0,), (0,)))
    grad_q = dot(tok_r, gq_all, ((0,), (0,)))
    keys_r = sums_r[:, 0].transpose(1, 0, 2, 3).reshape(H, -1, small)
    values_r = sums_r[:, 1].transpose(1, 0, 2, 3).reshape(H, -1, small)
    grad_k = jnp.einsum("hnw,nhd->whd", keys_r, key_all, preferred_element_type=F32)
    grad_v = jnp.einsum("hnw,nhd->whd", values_r, gctx_all, preferred_element_type=F32)
    grad_qkv_weight = jnp.concatenate(
        [grad_q, grad_k.reshape(small, width), grad_v.reshape(small, width)], axis=1
    )
    bias8 = bias_r[: 8 * small].reshape(8, small)
    return (
        hidden_out,
        loss_mean,
        grad_tokens,
        grad_qkv_weight,
        grad_proj,
        grad_in_weight,
        grad_out_weight,
        bias8[:6],
        bias_r[8 * small :],
        bias8[6:],
    )


def solution(mesh):
    in_specs = (
        P(AXES, None),
        P(AXES, None),
        P(AXES, None),
        P(AXES, None),
        P(AXES, None),
        P(None, AXES),
        P(AXES),
        P(None, AXES),
        P(AXES, None),
        P(AXES),
        P(None, None, AXES, None),
    )
    out_specs = (
        P(None, AXES, None),
        P(),
        P(AXES, None),
        P(AXES, None),
        P(AXES, None),
        P(AXES, None),
        P(AXES, None),
        P(None, AXES),
        P(AXES),
        P(None, AXES),
    )
    grid_fits = mesh.shape["dp"] == 8 and mesh.shape["fsdp"] == 4
    return jax.shard_map(
        functools.partial(per_device, grid_fits), mesh=mesh, in_specs=in_specs, out_specs=out_specs, check_vma=False
    )
```

```python
import functools

import jax
import jax.numpy as jnp
from jax import lax
from jax.experimental import pallas as pl
from jax.experimental.pallas import tpu as pltpu
from jax.sharding import PartitionSpec as P

H = 12
HD = 64

NEGATIVE = -1e30
NORM_EPSILON = 1e-12
UNIT_EPSILON = 1e-06
SOFTMAX_TEMP = 0.05
KEEP_SCALE = 1.0 / 0.9
FULL_PRECISION = lax.Precision.HIGHEST
AXES = ("dp", "fsdp")
BF = jnp.bfloat16
F32 = jnp.float32


def dot(a, b, dims=((1,), (0,))):
    return lax.dot_general(a, b, (dims, ((), ())), preferred_element_type=F32)


def layer_norm(inputs, gain_vec, shift_vec):
    centre = inputs - jnp.mean(inputs, axis=-1, keepdims=True)
    spread = jnp.mean(centre * centre, axis=-1, keepdims=True)
    return centre * lax.rsqrt(spread + NORM_EPSILON) * gain_vec + shift_vec


def normalize(inputs):
    return inputs * lax.rsqrt(jnp.sum(inputs * inputs, axis=-1, keepdims=True) + UNIT_EPSILON)


def exact_gelu(inputs):
    return jax.nn.gelu(inputs, approximate=False)


def sentence_layout(bucket_row, pad_row, rows_here):
    row_ids = jnp.arange(rows_here, dtype=jnp.int32)
    starts = jnp.cumsum(bucket_row) - bucket_row
    used = bucket_row > 0
    member = (row_ids[:, None] >= starts[None, :]) & used[None, :]
    sentence = jnp.sum(member.astype(jnp.int32), axis=1)
    allowed = (sentence[:, None] == sentence[None, :]) & (pad_row[None, :] > 0)
    select = ((row_ids[None, :] == starts[:, None]) & used[:, None]).astype(jnp.float32)
    slot_allowed = (
        (sentence[None, :] == jnp.arange(1, bucket_row.shape[0] + 1)[:, None])
        & used[:, None]
        & (pad_row[None, :] > 0)
    )
    return (allowed, select, slot_allowed)


def gather(x, axis=0):
    return lax.all_gather(x, AXES, axis=axis, tiled=True)


def all_to_all(x):
    return lax.all_to_all(x, AXES, split_axis=0, concat_axis=0, tiled=True)


def with_collectives(
    tokens,
    qkv_weight,
    proj_weight,
    ffn_in_weight,
    ffn_out_weight,
    bias_rows,
    ffn_bias,
    norm_gains,
    buckets,
    padding,
    dropout,
):
    rows_here, width = tokens.shape
    slots = buckets.shape[1]
    hidden = ffn_in_weight.shape[1]
    small = bias_rows.shape[1]
    devices = width // small
    hidden_small = hidden // devices
    me = lax.axis_index(AXES)
    score_scale = HD ** (-0.5)
    used_slot = (buckets[0] > 0).astype(BF)

    params = jnp.concatenate(
        [bias_rows.reshape(-1), norm_gains.reshape(-1), ffn_bias, used_slot]
    )
    params_all = gather(params[None])
    qp = gather(jnp.concatenate([qkv_weight, proj_weight], axis=1))
    qkv_full, proj_full = qp[:, : 3 * width], qp[:, 3 * width :]
    in_full = gather(ffn_in_weight)
    out_full = gather(ffn_out_weight)
    rows8 = params_all[:, : 8 * small].reshape(devices, 8, small).transpose(1, 0, 2)
    rows8 = rows8.reshape(8, width).astype(F32)
    bias_f, gain_f = rows8[:6], rows8[6:]
    ffn_bias_f = params_all[:, 8 * small : 8 * small + hidden_small].reshape(-1).astype(F32)
    used_all = params_all[:, 8 * small + hidden_small :].reshape(-1)

    allowed, select, slot_allowed = sentence_layout(buckets[0], padding, rows_here)
    select_low = select.astype(BF)
    zero_row = jnp.zeros((width,), F32)
    qkv = (dot(tokens, qkv_full) + jnp.concatenate([bias_f[0], zero_row, bias_f[1]])).astype(BF)
    head_view = qkv.reshape(rows_here, 3, H, HD)
    queries, key_rows, value_rows = (head_view[:, 0], head_view[:, 1], head_view[:, 2])

    scores = (
        jnp.einsum("qhd,khd->hqk", queries, key_rows, preferred_element_type=F32) * score_scale
    )
    scores = jnp.where(allowed[None], scores, NEGATIVE)
    exp_scores = jnp.exp(scores - jnp.max(scores, axis=-1, keepdims=True))
    probability = (exp_scores / jnp.sum(exp_scores, axis=-1, keepdims=True)).astype(BF)
    context = jnp.einsum("hqk,khd->qhd", probability, value_rows, preferred_element_type=F32)
    context = context.reshape(rows_here, width).astype(BF)
    branch = dot(context, proj_full) + bias_f[2]
    keep_mask = dropout.astype(F32)
    mixed_one = tokens.astype(F32)[None] + branch[None] * keep_mask[:, 0] * KEEP_SCALE
    normed = layer_norm(mixed_one, gain_f[0], bias_f[3])
    normed_low = normed.astype(BF)
    preact = dot(normed_low.reshape(-1, width), in_full) + ffn_bias_f
    activation = exact_gelu(preact).astype(BF)
    ffn_out = (dot(activation, out_full) + bias_f[4]).reshape(normed.shape)
    mixed_two = normed + ffn_out * keep_mask[:, 1] * KEEP_SCALE
    hidden_out = layer_norm(mixed_two, gain_f[1], bias_f[5]).astype(BF)

    tokens_s = dot(select_low, tokens)
    qkv_s = dot(select_low, qkv).astype(BF)
    queries_s = qkv_s[:, :width].reshape(slots, H, HD)
    scores_s = (
        jnp.einsum("shd,khd->hsk", queries_s, key_rows, preferred_element_type=F32) * score_scale
    )
    scores_s = jnp.where(slot_allowed[None], scores_s, NEGATIVE)
    peak_s = jnp.max(scores_s, axis=-1, keepdims=True)
    exp_s = jnp.exp(scores_s - peak_s) * slot_allowed[None].astype(F32)
    probability_f = exp_s / jnp.maximum(jnp.sum(exp_s, axis=-1, keepdims=True), 1e-30)
    probability_s = probability_f.astype(BF)
    context_s = dot(select_low, context).astype(BF)
    branch_s = dot(context_s, proj_full) + bias_f[2]
    keep_s = jnp.einsum(
        "sr,vbrd->vbsd", select_low, dropout.astype(BF), preferred_element_type=F32
    )
    mixed_s = tokens_s[None] + branch_s[None] * keep_s[:, 0] * KEEP_SCALE
    normed_s, first_back = jax.vjp(layer_norm, mixed_s, gain_f[0], bias_f[3])
    normed_s_low = normed_s.astype(BF).reshape(2 * slots, width)
    preact_s = dot(normed_s_low, in_full) + ffn_bias_f
    activation_sf, gelu_back = jax.vjp(exact_gelu, preact_s)
    activation_s = activation_sf.astype(BF)
    ffn_out_s = (dot(activation_s, out_full) + bias_f[4]).reshape(normed_s.shape)
    mixed_two_s = normed_s + ffn_out_s * keep_s[:, 1] * KEEP_SCALE
    final_s, second_back = jax.vjp(layer_norm, mixed_two_s, gain_f[1], bias_f[5])
    used_f = used_slot.astype(F32)
    final_s = final_s * used_f[None, :, None]
    unit_s, unit_back = jax.vjp(normalize, final_s)
    unit_low = unit_s.astype(BF)

    unit_all = gather(unit_low.reshape(1, 2, slots, width))
    unit_0 = unit_all[:, 0].reshape(-1, width)
    unit_1 = unit_all[:, 1].reshape(-1, width)
    logits = dot(unit_0, unit_1, ((1,), (1,))) / SOFTMAX_TEMP
    logits = jnp.where(used_all[None, :] > 0, logits, NEGATIVE)
    total = unit_0.shape[0]
    ids = jnp.arange(total, dtype=jnp.int32)
    diagonal = ids[:, None] == ids[None, :]
    logit_peak = jnp.max(logits, axis=-1, keepdims=True)
    logit_total = logit_peak[:, 0] + jnp.log(jnp.sum(jnp.exp(logits - logit_peak), axis=-1))
    positive = jnp.sum(jnp.where(diagonal, logits, 0.0), axis=1)
    used_all_f = used_all.astype(F32)
    loss_mean = jnp.sum((logit_total - positive) * used_all_f) / jnp.sum(used_all_f)
    soft = jnp.exp(logits - logit_total[:, None])
    logit_gradient = ((soft - diagonal.astype(F32)) * used_all_f[:, None]).astype(BF)
    mine_rows = lax.dynamic_slice_in_dim(logit_gradient, me * slots, slots, 0)
    mine_columns = lax.dynamic_slice_in_dim(logit_gradient, me * slots, slots, 1)
    grad_unit = jnp.stack(
        [dot(mine_rows, unit_1), dot(mine_columns, unit_0, ((0,), (0,)))]
    ) / SOFTMAX_TEMP
    (grad_final,) = unit_back(grad_unit)
    grad_final = grad_final * used_f[None, :, None]
    grad_mixed_two, grad_gain_two, grad_shift_two = second_back(grad_final)
    grad_ffn = (grad_mixed_two * keep_s[:, 1] * KEEP_SCALE).astype(BF).reshape(-1, width)
    grad_shift_out = jnp.sum(grad_ffn.astype(F32), axis=0)
    grad_act = dot(grad_ffn, out_full, ((1,), (1,)))
    (grad_preact_f,) = gelu_back(grad_act)
    grad_preact = grad_preact_f.astype(BF)
    grad_hidden_bias = jnp.sum(grad_preact.astype(F32), axis=0)
    grad_normed = dot(grad_preact, in_full, ((1,), (1,))).reshape(normed_s.shape) + grad_mixed_two
    grad_mixed, grad_gain_one, grad_shift_one = first_back(grad_normed)
    grad_branch = jnp.sum(grad_mixed * keep_s[:, 0] * KEEP_SCALE, axis=0).astype(BF)
    grad_shift_proj = jnp.sum(grad_branch.astype(F32), axis=0)
    grad_context = dot(grad_branch, proj_full, ((1,), (1,))).astype(BF)
    grad_context_h = grad_context.reshape(slots, H, HD)
    grad_probs = jnp.einsum(
        "shd,khd->hsk", grad_context_h, value_rows, preferred_element_type=F32
    )
    inner = jnp.sum(probability_f * grad_probs, axis=-1, keepdims=True)
    grad_scores = (probability_f * (grad_probs - inner)).astype(BF)
    grad_queries = (
        (jnp.einsum("hsk,khd->shd", grad_scores, key_rows, preferred_element_type=F32) * score_scale)
        .reshape(slots, width)
        .astype(BF)
    )
    pairs = jnp.concatenate([grad_scores, probability_s], axis=0).reshape(2 * H * slots, rows_here)
    token_sums = dot(pairs, tokens).astype(BF)
    key_factor = (queries_s.astype(F32) * score_scale).astype(BF)
    back_w = qkv_full.reshape(width, 3, H, HD)
    through = jnp.concatenate(
        [
            jnp.einsum("shd,whd->hsw", key_factor, back_w[:, 1], preferred_element_type=F32),
            jnp.einsum("shd,whd->hsw", grad_context_h, back_w[:, 2], preferred_element_type=F32),
        ],
        axis=0,
    ).reshape(2 * H * slots, width)
    start_grad = jnp.sum(grad_mixed, axis=0) + dot(
        grad_queries, qkv_full[:, :width], ((1,), (1,))
    )
    grad_tokens = dot(pairs, through.astype(BF), ((0,), (0,))) + lax.dot_general(
        select, start_grad, (((0,), (0,)), ((), ())), precision=FULL_PRECISION
    )
    value_sum = jnp.sum(probability_s.astype(F32), axis=-1).T
    grad_shift_value = jnp.sum(value_sum[:, :, None] * grad_context_h.astype(F32), axis=0).reshape(-1)
    grad_shift_query = jnp.sum(grad_queries.astype(F32), axis=0)

    wide = gather(jnp.concatenate([grad_ffn, grad_preact], axis=1))
    gffn_all, gpre_all = wide[:, :width], wide[:, width:]
    narrow = gather(
        jnp.concatenate([grad_branch, key_factor.reshape(slots, width), grad_context, grad_queries], axis=1)
    )
    gbranch_all = narrow[:, :width]
    key_all = narrow[:, width : 2 * width].reshape(-1, H, HD)
    gctx_all = narrow[:, 2 * width : 3 * width].reshape(-1, H, HD)
    gq_all = narrow[:, 3 * width :]

    def cut(x, n):
        return x.reshape(x.shape[0], devices, n).transpose(1, 0, 2).reshape(devices, -1)

    bias_sums = jnp.concatenate(
        [
            jnp.stack(
                [
                    grad_shift_query,
                    grad_shift_value,
                    grad_shift_proj,
                    grad_shift_one,
                    grad_shift_out,
                    grad_shift_two,
                    grad_gain_one,
                    grad_gain_two,
                ]
            )
            .reshape(8, devices, small)
            .transpose(1, 0, 2)
            .reshape(devices, -1),
            grad_hidden_bias.reshape(devices, -1),
        ],
        axis=1,
    )
    high = bias_sums.astype(BF)
    lower = (bias_sums - high.astype(F32)).astype(BF)
    pieces = [
        cut(activation_s, hidden_small),
        cut(normed_s_low, small),
        cut(context_s, small),
        cut(tokens_s.astype(BF), small),
        cut(token_sums, small),
        high,
        lower,
    ]
    sizes = [p.shape[1] for p in pieces]
    received = all_to_all(jnp.concatenate(pieces, axis=1))
    ends = []
    at = 0
    for n in sizes:
        ends.append(received[:, at : at + n])
        at += n
    act_r = ends[0].reshape(-1, hidden_small)
    normed_r = ends[1].reshape(-1, small)
    ctx_r = ends[2].reshape(-1, small)
    tok_r = ends[3].reshape(-1, small)
    sums_r = ends[4].reshape(devices, 2, H, slots, small)
    bias_r = jnp.sum(ends[5].astype(F32) + ends[6].astype(F32), axis=0)

    grad_out_weight = dot(act_r, gffn_all, ((0,), (0,)))
    grad_in_weight = dot(normed_r, gpre_all, ((0,), (0,)))
    grad_proj = dot(ctx_r, gbranch_all, ((0,), (0,)))
    grad_q = dot(tok_r, gq_all, ((0,), (0,)))
    keys_r = sums_r[:, 0].transpose(1, 0, 2, 3).reshape(H, -1, small)
    values_r = sums_r[:, 1].transpose(1, 0, 2, 3).reshape(H, -1, small)
    grad_k = jnp.einsum("hnw,nhd->whd", keys_r, key_all, preferred_element_type=F32)
    grad_v = jnp.einsum("hnw,nhd->whd", values_r, gctx_all, preferred_element_type=F32)
    grad_qkv_weight = jnp.concatenate(
        [grad_q, grad_k.reshape(small, width), grad_v.reshape(small, width)], axis=1
    )
    bias8 = bias_r[: 8 * small].reshape(8, small)
    return (
        hidden_out,
        loss_mean,
        grad_tokens,
        grad_qkv_weight,
        grad_proj,
        grad_in_weight,
        grad_out_weight,
        bias8[:6],
        bias_r[8 * small :],
        bias8[6:],
    )


MESH = pl.DeviceIdType.MESH
PW, QW, SW = 3072, 1536, 256
WIDE = PW + QW
HALF = 2304
HIGH = lax.Precision.HIGHEST
LAST = ((1,), (1,))
FIRST = ((0,), (0,))
SPLIT = (HALF, HALF, HALF, 384, 1920, 768)
WHOLE = (WIDE + SW, WIDE, WIDE, 768, 3840, 1536)


def place():
    dp = lax.axis_index("dp")
    fs = lax.axis_index("fsdp")
    return dp // 2, dp % 2, fs // 2, fs % 2


def peer_z(z, r):
    return (z + r) % 2 + 2 * ((z // 2 + r // 2) % 2)


def hot(rows, columns, shift):
    row = lax.broadcasted_iota(jnp.int32, (rows, columns), 0)
    column = lax.broadcasted_iota(jnp.int32, (rows, columns), 1)
    return row + shift == column


def as_number(flags):
    return jnp.where(flags, 1.0, 0.0)


def tail_of(x):
    t = 1.0 / (1.0 + (0.3275911 * 0.7071067811865476) * jnp.abs(x))
    bell = jnp.exp(x * x * -0.5)
    poly = 0.5 * 1.061405429
    for c in (-1.453152027, 1.421413741, -0.284496736, 0.254829592):
        poly = poly * t + 0.5 * c
    return poly * t * bell, bell


def gelu(x):
    tail, _ = tail_of(x)
    return jnp.maximum(x, 0.0) - jnp.abs(x) * tail


def gelu_slope(x):
    tail, bell = tail_of(x)
    return jnp.where(x >= 0.0, 1.0 - tail, tail) + x * bell * 0.3989422804014327


def mean(x):
    return jnp.sum(x, axis=-1, keepdims=True) * (1.0 / x.shape[-1])


def standardize(x):
    centre = x - mean(x)
    scale = lax.rsqrt(mean(centre * centre) + NORM_EPSILON)
    return centre * scale, scale


def norm_back(grad_hat, hat, scale):
    return scale * (grad_hat - mean(grad_hat) - hat * mean(grad_hat * hat))


def encoder_kernel(
    qkv_ref, proj_ref, in_ref, out_ref, bias_ref, gain_ref, fbias_ref, tokens, buckets_ref, pad_ref, drop_hbm,
    hidden, loss_ref, gtok, g_qkv, g_proj, g_in, g_out, g_bias, g_fbias, g_gain,
    wqp, win, wout, l0, l1, l2, f3, f4, f5, pb, stage, par,
    drop, qkv, madd, ctx, normed, nlow, act,
    cls, sm8, sel, pre_s, acts, p_f, pairs, through, mixer, mixer_t, unit0, unit1, sums, gacc,
    early, early_in, late, late_in, actw_in,
    sz, sx, sy, sa, sb, sc, scp, rz, rx, ry, ra, rb, rc, rcp, s_early, r_early, s_act, r_act, s_late, r_late, s_drop,
):
    z, c, y, x = place()
    me = 8 * z + 4 * c + 2 * y + x
    land = (l0, l1, l2)
    full = (f3, f4, f5)
    weights = (wqp, win, wout)
    lanes = functools.partial(lax.broadcasted_iota, jnp.int32)

    def dev(z_, c_, y_, x_):
        return (2 * z_ + c_, 2 * y_ + x_)

    def other(i):
        t = (me + i) % 32
        return t, (t // 4, t % 4)

    def loop(lo, hi, body):
        def step(i, carry):
            body(i)
            return carry

        lax.fori_loop(lo, hi, step, 0)

    bar = pltpu.get_barrier_semaphore()

    def greet(i):
        _, device = other(i)
        pl.semaphore_signal(bar, inc=1, device_id=device, device_id_type=MESH)

    loop(1, 32, greet)
    drop_copy = pltpu.make_async_copy(drop_hbm, drop, s_drop)
    drop_copy.start()

    def slot(ph, zz, yy, xx):
        if ph < 3:
            return land[ph].at[zz, yy, xx]
        return full[ph - 3].at[2 * zz + c, 2 * yy + xx]

    def rcopy(ref, s, r, device):
        return pltpu.make_async_remote_copy(
            src_ref=ref, dst_ref=ref, send_sem=s, recv_sem=r, device_id=device, device_id_type=MESH
        )

    def cp_z(ph, r):
        return rcopy(slot(ph, z, y, x), sz.at[ph, r], rz.at[ph, r], dev(peer_z(z, r), c, y, x))

    def cp_x(ph, r):
        return rcopy(slot(ph, peer_z(z, r), y, x), sx.at[ph, r], rx.at[ph, r], dev(z, c, y, 1 - x))

    def cp_y(ph, r):
        return rcopy(slot(ph, peer_z(z, r), y, x), sy.at[ph, r], ry.at[ph, r], dev(z, c, 1 - y, x))

    def cp_a(ph, r):
        ref = slot(ph, peer_z(z, r), y, 1 - x).at[:, 0 : SPLIT[ph]]
        return rcopy(ref, sa.at[ph, r], ra.at[ph, r], dev(z, c, 1 - y, x))

    def cp_b(ph, r):
        ref = slot(ph, peer_z(z, r), 1 - y, x).at[:, SPLIT[ph] : WHOLE[ph]]
        return rcopy(ref, sb.at[ph, r], rb.at[ph, r], dev(z, c, y, 1 - x))

    def cp_c(ph, r):
        group = 2 * peer_z(z, r) + c
        if ph < 3:
            n = 384 if ph == 2 else 96
            ref = weights[ph].at[pl.ds(pl.multiple_of(n * group, n), n)]
        else:
            ref = full[ph - 3].at[group]
        return rcopy(ref, sc.at[ph, r], rc.at[ph, r], dev(z, 1 - c, y, x))

    def cp_cp(r):
        return rcopy(pb.at[2 * peer_z(z, r) + c], scp.at[r], rcp.at[r], dev(z, 1 - c, y, x))

    def start_z(ph):
        loop(1, 4, lambda r: cp_z(ph, r).start())

    def start_xy(ph, r):
        cp_x(ph, r).start()
        cp_y(ph, r).start()

    def wait_z_start_xy(ph, r):
        cp_z(ph, r).wait_recv()
        start_xy(ph, r)

    def wait_xy_start_ab(ph, r):
        cp_x(ph, r).wait_recv()
        cp_a(ph, r).start()
        cp_y(ph, r).wait_recv()
        cp_b(ph, r).start()

    def merge(ph, r):
        zz = peer_z(z, r)
        group = 2 * zz + c
        if ph == 2:
            for yy in range(2):
                for xx in range(2):
                    base = 384 * group + 96 * (2 * yy + xx)
                    for j in range(6):
                        wout[pl.ds(pl.multiple_of(base + 16 * j, 16), 16), :] = l2[
                            zz, yy, xx, :, 768 * j : 768 * (j + 1)
                        ]
            return
        w = weights[ph]
        l = land[ph]
        spans = [(0, 2304, PW), (2304, 768, PW + 1152)] if ph == 0 else [(0, 3072, PW)]
        for yy in range(2):
            base = 96 * group + 48 * yy
            w[pl.ds(pl.multiple_of(base, 16), 16), :] = l[zz, yy, 0, :, 0:PW]
            w[pl.ds(pl.multiple_of(base + 32, 16), 16), :] = l[zz, yy, 1, :, 0:PW]
            middle = pl.ds(pl.multiple_of(base + 16, 16), 16)
            for at, n, qat in spans:
                qe = l[zz, yy, 0, :, qat : qat + n // 2].astype(F32)
                qo = l[zz, yy, 1, :, qat : qat + n // 2].astype(F32)
                w[middle, at : at + n // 2] = jnp.concatenate([qe[0:8], qo[0:8]], axis=0).astype(BF)
                w[middle, at + n // 2 : at + n] = jnp.concatenate([qe[8:16], qo[8:16]], axis=0).astype(BF)
        if ph == 0:
            for yy in range(2):
                for xx in range(2):
                    pb[group, 2 * yy + xx] = l0[zz, yy, xx, :, WIDE:]

    def wait_ab_start_c(ph, r):
        cp_a(ph, r).wait_recv()
        cp_b(ph, r).wait_recv()
        if ph < 3:
            merge(ph, r)
        cp_c(ph, r).start()
        if ph == 0:
            cp_cp(r).start()

    def wait_c(ph, r):
        cp_c(ph, r).wait_recv()
        if ph == 0:
            cp_cp(r).wait_recv()

    def pack(ph, parts):
        at, qat = 0, PW
        for ref in parts:
            v = ref[...].astype(F32)
            n = v.shape[1]
            p_rows = jnp.where(x == 0, v[0:16], v[8:24])
            q_rows = jnp.where(x == 0, v[16:24], v[0:8])
            land[ph][z, y, x, :, at : at + n] = p_rows.astype(BF)
            land[ph][z, y, x, :, qat : qat + n // 2] = jnp.concatenate(
                [q_rows[:, : n // 2], q_rows[:, n // 2 :]], axis=0
            ).astype(BF)
            at += n
            qat += n // 2

    pack(0, (qkv_ref, proj_ref))

    def put(v, shift):
        return dot(v.astype(BF), as_number(hot(v.shape[1], SW, shift)).astype(BF))

    bk = buckets_ref[...].astype(F32)
    stage[...] = jnp.zeros_like(stage)
    stage[0:6, :] = put(bias_ref[...], (24 * me) % 128)
    stage[6:8, :] = put(gain_ref[...], (24 * me) % 128)
    stage[8:9, :] = put(fbias_ref[...], (96 * me) % 128)
    stage[9:10, :] = put(as_number(bk > 0.0), (8 * me) % 128)
    l0[z, y, x, :, WIDE:] = stage[...].astype(BF)
    pl.semaphore_wait(bar, 31)

    start_z(0)
    start_xy(0, 0)
    pack(1, (in_ref,))
    for j in range(6):
        l2[z, y, x, :, 768 * j : 768 * (j + 1)] = out_ref[16 * j : 16 * (j + 1), :]

    row8, lane8 = lanes((8, 8), 0), lanes((8, 8), 1)
    bk_col = jnp.sum(jnp.where(row8 == lane8, bk, 0.0), axis=1, keepdims=True)
    starts_col = jnp.sum(jnp.where(lane8 < row8, bk, 0.0), axis=1, keepdims=True)
    starts_row = jnp.sum(jnp.where(row8 < lane8, bk_col, 0.0), axis=0, keepdims=True)
    used_mine = as_number(bk_col > 0.0)
    used16 = jnp.concatenate([used_mine, used_mine], axis=0)
    row_ids = lanes((512, 8), 0).astype(F32)
    column_ids = lanes((8, 512), 1).astype(F32)
    sent_row = jnp.sum(as_number((row_ids >= starts_row) & (bk > 0.0)), axis=1, keepdims=True)
    sent_col = jnp.sum(as_number((column_ids >= starts_col) & (bk_col > 0.0)), axis=0, keepdims=True)
    key_of = jnp.where(pad_ref[...] > 0, sent_col, 0.0)
    madd[...] = jnp.where(sent_row == key_of, 0.0, NEGATIVE)
    sm8[...] = as_number(key_of == (lanes((8, 512), 0) + 1).astype(F32))
    sel[...] = as_number((column_ids == starts_col) & (bk_col > 0.0)).astype(BF)

    wait_z_start_xy(0, 1)
    wait_xy_start_ab(0, 0)
    wait_z_start_xy(0, 2)
    wait_z_start_xy(0, 3)
    start_z(1)
    start_xy(1, 0)
    start_z(2)
    loop(1, 4, lambda r: wait_xy_start_ab(0, r))
    loop(1, 4, lambda r: wait_z_start_xy(1, r))
    loop(0, 4, lambda r: wait_ab_start_c(0, r))
    drop_copy.wait()
    loop(0, 4, lambda r: wait_c(0, r))
    par[...] = jnp.zeros_like(par)
    for d in range(32):
        w = pb[d // 4, d % 4].astype(F32)
        t, t2, t3 = 24 * d // 128, 96 * d // 128, 8 * d // 128
        par[0:8, 128 * t : 128 * t + 256] += w[0:8]
        par[8:9, 128 * t2 : 128 * t2 + 256] += w[8:9]
        par[9:10, 128 * t3 : 128 * t3 + 256] += w[9:10]

    def bias(i):
        return par[i : i + 1, 0:768]

    def gain(i):
        return par[6 + i : 7 + i, 0:768]

    def qkv_part(i):
        columns = pl.ds(pl.multiple_of(256 * i, 256), 256)
        inside = pl.ds(pl.multiple_of(256 * (i % 3), 256), 256)
        both = par[0:8, inside]
        part = jnp.where(i < 3, both[0:1], jnp.where(i < 6, 0.0, both[1:2]))
        qkv[:, columns] = (dot(tokens[...], wqp[:, columns]) + part).astype(BF)

    loop(0, 9, qkv_part)
    wait_xy_start_ab(1, 0)
    wait_z_start_xy(2, 1)
    start_xy(2, 0)

    left = lanes((1, 128), 1) < 64
    left_scale = jnp.where(left, HD**-0.5, 0.0)
    right_scale = jnp.where(left, 0.0, HD**-0.5)

    def attend(pair):
        def columns(part):
            return pl.ds(pl.multiple_of(768 * part + 128 * pair, 128), 128)

        def block(i):
            rows = pl.ds(pl.multiple_of(128 * i, 128), 128)
            q = qkv[rows, columns(0)].astype(F32)
            results = []
            for scale in (left_scale, right_scale):
                s = dot((q * scale).astype(BF), qkv[:, columns(1)], LAST) + madd[rows, :]
                e = jnp.exp(s - jnp.max(s, axis=-1, keepdims=True))
                p = (e * (1.0 / jnp.sum(e, axis=-1, keepdims=True))).astype(BF)
                results.append(dot(p, qkv[:, columns(2)]))
            ctx[rows, columns(0)] = jnp.where(left, results[0], results[1]).astype(BF)

        loop(0, 4, block)

    def attend_and_send(r):
        attend(2 * (r - 1))
        wait_xy_start_ab(1, r)
        attend(2 * (r - 1) + 1)

    loop(1, 4, attend_and_send)
    loop(2, 4, lambda r: wait_z_start_xy(2, r))

    def first_norm(i):
        rows = pl.ds(pl.multiple_of(128 * i, 128), 128)
        branch = (dot(ctx[rows, :], wqp[:, 2304:3072]) + bias(2)) * KEEP_SCALE
        token_rows = tokens[rows, :].astype(F32)
        for v in range(2):
            hat, _ = standardize(token_rows + branch * drop[v, 0, rows, :].astype(F32))
            n = hat * gain(0) + bias(3)
            normed[v, rows, :] = n
            nlow[pl.ds(pl.multiple_of(512 * v + 128 * i, 128), 128), :] = n.astype(BF)

    loop(0, 4, first_norm)

    TOK, QRY, CTX, KEEP1, KEEP2, HAT1, NRM, HAT2, FIN = 0, 8, 16, 24, 40, 56, 72, 88, 104
    pick = sel[...]
    cls[TOK : TOK + 8, :] = dot(pick, tokens[...])
    cls[QRY : QRY + 8, :] = dot(pick, qkv[:, 0:768]) * HD**-0.5
    cls[CTX : CTX + 8, :] = dot(pick, ctx[...])
    for v in range(2):
        cls[KEEP1 + 8 * v : KEEP1 + 8 * v + 8, :] = dot(pick, drop[v, 0].astype(F32).astype(BF)) * KEEP_SCALE
        cls[KEEP2 + 8 * v : KEEP2 + 8 * v + 8, :] = dot(pick, drop[v, 1].astype(F32).astype(BF)) * KEEP_SCALE

    def twice(v):
        return jnp.concatenate([v, v], axis=0)

    head = lax.broadcasted_iota(jnp.int32, (12, 8, 768), 0) * 64
    lane = lax.broadcasted_iota(jnp.int32, (12, 8, 768), 2)
    own_head = (lane >= head) & (lane < head + 64)

    def spread(rows8):
        return jnp.where(own_head, rows8[None], 0.0).reshape(96, 768).astype(BF)

    def gathered(rows96):
        return jnp.sum(jnp.where(own_head, rows96.reshape(12, 8, 768), 0.0), axis=0)

    branch_s = dot(cls[CTX : CTX + 8, :].astype(BF), wqp[:, 2304:3072]) + bias(2)
    hat1, scale1 = standardize(twice(cls[TOK : TOK + 8, :]) + twice(branch_s) * cls[KEEP1 : KEEP1 + 16, :])
    normed_s = hat1 * gain(0) + bias(3)
    cls[HAT1 : HAT1 + 16, :] = hat1
    cls[NRM : NRM + 16, :] = normed_s
    query_big = spread(cls[QRY : QRY + 8, :])
    seen = jnp.broadcast_to(sm8[...][None], (12, 8, 512)).reshape(96, 512)
    s = jnp.where(seen > 0.0, dot(query_big, qkv[:, 768:1536], LAST), NEGATIVE)
    e = jnp.exp(s - jnp.max(s, axis=-1, keepdims=True)) * seen
    prob = e * (1.0 / jnp.maximum(jnp.sum(e, axis=-1, keepdims=True), 1e-30))
    p_f[...] = prob
    pairs[96:192, :] = prob.astype(BF)
    pairs[192:208, :] = twice(pick.astype(F32)).astype(BF)
    mixer[0:96, :] = dot(prob.astype(BF), tokens[...])
    mixer[96:104, :] = cls[CTX : CTX + 8, :]
    mixer[104:112, :] = cls[TOK : TOK + 8, :]
    mixer[112:128, :] = normed_s

    def send_mixer(box, box_in, s_sem, r_sem):
        mixer_t[...] = jnp.transpose(mixer[...])

        def cut(t):
            v = mixer_t[pl.ds(pl.multiple_of(24 * t, 8), 24), :]
            box[t] = jnp.concatenate([v, jnp.zeros((8, 128), F32)], axis=0).astype(BF)

        loop(0, 32, cut)
        box_in[me] = box[me]

        def send(i):
            t, device = other(i)
            pltpu.make_async_remote_copy(
                src_ref=box.at[t],
                dst_ref=box_in.at[me],
                send_sem=s_sem,
                recv_sem=r_sem,
                device_id=device,
                device_id_type=MESH,
            ).start()

        loop(1, 32, send)

    def wait_boxes(ref, sem):
        part = ref.at[pl.ds(0, 31)]
        pltpu.make_async_copy(part, part, sem).wait()

    send_mixer(early, early_in, s_early, r_early)

    loop(0, 4, lambda r: wait_ab_start_c(1, r))
    loop(0, 4, lambda r: wait_c(1, r))

    def ffn_in(i):
        rows = pl.ds(pl.multiple_of(512 * (i // 12), 512), 512)
        columns = pl.ds(pl.multiple_of(256 * (i % 12), 256), 256)
        act[rows, columns] = gelu(dot(nlow[rows, :], win[:, columns]) + par[8:9, columns]).astype(BF)

    def ffn_in_and_send(r):
        wait_xy_start_ab(2, r)
        loop(6 * r, 6 * r + 6, ffn_in)

    loop(0, 4, ffn_in_and_send)

    preact_s = dot(cls[NRM : NRM + 16, :].astype(BF), win[...]) + par[8:9, 0:3072]
    pre_s[...] = preact_s
    acts[:, 0:3072] = gelu(preact_s).astype(BF)
    acts[:, 3072:3200] = jnp.zeros((16, 128), BF)

    def window(t):
        return acts.at[:, pl.ds(pl.multiple_of(128 * ((96 * t) // 128), 128), 256)]

    def send_act(i):
        t, device = other(i)
        pltpu.make_async_remote_copy(
            src_ref=window(t),
            dst_ref=actw_in.at[me],
            send_sem=s_act,
            recv_sem=r_act,
            device_id=device,
            device_id_type=MESH,
        ).start()

    loop(1, 32, send_act)
    actw_in[me] = window(me)[...]

    loop(0, 4, lambda r: wait_ab_start_c(2, r))
    loop(0, 4, lambda r: wait_c(2, r))
    keep2 = cls[KEEP2 : KEEP2 + 16, :]
    ffn_s = dot(acts[:, 0:3072], wout[...]) + bias(4)
    hat2, scale2 = standardize(cls[NRM : NRM + 16, :] + ffn_s * keep2)
    final_s = (hat2 * gain(1) + bias(5)) * used16
    length = lax.rsqrt(jnp.sum(final_s * final_s, axis=-1, keepdims=True) + UNIT_EPSILON)
    cls[HAT2 : HAT2 + 16, :] = hat2
    cls[FIN : FIN + 16, :] = final_s
    f3[2 * z + c, 2 * y + x] = (final_s * length).astype(BF)
    start_z(3)
    start_xy(3, 0)

    def ffn_out(i):
        v = i // 2
        rows = pl.ds(pl.multiple_of(256 * (i % 2), 256), 256)
        flat = pl.ds(pl.multiple_of(256 * i, 256), 256)
        out = dot(act[flat, :], wout[...]) + bias(4)
        hat, _ = standardize(normed[v, rows, :] + out * (drop[v, 1, rows, :].astype(F32) * KEEP_SCALE))
        hidden[v, rows, :] = (hat * gain(1) + bias(5)).astype(BF)

    ffn_out(0)
    loop(1, 4, lambda r: wait_z_start_xy(3, r))
    ffn_out(1)
    loop(0, 4, lambda r: wait_xy_start_ab(3, r))
    ffn_out(2)
    loop(0, 4, lambda r: wait_ab_start_c(3, r))
    loop(0, 4, lambda r: wait_c(3, r))

    def part_units(i):
        v = f3[i // 4, i % 4].astype(F32)
        rows = pl.ds(pl.multiple_of(8 * i, 8), 8)
        unit0[rows, :] = v[0:8]
        unit1[rows, :] = v[8:16]

    loop(0, 32, part_units)
    u0, u1 = unit0[...].astype(BF), unit1[...].astype(BF)
    mine = pl.ds(pl.multiple_of(8 * me, 8), 8)
    u0_mine, u1_mine = unit0[mine, :].astype(BF), unit1[mine, :].astype(BF)
    used_row = par[9:10, 0:256]
    eye = hot(256, 256, 0)
    used_col = jnp.sum(jnp.where(eye, used_row, 0.0), axis=1, keepdims=True)
    by_column = jnp.where(used_col > 0.0, dot(u1, u0, LAST) * (1.0 / SOFTMAX_TEMP), NEGATIVE)
    peak = jnp.max(by_column, axis=0, keepdims=True)
    total = peak + jnp.log(jnp.sum(jnp.exp(by_column - peak), axis=0, keepdims=True))
    positive = jnp.sum(jnp.where(eye, by_column, 0.0), axis=0, keepdims=True)
    loss_sum = jnp.sum((total - positive) * used_row, axis=1, keepdims=True)
    loss_ref[...] = loss_sum / jnp.sum(used_row, axis=1, keepdims=True)
    target = as_number(hot(8, 256, 8 * me))
    mine_1 = jnp.where(used_mine > 0.0, dot(u1_mine, u0, LAST) * (1.0 / SOFTMAX_TEMP), NEGATIVE)
    grad_1 = ((jnp.exp(mine_1 - total) - target) * used_row).astype(BF)
    mine_0 = jnp.where(used_row > 0.0, dot(u0_mine, u1, LAST) * (1.0 / SOFTMAX_TEMP), NEGATIVE)
    peak_0 = jnp.max(mine_0, axis=1, keepdims=True)
    total_0 = peak_0 + jnp.log(jnp.sum(jnp.exp(mine_0 - peak_0), axis=1, keepdims=True))
    grad_0 = ((jnp.exp(mine_0 - total_0) - target) * used_mine).astype(BF)
    grad_unit = jnp.concatenate([dot(grad_0, u1), dot(grad_1, u0)], axis=0) * (1.0 / SOFTMAX_TEMP)
    final_s = cls[FIN : FIN + 16, :]
    hat2 = cls[HAT2 : HAT2 + 16, :]
    pull = jnp.sum(grad_unit * final_s, axis=-1, keepdims=True)
    grad_final = (grad_unit - final_s * (pull * length * length)) * length * used16

    grad_mixed_two = norm_back(grad_final * gain(1), hat2, scale2)
    grad_ffn = (grad_mixed_two * cls[KEEP2 : KEEP2 + 16, :]).astype(BF)
    grad_pre = (dot(grad_ffn, wout[...], LAST) * gelu_slope(pre_s[...])).astype(BF)
    f4[2 * z + c, 2 * y + x, :, 0:768] = grad_ffn
    f4[2 * z + c, 2 * y + x, :, 768:3840] = grad_pre
    start_z(4)
    start_xy(4, 0)
    grad_normed = dot(grad_pre, win[...], LAST) + grad_mixed_two
    hat1 = cls[HAT1 : HAT1 + 16, :]
    grad_mixed = norm_back(grad_normed * gain(0), hat1, scale1)
    dropped = grad_mixed * cls[KEEP1 : KEEP1 + 16, :]
    grad_branch = (dropped[0:8] + dropped[8:16]).astype(BF)
    grad_ctx = dot(grad_branch, wqp[:, 2304:3072], LAST).astype(BF)
    loop(1, 4, lambda r: wait_z_start_xy(4, r))
    grad_big = spread(grad_ctx.astype(F32))
    query_big = spread(cls[QRY : QRY + 8, :])
    grad_probs = dot(grad_big, qkv[:, 1536:2304], LAST)
    prob = p_f[...]
    weighted = prob * grad_probs
    grad_scores = (weighted - prob * jnp.sum(weighted, axis=-1, keepdims=True)).astype(BF)
    pairs[0:96, :] = grad_scores
    grad_q = (gathered(dot(grad_scores, qkv[:, 768:1536])) * HD**-0.5).astype(BF)
    own5 = f5.at[2 * z + c, 2 * y + x]
    own5[:, 0:768] = jnp.concatenate([grad_branch.astype(F32), grad_ctx.astype(F32)], axis=0).astype(BF)
    own5[:, 768:1536] = jnp.concatenate([grad_q.astype(F32), cls[QRY : QRY + 8, :]], axis=0).astype(BF)
    start_z(5)
    start_xy(5, 0)
    wait_boxes(early, s_early)
    mixer[0:96, :] = dot(grad_scores, tokens[...])
    value_sum = jnp.sum(pairs[96:192, :].astype(F32), axis=-1, keepdims=True)
    own_sums = [
        jnp.sum(value_sum * grad_big.astype(F32), axis=0, keepdims=True),
        jnp.sum(grad_normed, axis=0, keepdims=True),
        jnp.sum(grad_final, axis=0, keepdims=True),
        jnp.sum(grad_normed * hat1, axis=0, keepdims=True),
        jnp.sum(grad_final * hat2, axis=0, keepdims=True),
    ]
    mixer[96:128, :] = jnp.zeros((32, 768), F32)
    for j, v in enumerate(own_sums):
        upper = v.astype(BF).astype(F32)
        mixer[96 + j : 97 + j, :] = upper
        mixer[104 + j : 105 + j, :] = v - upper
    send_mixer(late, late_in, s_late, r_late)
    loop(0, 4, lambda r: wait_xy_start_ab(4, r))
    loop(1, 4, lambda r: wait_z_start_xy(5, r))

    through[0:96, :] = dot(query_big, wqp[:, 768:1536], LAST).astype(BF)
    through[96:192, :] = dot(grad_big, wqp[:, 1536:2304], LAST).astype(BF)
    start_grad = grad_mixed[0:8] + grad_mixed[8:16] + dot(grad_q, wqp[:, 0:768], LAST)
    upper = start_grad.astype(BF).astype(F32)
    through[192:208, :] = jnp.concatenate([upper, start_grad - upper], axis=0).astype(BF)

    def token_grad(i):
        columns = pl.ds(pl.multiple_of(256 * i, 256), 256)
        gtok[:, columns] = dot(pairs[...], through[:, columns], FIRST)

    loop(0, 3, token_grad)
    loop(0, 4, lambda r: wait_xy_start_ab(5, r))
    ffn_out(3)
    loop(0, 4, lambda r: wait_ab_start_c(4, r))
    loop(0, 4, lambda r: wait_ab_start_c(5, r))
    wait_boxes(actw_in, r_act)
    wait_boxes(early_in, r_early)
    loop(0, 4, lambda r: wait_c(4, r))

    gffn = f4[:, :, :, 0:768].reshape(512, 768)
    act_mine = dot(actw_in[...].reshape(512, 256), as_number(hot_back(256, 128, (96 * me) % 128)).astype(BF)).astype(BF)
    g_out[...] = dot(act_mine, gffn, FIRST)[0:96]
    ones = jnp.ones((16, 512), BF)
    sums[...] = jnp.zeros_like(sums)
    sums[4:5, 0:768] = dot(ones, gffn)[0:1]

    def hidden_sums(i):
        columns = pl.ds(pl.multiple_of(768 + 256 * i, 256), 256)
        sums[8:16, pl.ds(pl.multiple_of(256 * i, 256), 256)] = dot(ones, f4[:, :, :, columns].reshape(512, 256))[0:8]

    loop(0, 12, hidden_sums)
    loop(0, 4, lambda r: wait_c(5, r))
    wait_boxes(late_in, r_late)
    gacc[...] = jnp.zeros_like(gacc)

    def factors(d):
        mix_v = early_in[d][0:24]
        mix_k = late_in[d][0:24]
        f5_d = f5[d // 4, d % 4].astype(F32)
        gbr, gcx = f5_d[0:8, 0:768], f5_d[8:16, 0:768]
        gq, qry = f5_d[0:8, 768:1536], f5_d[8:16, 768:1536]
        g_in_d = dot(mix_v[:, 112:128], f4[d // 4, d % 4, :, 768:3840])
        gacc[0:24, 0:768] += dot(mix_v[:, 104:112], gq.astype(BF))
        gacc[0:24, 768:1536] += dot(mix_k[:, 0:96], spread(qry))
        gacc[0:24, 1536:2304] += dot(mix_v[:, 0:96], spread(gcx))
        gacc[0:24, 2304:3072] += dot(mix_v[:, 96:104], gbr.astype(BF))
        gacc[0:24, 3072:6144] += g_in_d
        gacc[24:48, 0:128] += mix_k.astype(F32)
        gacc[48:56, 0:768] += gq
        gacc[56:64, 0:768] += gbr

    loop(0, 32, factors)
    g_qkv[...] = gacc[0:24, 0:2304]
    g_proj[...] = gacc[0:24, 2304:3072]
    g_in[...] = gacc[0:24, 3072:6144]
    sums[0:1, 0:768] = jnp.sum(gacc[48:56, 0:768], axis=0, keepdims=True)
    sums[2:3, 0:768] = jnp.sum(gacc[56:64, 0:768], axis=0, keepdims=True)
    near = sums[0:8, pl.ds(pl.multiple_of(128 * ((24 * me) // 128), 128), 256)]
    rows_a = dot_exact(near, as_number(hot_back(256, 24, (24 * me) % 128)))
    row_of = lanes((8, 128), 0)
    lane_of = lanes((8, 128), 1)
    chosen = jnp.zeros((8, 128), F32)
    for j, row in enumerate((1, 3, 5, 6, 7)):
        chosen += as_number((row_of == row) & ((lane_of == 96 + j) | (lane_of == 104 + j)))
    rows_b = dot_exact(chosen, gacc[24:48, 0:128], LAST)
    rows_ab = rows_a + rows_b
    g_bias[...] = rows_ab[0:6]
    g_gain[...] = rows_ab[6:8]
    near = sums[8:16, pl.ds(pl.multiple_of(128 * ((96 * me) // 128), 128), 256)]
    g_fbias[...] = dot_exact(near, as_number(hot_back(256, 96, (96 * me) % 128)))[0:1]

    for ph in range(6):
        def sent(r, ph=ph):
            cp_x(ph, r).wait_send()
            cp_y(ph, r).wait_send()
            cp_a(ph, r).wait_send()
            cp_b(ph, r).wait_send()
            cp_c(ph, r).wait_send()
            if ph == 0:
                cp_cp(r).wait_send()

        loop(0, 4, sent)
        loop(1, 4, lambda r, ph=ph: cp_z(ph, r).wait_send())
    wait_boxes(actw_in, s_act)
    wait_boxes(late, s_late)


def hot_back(rows, columns, shift):
    row = lax.broadcasted_iota(jnp.int32, (rows, columns), 0)
    column = lax.broadcasted_iota(jnp.int32, (rows, columns), 1)
    return row == column + shift


def dot_exact(a, b, dims=((1,), (0,))):
    return lax.dot_general(a, b, (dims, ((), ())), preferred_element_type=F32, precision=HIGH)


def encoder_step(
    tokens, qkv_weight, proj_weight, ffn_in_weight, ffn_out_weight, bias_rows, ffn_bias, norm_gains, buckets, padding, dropout
):
    def vm(*shape):
        return pltpu.VMEM(shape, BF)

    def vf(*shape):
        return pltpu.VMEM(shape, F32)

    def sems(*shape):
        return pltpu.SemaphoreType.DMA(shape)

    one = pltpu.SemaphoreType.DMA
    inside = pl.BlockSpec(memory_space=pltpu.VMEM)
    engine = [sems(6, 4)] * 6 + [sems(4)]
    out = pl.pallas_call(
        encoder_kernel,
        name="encoder_step",
        out_shape=[
            jax.ShapeDtypeStruct((2, 512, 768), BF),
            jax.ShapeDtypeStruct((1, 1), F32),
            jax.ShapeDtypeStruct((512, 768), F32),
            jax.ShapeDtypeStruct((24, 2304), F32),
            jax.ShapeDtypeStruct((24, 768), F32),
            jax.ShapeDtypeStruct((24, 3072), F32),
            jax.ShapeDtypeStruct((96, 768), F32),
            jax.ShapeDtypeStruct((6, 24), F32),
            jax.ShapeDtypeStruct((1, 96), F32),
            jax.ShapeDtypeStruct((2, 24), F32),
        ],
        in_specs=[inside] * 10 + [pl.BlockSpec(memory_space=pl.ANY)],
        out_specs=[inside] * 10,
        scratch_shapes=[
            vm(768, PW), vm(768, 3072), vm(3072, 768),
            vm(4, 2, 2, 16, WIDE + SW), vm(4, 2, 2, 16, WIDE), vm(4, 2, 2, 16, WIDE),
            vm(8, 4, 16, 768), vm(8, 4, 16, 3840), vm(8, 4, 16, 1536),
            vm(8, 4, 16, SW), vf(16, SW), vf(16, 3328),
            pltpu.VMEM((2, 2, 512, 768), jnp.int32), vm(512, 2304), vf(512, 512), vm(512, 768),
            vf(2, 512, 768), vm(1024, 768), vm(1024, 3072),
            vf(120, 768), vf(8, 512), vm(8, 512), vf(16, 3072), vm(16, 3200), vf(96, 512),
            vm(208, 512), vm(208, 768), vf(128, 768), vf(768, 128), vf(256, 768), vf(256, 768), vf(16, 3328), vf(64, 6144),
            vm(32, 32, 128), vm(32, 32, 128), vm(32, 32, 128), vm(32, 32, 128), vm(32, 16, 256),
        ] + engine + engine + [one] * 7,
        compiler_params=pltpu.CompilerParams(
            collective_id=0, has_side_effects=True, vmem_limit_bytes=63 * 2**20
        ),
    )(
        qkv_weight, proj_weight, ffn_in_weight, ffn_out_weight, bias_rows, norm_gains,
        ffn_bias[None], tokens, buckets, padding[None], dropout,
    )
    hidden, loss, gtok, g_qkv, g_proj, g_in, g_out, g_bias, g_fbias, g_gain = out
    return (hidden, loss[0, 0], gtok, g_qkv, g_proj, g_in, g_out, g_bias, g_fbias[0], g_gain)


def solution(mesh):
    in_specs = (
        P(AXES, None),
        P(AXES, None),
        P(AXES, None),
        P(AXES, None),
        P(AXES, None),
        P(None, AXES),
        P(AXES),
        P(None, AXES),
        P(AXES, None),
        P(AXES),
        P(None, None, AXES, None),
    )
    out_specs = (
        P(None, AXES, None),
        P(),
        P(AXES, None),
        P(AXES, None),
        P(AXES, None),
        P(AXES, None),
        P(AXES, None),
        P(None, AXES),
        P(AXES),
        P(None, AXES),
    )
    grid_fits = mesh.shape["dp"] == 8 and mesh.shape["fsdp"] == 4
    return jax.shard_map(
        encoder_step if grid_fits else with_collectives, mesh=mesh, in_specs=in_specs, out_specs=out_specs, check_vma=False
    )
```

```python
import functools

import jax
import jax.numpy as jnp
from jax import lax
from jax.experimental import pallas as pl
from jax.experimental.pallas import tpu as pltpu
from jax.sharding import PartitionSpec as P

H = 12
HD = 64

NEGATIVE = -1e30
NORM_EPSILON = 1e-12
UNIT_EPSILON = 1e-06
SOFTMAX_TEMP = 0.05
KEEP_SCALE = 1.0 / 0.9
FULL_PRECISION = lax.Precision.HIGHEST
AXES = ("dp", "fsdp")
BF = jnp.bfloat16
F32 = jnp.float32


def dot(a, b, dims=((1,), (0,))):
    return lax.dot_general(a, b, (dims, ((), ())), preferred_element_type=F32)


def layer_norm(inputs, gain_vec, shift_vec):
    centre = inputs - jnp.mean(inputs, axis=-1, keepdims=True)
    spread = jnp.mean(centre * centre, axis=-1, keepdims=True)
    return centre * lax.rsqrt(spread + NORM_EPSILON) * gain_vec + shift_vec


def normalize(inputs):
    return inputs * lax.rsqrt(jnp.sum(inputs * inputs, axis=-1, keepdims=True) + UNIT_EPSILON)


def exact_gelu(inputs):
    return jax.nn.gelu(inputs, approximate=False)


def sentence_layout(bucket_row, pad_row, rows_here):
    row_ids = jnp.arange(rows_here, dtype=jnp.int32)
    starts = jnp.cumsum(bucket_row) - bucket_row
    used = bucket_row > 0
    member = (row_ids[:, None] >= starts[None, :]) & used[None, :]
    sentence = jnp.sum(member.astype(jnp.int32), axis=1)
    allowed = (sentence[:, None] == sentence[None, :]) & (pad_row[None, :] > 0)
    select = ((row_ids[None, :] == starts[:, None]) & used[:, None]).astype(jnp.float32)
    slot_allowed = (
        (sentence[None, :] == jnp.arange(1, bucket_row.shape[0] + 1)[:, None])
        & used[:, None]
        & (pad_row[None, :] > 0)
    )
    return (allowed, select, slot_allowed)


def gather(x, axis=0):
    return lax.all_gather(x, AXES, axis=axis, tiled=True)


def all_to_all(x):
    return lax.all_to_all(x, AXES, split_axis=0, concat_axis=0, tiled=True)


def with_collectives(
    tokens,
    qkv_weight,
    proj_weight,
    ffn_in_weight,
    ffn_out_weight,
    bias_rows,
    ffn_bias,
    norm_gains,
    buckets,
    padding,
    dropout,
):
    rows_here, width = tokens.shape
    slots = buckets.shape[1]
    hidden = ffn_in_weight.shape[1]
    small = bias_rows.shape[1]
    devices = width // small
    hidden_small = hidden // devices
    me = lax.axis_index(AXES)
    score_scale = HD ** (-0.5)
    used_slot = (buckets[0] > 0).astype(BF)

    params = jnp.concatenate(
        [bias_rows.reshape(-1), norm_gains.reshape(-1), ffn_bias, used_slot]
    )
    params_all = gather(params[None])
    qp = gather(jnp.concatenate([qkv_weight, proj_weight], axis=1))
    qkv_full, proj_full = qp[:, : 3 * width], qp[:, 3 * width :]
    in_full = gather(ffn_in_weight)
    out_full = gather(ffn_out_weight)
    rows8 = params_all[:, : 8 * small].reshape(devices, 8, small).transpose(1, 0, 2)
    rows8 = rows8.reshape(8, width).astype(F32)
    bias_f, gain_f = rows8[:6], rows8[6:]
    ffn_bias_f = params_all[:, 8 * small : 8 * small + hidden_small].reshape(-1).astype(F32)
    used_all = params_all[:, 8 * small + hidden_small :].reshape(-1)

    allowed, select, slot_allowed = sentence_layout(buckets[0], padding, rows_here)
    select_low = select.astype(BF)
    zero_row = jnp.zeros((width,), F32)
    qkv = (dot(tokens, qkv_full) + jnp.concatenate([bias_f[0], zero_row, bias_f[1]])).astype(BF)
    head_view = qkv.reshape(rows_here, 3, H, HD)
    queries, key_rows, value_rows = (head_view[:, 0], head_view[:, 1], head_view[:, 2])

    scores = (
        jnp.einsum("qhd,khd->hqk", queries, key_rows, preferred_element_type=F32) * score_scale
    )
    scores = jnp.where(allowed[None], scores, NEGATIVE)
    exp_scores = jnp.exp(scores - jnp.max(scores, axis=-1, keepdims=True))
    probability = (exp_scores / jnp.sum(exp_scores, axis=-1, keepdims=True)).astype(BF)
    context = jnp.einsum("hqk,khd->qhd", probability, value_rows, preferred_element_type=F32)
    context = context.reshape(rows_here, width).astype(BF)
    branch = dot(context, proj_full) + bias_f[2]
    keep_mask = dropout.astype(F32)
    mixed_one = tokens.astype(F32)[None] + branch[None] * keep_mask[:, 0] * KEEP_SCALE
    normed = layer_norm(mixed_one, gain_f[0], bias_f[3])
    normed_low = normed.astype(BF)
    preact = dot(normed_low.reshape(-1, width), in_full) + ffn_bias_f
    activation = exact_gelu(preact).astype(BF)
    ffn_out = (dot(activation, out_full) + bias_f[4]).reshape(normed.shape)
    mixed_two = normed + ffn_out * keep_mask[:, 1] * KEEP_SCALE
    hidden_out = layer_norm(mixed_two, gain_f[1], bias_f[5]).astype(BF)

    tokens_s = dot(select_low, tokens)
    qkv_s = dot(select_low, qkv).astype(BF)
    queries_s = qkv_s[:, :width].reshape(slots, H, HD)
    scores_s = (
        jnp.einsum("shd,khd->hsk", queries_s, key_rows, preferred_element_type=F32) * score_scale
    )
    scores_s = jnp.where(slot_allowed[None], scores_s, NEGATIVE)
    peak_s = jnp.max(scores_s, axis=-1, keepdims=True)
    exp_s = jnp.exp(scores_s - peak_s) * slot_allowed[None].astype(F32)
    probability_f = exp_s / jnp.maximum(jnp.sum(exp_s, axis=-1, keepdims=True), 1e-30)
    probability_s = probability_f.astype(BF)
    context_s = dot(select_low, context).astype(BF)
    branch_s = dot(context_s, proj_full) + bias_f[2]
    keep_s = jnp.einsum(
        "sr,vbrd->vbsd", select_low, dropout.astype(BF), preferred_element_type=F32
    )
    mixed_s = tokens_s[None] + branch_s[None] * keep_s[:, 0] * KEEP_SCALE
    normed_s, first_back = jax.vjp(layer_norm, mixed_s, gain_f[0], bias_f[3])
    normed_s_low = normed_s.astype(BF).reshape(2 * slots, width)
    preact_s = dot(normed_s_low, in_full) + ffn_bias_f
    activation_sf, gelu_back = jax.vjp(exact_gelu, preact_s)
    activation_s = activation_sf.astype(BF)
    ffn_out_s = (dot(activation_s, out_full) + bias_f[4]).reshape(normed_s.shape)
    mixed_two_s = normed_s + ffn_out_s * keep_s[:, 1] * KEEP_SCALE
    final_s, second_back = jax.vjp(layer_norm, mixed_two_s, gain_f[1], bias_f[5])
    used_f = used_slot.astype(F32)
    final_s = final_s * used_f[None, :, None]
    unit_s, unit_back = jax.vjp(normalize, final_s)
    unit_low = unit_s.astype(BF)

    unit_all = gather(unit_low.reshape(1, 2, slots, width))
    unit_0 = unit_all[:, 0].reshape(-1, width)
    unit_1 = unit_all[:, 1].reshape(-1, width)
    logits = dot(unit_0, unit_1, ((1,), (1,))) / SOFTMAX_TEMP
    logits = jnp.where(used_all[None, :] > 0, logits, NEGATIVE)
    total = unit_0.shape[0]
    ids = jnp.arange(total, dtype=jnp.int32)
    diagonal = ids[:, None] == ids[None, :]
    logit_peak = jnp.max(logits, axis=-1, keepdims=True)
    logit_total = logit_peak[:, 0] + jnp.log(jnp.sum(jnp.exp(logits - logit_peak), axis=-1))
    positive = jnp.sum(jnp.where(diagonal, logits, 0.0), axis=1)
    used_all_f = used_all.astype(F32)
    loss_mean = jnp.sum((logit_total - positive) * used_all_f) / jnp.sum(used_all_f)
    soft = jnp.exp(logits - logit_total[:, None])
    logit_gradient = ((soft - diagonal.astype(F32)) * used_all_f[:, None]).astype(BF)
    mine_rows = lax.dynamic_slice_in_dim(logit_gradient, me * slots, slots, 0)
    mine_columns = lax.dynamic_slice_in_dim(logit_gradient, me * slots, slots, 1)
    grad_unit = jnp.stack(
        [dot(mine_rows, unit_1), dot(mine_columns, unit_0, ((0,), (0,)))]
    ) / SOFTMAX_TEMP
    (grad_final,) = unit_back(grad_unit)
    grad_final = grad_final * used_f[None, :, None]
    grad_mixed_two, grad_gain_two, grad_shift_two = second_back(grad_final)
    grad_ffn = (grad_mixed_two * keep_s[:, 1] * KEEP_SCALE).astype(BF).reshape(-1, width)
    grad_shift_out = jnp.sum(grad_ffn.astype(F32), axis=0)
    grad_act = dot(grad_ffn, out_full, ((1,), (1,)))
    (grad_preact_f,) = gelu_back(grad_act)
    grad_preact = grad_preact_f.astype(BF)
    grad_hidden_bias = jnp.sum(grad_preact.astype(F32), axis=0)
    grad_normed = dot(grad_preact, in_full, ((1,), (1,))).reshape(normed_s.shape) + grad_mixed_two
    grad_mixed, grad_gain_one, grad_shift_one = first_back(grad_normed)
    grad_branch = jnp.sum(grad_mixed * keep_s[:, 0] * KEEP_SCALE, axis=0).astype(BF)
    grad_shift_proj = jnp.sum(grad_branch.astype(F32), axis=0)
    grad_context = dot(grad_branch, proj_full, ((1,), (1,))).astype(BF)
    grad_context_h = grad_context.reshape(slots, H, HD)
    grad_probs = jnp.einsum(
        "shd,khd->hsk", grad_context_h, value_rows, preferred_element_type=F32
    )
    inner = jnp.sum(probability_f * grad_probs, axis=-1, keepdims=True)
    grad_scores = (probability_f * (grad_probs - inner)).astype(BF)
    grad_queries = (
        (jnp.einsum("hsk,khd->shd", grad_scores, key_rows, preferred_element_type=F32) * score_scale)
        .reshape(slots, width)
        .astype(BF)
    )
    pairs = jnp.concatenate([grad_scores, probability_s], axis=0).reshape(2 * H * slots, rows_here)
    token_sums = dot(pairs, tokens).astype(BF)
    key_factor = (queries_s.astype(F32) * score_scale).astype(BF)
    back_w = qkv_full.reshape(width, 3, H, HD)
    through = jnp.concatenate(
        [
            jnp.einsum("shd,whd->hsw", key_factor, back_w[:, 1], preferred_element_type=F32),
            jnp.einsum("shd,whd->hsw", grad_context_h, back_w[:, 2], preferred_element_type=F32),
        ],
        axis=0,
    ).reshape(2 * H * slots, width)
    start_grad = jnp.sum(grad_mixed, axis=0) + dot(
        grad_queries, qkv_full[:, :width], ((1,), (1,))
    )
    grad_tokens = dot(pairs, through.astype(BF), ((0,), (0,))) + lax.dot_general(
        select, start_grad, (((0,), (0,)), ((), ())), precision=FULL_PRECISION
    )
    value_sum = jnp.sum(probability_s.astype(F32), axis=-1).T
    grad_shift_value = jnp.sum(value_sum[:, :, None] * grad_context_h.astype(F32), axis=0).reshape(-1)
    grad_shift_query = jnp.sum(grad_queries.astype(F32), axis=0)

    wide = gather(jnp.concatenate([grad_ffn, grad_preact], axis=1))
    gffn_all, gpre_all = wide[:, :width], wide[:, width:]
    narrow = gather(
        jnp.concatenate([grad_branch, key_factor.reshape(slots, width), grad_context, grad_queries], axis=1)
    )
    gbranch_all = narrow[:, :width]
    key_all = narrow[:, width : 2 * width].reshape(-1, H, HD)
    gctx_all = narrow[:, 2 * width : 3 * width].reshape(-1, H, HD)
    gq_all = narrow[:, 3 * width :]

    def cut(x, n):
        return x.reshape(x.shape[0], devices, n).transpose(1, 0, 2).reshape(devices, -1)

    bias_sums = jnp.concatenate(
        [
            jnp.stack(
                [
                    grad_shift_query,
                    grad_shift_value,
                    grad_shift_proj,
                    grad_shift_one,
                    grad_shift_out,
                    grad_shift_two,
                    grad_gain_one,
                    grad_gain_two,
                ]
            )
            .reshape(8, devices, small)
            .transpose(1, 0, 2)
            .reshape(devices, -1),
            grad_hidden_bias.reshape(devices, -1),
        ],
        axis=1,
    )
    high = bias_sums.astype(BF)
    lower = (bias_sums - high.astype(F32)).astype(BF)
    pieces = [
        cut(activation_s, hidden_small),
        cut(normed_s_low, small),
        cut(context_s, small),
        cut(tokens_s.astype(BF), small),
        cut(token_sums, small),
        high,
        lower,
    ]
    sizes = [p.shape[1] for p in pieces]
    received = all_to_all(jnp.concatenate(pieces, axis=1))
    ends = []
    at = 0
    for n in sizes:
        ends.append(received[:, at : at + n])
        at += n
    act_r = ends[0].reshape(-1, hidden_small)
    normed_r = ends[1].reshape(-1, small)
    ctx_r = ends[2].reshape(-1, small)
    tok_r = ends[3].reshape(-1, small)
    sums_r = ends[4].reshape(devices, 2, H, slots, small)
    bias_r = jnp.sum(ends[5].astype(F32) + ends[6].astype(F32), axis=0)

    grad_out_weight = dot(act_r, gffn_all, ((0,), (0,)))
    grad_in_weight = dot(normed_r, gpre_all, ((0,), (0,)))
    grad_proj = dot(ctx_r, gbranch_all, ((0,), (0,)))
    grad_q = dot(tok_r, gq_all, ((0,), (0,)))
    keys_r = sums_r[:, 0].transpose(1, 0, 2, 3).reshape(H, -1, small)
    values_r = sums_r[:, 1].transpose(1, 0, 2, 3).reshape(H, -1, small)
    grad_k = jnp.einsum("hnw,nhd->whd", keys_r, key_all, preferred_element_type=F32)
    grad_v = jnp.einsum("hnw,nhd->whd", values_r, gctx_all, preferred_element_type=F32)
    grad_qkv_weight = jnp.concatenate(
        [grad_q, grad_k.reshape(small, width), grad_v.reshape(small, width)], axis=1
    )
    bias8 = bias_r[: 8 * small].reshape(8, small)
    return (
        hidden_out,
        loss_mean,
        grad_tokens,
        grad_qkv_weight,
        grad_proj,
        grad_in_weight,
        grad_out_weight,
        bias8[:6],
        bias_r[8 * small :],
        bias8[6:],
    )


MESH = pl.DeviceIdType.MESH
PW, QW, SW = 3072, 1536, 256
WIDE = PW + QW
HIGH = lax.Precision.HIGHEST
LAST = ((1,), (1,))
FIRST = ((0,), (0,))
WHOLE = (WIDE + SW, WIDE, WIDE, 768, 3840, 1536)


def place():
    dp = lax.axis_index("dp")
    fs = lax.axis_index("fsdp")
    return dp // 2, dp % 2, fs // 2, fs % 2


def peer_z(z, r):
    return (z + r) % 2 + 2 * ((z // 2 + r // 2) % 2)


def hot(rows, columns, shift):
    row = lax.broadcasted_iota(jnp.int32, (rows, columns), 0)
    column = lax.broadcasted_iota(jnp.int32, (rows, columns), 1)
    return row + shift == column


def as_number(flags):
    return jnp.where(flags, 1.0, 0.0)


def tail_of(x):
    t = 1.0 / (1.0 + (0.3275911 * 0.7071067811865476) * jnp.abs(x))
    bell = jnp.exp(x * x * -0.5)
    poly = 0.5 * 1.061405429
    for c in (-1.453152027, 1.421413741, -0.284496736, 0.254829592):
        poly = poly * t + 0.5 * c
    return poly * t * bell, bell


def gelu(x):
    tail, _ = tail_of(x)
    return jnp.maximum(x, 0.0) - jnp.abs(x) * tail


def gelu_slope(x):
    tail, bell = tail_of(x)
    return jnp.where(x >= 0.0, 1.0 - tail, tail) + x * bell * 0.3989422804014327


def mean(x):
    return jnp.sum(x, axis=-1, keepdims=True) * (1.0 / x.shape[-1])


def standardize(x):
    centre = x - mean(x)
    scale = lax.rsqrt(mean(centre * centre) + NORM_EPSILON)
    return centre * scale, scale


def norm_back(grad_hat, hat, scale):
    return scale * (grad_hat - mean(grad_hat) - hat * mean(grad_hat * hat))


def encoder_kernel(
    qkv_ref, proj_ref, in_ref, out_ref, bias_ref, gain_ref, fbias_ref, tokens, buckets_ref, pad_ref, drop_hbm,
    hidden_hbm, loss_ref, gtok_hbm, g_qkv, g_proj, g_in, g_out, g_bias, g_fbias, g_gain,
    wqp, win, wout, l0, l1, l2, f3, f4, f5, pb, stage, par,
    drop, qkv, madd, ctx, normed, nlow, act,
    cls, sm8, sel, pre_s, acts, p_f, pairs, through, mixer, mixer_t, unit0, unit1, sums,
    early, early_in, late, late_in, actw_in, gtok, keys_t, values1, mix_n, mix_c, mix_t, rest,
    sz, sx, sy, sa, sb, sc, scp, rz, rx, ry, ra, rb, rc, rcp, s_early, r_early, s_act, r_act, s_late, r_late, s_drop, s_hid, s_tok,
):
    z, c, y, x = place()
    me = 8 * z + 4 * c + 2 * y + x
    land = (l0, l1, l2)
    full = (f3, f4, f5)
    weights = (wqp, win, wout)
    lanes = functools.partial(lax.broadcasted_iota, jnp.int32)

    def dev(z_, c_, y_, x_):
        return (2 * z_ + c_, 2 * y_ + x_)

    def other(i):
        t = (me + i) % 32
        return t, (t // 4, t % 4)

    def loop(lo, hi, body):
        def step(i, carry):
            body(i)
            return carry

        lax.fori_loop(lo, hi, step, 0)

    bar = pltpu.get_barrier_semaphore()

    def greet(i):
        _, device = other(i)
        pl.semaphore_signal(bar, inc=1, device_id=device, device_id_type=MESH)

    loop(1, 32, greet)
    drop_copy = pltpu.make_async_copy(drop_hbm.at[:, 0], drop, s_drop.at[0])
    drop_copy.start()

    def slot(ph, zz, yy, xx):
        if ph < 3:
            return land[ph].at[zz, yy, xx]
        return full[ph - 3].at[2 * zz + c, 2 * yy + xx]

    def rcopy(ref, s, r, device):
        return pltpu.make_async_remote_copy(
            src_ref=ref, dst_ref=ref, send_sem=s, recv_sem=r, device_id=device, device_id_type=MESH
        )

    def cp_z(ph, r):
        return rcopy(slot(ph, z, y, x), sz.at[ph, r], rz.at[ph, r], dev(peer_z(z, r), c, y, x))

    def cp_x(ph, r):
        return rcopy(slot(ph, peer_z(z, r), y, x), sx.at[ph, r], rx.at[ph, r], dev(z, c, y, 1 - x))

    def cp_y(ph, r):
        return rcopy(slot(ph, peer_z(z, r), y, x), sy.at[ph, r], ry.at[ph, r], dev(z, c, 1 - y, x))

    def half(ph):
        return WHOLE[ph] // 256 * 128

    def cp_a(ph, r):
        ref = slot(ph, peer_z(z, r), y, 1 - x).at[:, 0 : half(ph)]
        return rcopy(ref, sa.at[ph, r], ra.at[ph, r], dev(z, c, 1 - y, x))

    def cp_b(ph, r):
        ref = slot(ph, peer_z(z, r), 1 - y, x).at[:, half(ph) : WHOLE[ph]]
        return rcopy(ref, sb.at[ph, r], rb.at[ph, r], dev(z, c, y, 1 - x))

    def cp_c(ph, r):
        group = 2 * peer_z(z, r) + c
        if ph < 3:
            n = 384 if ph == 2 else 96
            ref = weights[ph].at[pl.ds(pl.multiple_of(n * group, n), n)]
        else:
            ref = full[ph - 3].at[group]
        return rcopy(ref, sc.at[ph, r], rc.at[ph, r], dev(z, 1 - c, y, x))

    def cp_cp(r):
        return rcopy(pb.at[2 * peer_z(z, r) + c], scp.at[r], rcp.at[r], dev(z, 1 - c, y, x))

    def start_z(ph):
        loop(1, 4, lambda r: cp_z(ph, r).start())

    def start_xy(ph, r):
        cp_x(ph, r).start()
        cp_y(ph, r).start()

    def wait_z_start_xy(ph, r):
        cp_z(ph, r).wait_recv()
        start_xy(ph, r)

    def wait_xy_start_ab(ph, r):
        cp_x(ph, r).wait_recv()
        cp_a(ph, r).start()
        cp_y(ph, r).wait_recv()
        cp_b(ph, r).start()

    def merge(ph, r):
        zz = peer_z(z, r)
        group = 2 * zz + c
        if ph == 2:
            for yy in range(2):
                for xx in range(2):
                    base = 384 * group + 96 * (2 * yy + xx)
                    for j in range(6):
                        wout[pl.ds(pl.multiple_of(base + 16 * j, 16), 16), :] = l2[
                            zz, yy, xx, :, 768 * j : 768 * (j + 1)
                        ]
            return
        w = weights[ph]
        l = land[ph]
        spans = [(0, 2304, PW), (2304, 768, PW + 1152)] if ph == 0 else [(0, 3072, PW)]
        for yy in range(2):
            base = 96 * group + 48 * yy
            w[pl.ds(pl.multiple_of(base, 16), 16), :] = l[zz, yy, 0, :, 0:PW]
            w[pl.ds(pl.multiple_of(base + 32, 16), 16), :] = l[zz, yy, 1, :, 0:PW]
            middle = pl.ds(pl.multiple_of(base + 16, 16), 16)
            for at, n, qat in spans:
                qe = l[zz, yy, 0, :, qat : qat + n // 2].astype(F32)
                qo = l[zz, yy, 1, :, qat : qat + n // 2].astype(F32)
                w[middle, at : at + n // 2] = jnp.concatenate([qe[0:8], qo[0:8]], axis=0).astype(BF)
                w[middle, at + n // 2 : at + n] = jnp.concatenate([qe[8:16], qo[8:16]], axis=0).astype(BF)
        if ph == 0:
            for yy in range(2):
                for xx in range(2):
                    pb[group, 2 * yy + xx] = l0[zz, yy, xx, :, WIDE:]

    def wait_ab_start_c(ph, r):
        cp_a(ph, r).wait_recv()
        cp_b(ph, r).wait_recv()
        if ph < 3:
            merge(ph, r)
        cp_c(ph, r).start()
        if ph == 0:
            cp_cp(r).start()

    def wait_c(ph, r):
        cp_c(ph, r).wait_recv()
        if ph == 0:
            cp_cp(r).wait_recv()

    def pack(ph, parts):
        at, qat = 0, PW
        for ref in parts:
            v = ref[...].astype(F32)
            n = v.shape[1]
            p_rows = jnp.where(x == 0, v[0:16], v[8:24])
            q_rows = jnp.where(x == 0, v[16:24], v[0:8])
            land[ph][z, y, x, :, at : at + n] = p_rows.astype(BF)
            land[ph][z, y, x, :, qat : qat + n // 2] = jnp.concatenate(
                [q_rows[:, : n // 2], q_rows[:, n // 2 :]], axis=0
            ).astype(BF)
            at += n
            qat += n // 2

    pack(0, (qkv_ref, proj_ref))

    def put(v, shift):
        return dot(v.astype(BF), as_number(hot(v.shape[1], SW, shift)).astype(BF))

    bk = buckets_ref[...].astype(F32)
    stage[...] = jnp.zeros_like(stage)
    stage[0:6, :] = put(bias_ref[...], (24 * me) % 128)
    stage[6:8, :] = put(gain_ref[...], (24 * me) % 128)
    stage[8:9, :] = put(fbias_ref[...], (96 * me) % 128)
    stage[9:10, :] = put(as_number(bk > 0.0), (8 * me) % 128)
    l0[z, y, x, :, WIDE:] = stage[...].astype(BF)
    pl.semaphore_wait(bar, 31)

    start_z(0)
    start_xy(0, 0)
    pack(1, (in_ref,))
    for j in range(6):
        l2[z, y, x, :, 768 * j : 768 * (j + 1)] = out_ref[16 * j : 16 * (j + 1), :]

    row8, lane8 = lanes((8, 8), 0), lanes((8, 8), 1)
    bk_col = jnp.sum(jnp.where(row8 == lane8, bk, 0.0), axis=1, keepdims=True)
    starts_col = jnp.sum(jnp.where(lane8 < row8, bk, 0.0), axis=1, keepdims=True)
    starts_row = jnp.sum(jnp.where(row8 < lane8, bk_col, 0.0), axis=0, keepdims=True)
    used_mine = as_number(bk_col > 0.0)
    used16 = jnp.concatenate([used_mine, used_mine], axis=0)
    row_ids = lanes((512, 8), 0).astype(F32)
    column_ids = lanes((8, 512), 1).astype(F32)
    sent_row = jnp.sum(as_number((row_ids >= starts_row) & (bk > 0.0)), axis=1, keepdims=True)
    sent_col = jnp.sum(as_number((column_ids >= starts_col) & (bk_col > 0.0)), axis=0, keepdims=True)
    key_of = jnp.where(pad_ref[...] > 0, sent_col, 0.0)
    madd[...] = jnp.where(sent_row == key_of, 0.0, NEGATIVE)
    sm8[...] = as_number(key_of == (lanes((8, 512), 0) + 1).astype(F32))
    sel[...] = as_number((column_ids == starts_col) & (bk_col > 0.0)).astype(BF)

    wait_z_start_xy(0, 1)
    wait_xy_start_ab(0, 0)
    wait_z_start_xy(0, 2)
    wait_z_start_xy(0, 3)
    start_z(1)
    start_xy(1, 0)
    loop(1, 4, lambda r: wait_xy_start_ab(0, r))
    loop(1, 4, lambda r: wait_z_start_xy(1, r))
    start_z(2)
    loop(0, 4, lambda r: wait_ab_start_c(0, r))
    drop_copy.wait()
    loop(0, 4, lambda r: wait_c(0, r))
    par[...] = jnp.zeros_like(par)
    for d in range(32):
        w = pb[d // 4, d % 4].astype(F32)
        t, t2, t3 = 24 * d // 128, 96 * d // 128, 8 * d // 128
        par[0:8, 128 * t : 128 * t + 256] += w[0:8]
        par[8:9, 128 * t2 : 128 * t2 + 256] += w[8:9]
        par[9:10, 128 * t3 : 128 * t3 + 256] += w[9:10]

    def bias(i):
        return par[i : i + 1, 0:768]

    def gain(i):
        return par[6 + i : 7 + i, 0:768]

    def qkv_part(i):
        columns = pl.ds(pl.multiple_of(256 * i, 256), 256)
        inside = pl.ds(pl.multiple_of(256 * (i % 3), 256), 256)
        both = par[0:8, inside]
        part = jnp.where(i < 3, both[0:1], jnp.where(i < 6, 0.0, both[1:2]))
        qkv[:, columns] = (dot(tokens[...], wqp[:, columns]) + part).astype(BF)

    loop(0, 9, qkv_part)
    wait_xy_start_ab(1, 0)
    wait_z_start_xy(2, 1)
    start_xy(2, 0)

    left = lanes((1, 128), 1) < 64
    left_scale = jnp.where(left, HD**-0.5, 0.0)
    right_scale = jnp.where(left, 0.0, HD**-0.5)

    def turn_keys(i):
        columns = pl.ds(pl.multiple_of(768 + 128 * i, 128), 128)
        keys_t[pl.ds(pl.multiple_of(128 * i, 128), 128), :] = jnp.transpose(qkv[:, columns].astype(F32)).astype(BF)

    loop(0, 6, turn_keys)
    values1[:, 128:256] = jnp.ones((512, 128), BF)

    def attend(pair):
        def columns(part):
            return pl.ds(pl.multiple_of(768 * part + 128 * pair, 128), 128)

        values1[:, 0:128] = qkv[:, columns(2)]

        def block(i):
            rows = pl.ds(pl.multiple_of(128 * i, 128), 128)
            q = qkv[rows, columns(0)].astype(F32)
            results = []
            for scale in (left_scale, right_scale):
                s = dot((q * scale).astype(BF), keys_t[columns(0), :]) + madd[rows, :]
                e = jnp.exp(s - jnp.max(s, axis=-1, keepdims=True)).astype(BF)
                both = dot(e, values1[...])
                results.append(both[:, 0:128] * (1.0 / both[:, 128:256]))
            ctx[rows, columns(0)] = jnp.where(left, results[0], results[1]).astype(BF)

        loop(0, 4, block)

    attend(0)
    wait_xy_start_ab(1, 1)
    attend(1)
    wait_z_start_xy(2, 2)
    attend(2)
    wait_xy_start_ab(1, 2)
    attend(3)
    wait_z_start_xy(2, 3)
    attend(4)
    wait_xy_start_ab(1, 3)
    attend(5)
    wait_xy_start_ab(2, 0)

    def first_norm(i):
        rows = pl.ds(pl.multiple_of(128 * i, 128), 128)
        branch = (dot(ctx[rows, :], wqp[:, 2304:3072]) + bias(2)) * KEEP_SCALE
        token_rows = tokens[rows, :].astype(F32)
        for v in range(2):
            hat, _ = standardize(token_rows + branch * drop[v, rows, :].astype(F32))
            n = hat * gain(0) + bias(3)
            normed[v, rows, :] = n
            nlow[pl.ds(pl.multiple_of(512 * v + 128 * i, 128), 128), :] = n.astype(BF)

    loop(0, 4, first_norm)

    TOK, QRY, CTX, KEEP1, KEEP2, HAT1, NRM, HAT2, FIN = 0, 8, 16, 24, 40, 56, 72, 88, 104
    pick = sel[...]
    cls[TOK : TOK + 8, :] = dot(pick, tokens[...])
    cls[QRY : QRY + 8, :] = dot(pick, qkv[:, 0:768]) * HD**-0.5
    cls[CTX : CTX + 8, :] = dot(pick, ctx[...])
    for v in range(2):
        cls[KEEP1 + 8 * v : KEEP1 + 8 * v + 8, :] = dot(pick, drop[v].astype(F32).astype(BF)) * KEEP_SCALE
    drop_copy = pltpu.make_async_copy(drop_hbm.at[:, 1], drop, s_drop.at[1])
    drop_copy.start()

    def twice(v):
        return jnp.concatenate([v, v], axis=0)

    head = lax.broadcasted_iota(jnp.int32, (12, 8, 768), 0) * 64
    lane = lax.broadcasted_iota(jnp.int32, (12, 8, 768), 2)
    own_head = (lane >= head) & (lane < head + 64)

    def spread(rows8):
        return jnp.where(own_head, rows8[None], 0.0).reshape(96, 768).astype(BF)

    def gathered(rows96):
        return jnp.sum(jnp.where(own_head, rows96.reshape(12, 8, 768), 0.0), axis=0)

    branch_s = dot(cls[CTX : CTX + 8, :].astype(BF), wqp[:, 2304:3072]) + bias(2)
    hat1, scale1 = standardize(twice(cls[TOK : TOK + 8, :]) + twice(branch_s) * cls[KEEP1 : KEEP1 + 16, :])
    normed_s = hat1 * gain(0) + bias(3)
    cls[HAT1 : HAT1 + 16, :] = hat1
    cls[NRM : NRM + 16, :] = normed_s
    query_big = spread(cls[QRY : QRY + 8, :])
    seen = jnp.broadcast_to(sm8[...][None], (12, 8, 512)).reshape(96, 512)
    s = jnp.where(seen > 0.0, dot(query_big, qkv[:, 768:1536], LAST), NEGATIVE)
    e = jnp.exp(s - jnp.max(s, axis=-1, keepdims=True)) * seen
    prob = e * (1.0 / jnp.maximum(jnp.sum(e, axis=-1, keepdims=True), 1e-30))
    p_f[...] = prob
    pairs[96:192, :] = prob.astype(BF)
    pairs[192:208, :] = twice(pick.astype(F32)).astype(BF)
    mixer[0:96, :] = dot(prob.astype(BF), tokens[...])
    mixer[96:104, :] = cls[CTX : CTX + 8, :]
    mixer[104:112, :] = cls[TOK : TOK + 8, :]
    mixer[112:128, :] = normed_s

    def send_mixer(box, box_in, s_sem, r_sem):
        mixer_t[...] = jnp.transpose(mixer[...])

        def cut(t):
            v = mixer_t[pl.ds(pl.multiple_of(24 * t, 8), 24), :]
            box[t] = jnp.concatenate([v, jnp.zeros((8, 128), F32)], axis=0).astype(BF)

        loop(0, 32, cut)
        box_in[me] = box[me]

        def send(i):
            t, device = other(i)
            pltpu.make_async_remote_copy(
                src_ref=box.at[t],
                dst_ref=box_in.at[me],
                send_sem=s_sem,
                recv_sem=r_sem,
                device_id=device,
                device_id_type=MESH,
            ).start()

        loop(1, 32, send)

    def wait_boxes(ref, sem):
        part = ref.at[pl.ds(0, 31)]
        pltpu.make_async_copy(part, part, sem).wait()

    send_mixer(early, early_in, s_early, r_early)

    wait_xy_start_ab(2, 1)
    loop(0, 4, lambda r: wait_ab_start_c(1, r))
    loop(2, 4, lambda r: wait_xy_start_ab(2, r))
    loop(0, 4, lambda r: wait_c(1, r))

    def ffn_in(i):
        rows = pl.ds(pl.multiple_of(512 * (i // 12), 512), 512)
        columns = pl.ds(pl.multiple_of(256 * (i % 12), 256), 256)
        act[rows, columns] = gelu(dot(nlow[rows, :], win[:, columns]) + par[8:9, columns]).astype(BF)

    drop_copy.wait()
    for v in range(2):
        cls[KEEP2 + 8 * v : KEEP2 + 8 * v + 8, :] = dot(pick, drop[v].astype(F32).astype(BF)) * KEEP_SCALE
    preact_s = dot(cls[NRM : NRM + 16, :].astype(BF), win[...]) + par[8:9, 0:3072]
    pre_s[...] = preact_s
    acts[:, 0:3072] = gelu(preact_s).astype(BF)
    acts[:, 3072:3200] = jnp.zeros((16, 128), BF)

    def window(t):
        return acts.at[:, pl.ds(pl.multiple_of(128 * ((96 * t) // 128), 128), 256)]

    def send_act(i):
        t, device = other(i)
        pltpu.make_async_remote_copy(
            src_ref=window(t),
            dst_ref=actw_in.at[me],
            send_sem=s_act,
            recv_sem=r_act,
            device_id=device,
            device_id_type=MESH,
        ).start()

    loop(1, 32, send_act)
    actw_in[me] = window(me)[...]

    loop(0, 4, lambda r: wait_ab_start_c(2, r))
    loop(0, 4, lambda r: wait_c(2, r))
    keep2 = cls[KEEP2 : KEEP2 + 16, :]
    ffn_s = dot(acts[:, 0:3072], wout[...]) + bias(4)
    hat2, scale2 = standardize(cls[NRM : NRM + 16, :] + ffn_s * keep2)
    final_s = (hat2 * gain(1) + bias(5)) * used16
    length = lax.rsqrt(jnp.sum(final_s * final_s, axis=-1, keepdims=True) + UNIT_EPSILON)
    cls[HAT2 : HAT2 + 16, :] = hat2
    cls[FIN : FIN + 16, :] = final_s
    f3[2 * z + c, 2 * y + x] = (final_s * length).astype(BF)
    start_z(3)
    start_xy(3, 0)

    def ffn_out(i):
        v = i // 2
        rows = pl.ds(pl.multiple_of(256 * (i % 2), 256), 256)
        flat = pl.ds(pl.multiple_of(256 * i, 256), 256)
        out = dot(act[flat, :], wout[...]) + bias(4)
        hat, _ = standardize(normed[v, rows, :] + out * (drop[v, rows, :].astype(F32) * KEEP_SCALE))
        nlow[flat, :] = (hat * gain(1) + bias(5)).astype(BF)
        pltpu.make_async_copy(nlow.at[flat], hidden_hbm.at[v, rows], s_hid.at[i]).start()

    loop(0, 3, ffn_in)
    loop(1, 4, lambda r: wait_z_start_xy(3, r))
    loop(3, 6, ffn_in)
    loop(0, 4, lambda r: wait_xy_start_ab(3, r))
    loop(6, 9, ffn_in)
    loop(0, 4, lambda r: wait_ab_start_c(3, r))
    loop(9, 11, ffn_in)
    loop(0, 4, lambda r: wait_c(3, r))

    def sent(ph):
        def of(r):
            for copy in (cp_x, cp_y, cp_a, cp_b, cp_c):
                copy(ph, r).wait_send()
            if ph == 0:
                cp_cp(r).wait_send()

        def to_peers(r):
            of(r)
            cp_z(ph, r).wait_send()

        of(0)
        loop(1, 4, to_peers)

    def part_units(i):
        v = f3[i // 4, i % 4].astype(F32)
        rows = pl.ds(pl.multiple_of(8 * i, 8), 8)
        unit0[rows, :] = v[0:8]
        unit1[rows, :] = v[8:16]

    loop(0, 32, part_units)
    u0, u1 = unit0[...].astype(BF), unit1[...].astype(BF)
    mine = pl.ds(pl.multiple_of(8 * me, 8), 8)
    u0_mine, u1_mine = unit0[mine, :].astype(BF), unit1[mine, :].astype(BF)
    used_row = par[9:10, 0:256]
    eye = hot(256, 256, 0)
    used_col = jnp.sum(jnp.where(eye, used_row, 0.0), axis=1, keepdims=True)
    by_column = jnp.where(used_col > 0.0, dot(u1, u0, LAST) * (1.0 / SOFTMAX_TEMP), NEGATIVE)
    peak = jnp.max(by_column, axis=0, keepdims=True)
    total = peak + jnp.log(jnp.sum(jnp.exp(by_column - peak), axis=0, keepdims=True))
    positive = jnp.sum(jnp.where(eye, by_column, 0.0), axis=0, keepdims=True)
    loss_sum = jnp.sum((total - positive) * used_row, axis=1, keepdims=True)
    loss_ref[...] = loss_sum / jnp.sum(used_row, axis=1, keepdims=True)
    target = as_number(hot(8, 256, 8 * me))
    mine_1 = jnp.where(used_mine > 0.0, dot(u1_mine, u0, LAST) * (1.0 / SOFTMAX_TEMP), NEGATIVE)
    grad_1 = ((jnp.exp(mine_1 - total) - target) * used_row).astype(BF)
    mine_0 = jnp.where(used_row > 0.0, dot(u0_mine, u1, LAST) * (1.0 / SOFTMAX_TEMP), NEGATIVE)
    peak_0 = jnp.max(mine_0, axis=1, keepdims=True)
    total_0 = peak_0 + jnp.log(jnp.sum(jnp.exp(mine_0 - peak_0), axis=1, keepdims=True))
    grad_0 = ((jnp.exp(mine_0 - total_0) - target) * used_mine).astype(BF)
    grad_unit = jnp.concatenate([dot(grad_0, u1), dot(grad_1, u0)], axis=0) * (1.0 / SOFTMAX_TEMP)
    final_s = cls[FIN : FIN + 16, :]
    hat2 = cls[HAT2 : HAT2 + 16, :]
    pull = jnp.sum(grad_unit * final_s, axis=-1, keepdims=True)
    grad_final = (grad_unit - final_s * (pull * length * length)) * length * used16

    grad_mixed_two = norm_back(grad_final * gain(1), hat2, scale2)
    grad_ffn = (grad_mixed_two * cls[KEEP2 : KEEP2 + 16, :]).astype(BF)
    grad_pre = (dot(grad_ffn, wout[...], LAST) * gelu_slope(pre_s[...])).astype(BF)
    f4[2 * z + c, 2 * y + x, :, 0:768] = grad_ffn
    f4[2 * z + c, 2 * y + x, :, 768:3840] = grad_pre
    start_z(4)
    start_xy(4, 0)
    grad_normed = dot(grad_pre, win[...], LAST) + grad_mixed_two
    hat1 = cls[HAT1 : HAT1 + 16, :]
    grad_mixed = norm_back(grad_normed * gain(0), hat1, scale1)
    dropped = grad_mixed * cls[KEEP1 : KEEP1 + 16, :]
    grad_branch = (dropped[0:8] + dropped[8:16]).astype(BF)
    grad_ctx = dot(grad_branch, wqp[:, 2304:3072], LAST).astype(BF)
    loop(1, 4, lambda r: wait_z_start_xy(4, r))
    grad_big = spread(grad_ctx.astype(F32))
    query_big = spread(cls[QRY : QRY + 8, :])
    grad_probs = dot(grad_big, qkv[:, 1536:2304], LAST)
    prob = p_f[...]
    weighted = prob * grad_probs
    grad_scores = (weighted - prob * jnp.sum(weighted, axis=-1, keepdims=True)).astype(BF)
    pairs[0:96, :] = grad_scores
    grad_q = (gathered(dot(grad_scores, qkv[:, 768:1536])) * HD**-0.5).astype(BF)
    own5 = f5.at[2 * z + c, 2 * y + x]
    own5[:, 0:768] = jnp.concatenate([grad_branch.astype(F32), grad_ctx.astype(F32)], axis=0).astype(BF)
    own5[:, 768:1536] = jnp.concatenate([grad_q.astype(F32), cls[QRY : QRY + 8, :]], axis=0).astype(BF)
    start_z(5)
    start_xy(5, 0)
    wait_boxes(early, s_early)
    mixer[0:96, :] = dot(grad_scores, tokens[...])
    value_sum = jnp.sum(pairs[96:192, :].astype(F32), axis=-1, keepdims=True)
    own_sums = [
        jnp.sum(value_sum * grad_big.astype(F32), axis=0, keepdims=True),
        jnp.sum(grad_normed, axis=0, keepdims=True),
        jnp.sum(grad_final, axis=0, keepdims=True),
        jnp.sum(grad_normed * hat1, axis=0, keepdims=True),
        jnp.sum(grad_final * hat2, axis=0, keepdims=True),
    ]
    mixer[96:128, :] = jnp.zeros((32, 768), F32)
    for j, v in enumerate(own_sums):
        upper = v.astype(BF).astype(F32)
        mixer[96 + j : 97 + j, :] = upper
        mixer[104 + j : 105 + j, :] = v - upper
    send_mixer(late, late_in, s_late, r_late)
    loop(11, 14, ffn_in)
    loop(0, 4, lambda r: wait_xy_start_ab(4, r))
    loop(1, 4, lambda r: wait_z_start_xy(5, r))
    loop(14, 18, ffn_in)

    for ph in range(4):
        sent(ph)

    through[0:96, :] = dot(query_big, wqp[:, 768:1536], LAST).astype(BF)
    through[96:192, :] = dot(grad_big, wqp[:, 1536:2304], LAST).astype(BF)
    start_grad = grad_mixed[0:8] + grad_mixed[8:16] + dot(grad_q, wqp[:, 0:768], LAST)
    upper = start_grad.astype(BF).astype(F32)
    through[192:208, :] = jnp.concatenate([upper, start_grad - upper], axis=0).astype(BF)

    def token_grad(i):
        columns = pl.ds(pl.multiple_of(256 * i, 256), 256)
        gtok[:, columns] = dot(pairs[...], through[:, columns], FIRST)

    loop(0, 3, token_grad)
    token_copy = pltpu.make_async_copy(gtok, gtok_hbm, s_tok)
    token_copy.start()
    loop(0, 4, lambda r: wait_xy_start_ab(5, r))
    loop(18, 24, ffn_in)
    wait_boxes(early_in, r_early)

    column32 = lanes((16, 32), 1)
    first8 = lanes((16, 32), 0) < 8
    ones8 = as_number(first8 & (column32 == 24))

    def turn_early(i):
        for d in range(4):
            m = jnp.transpose(early_in[4 * i + d].astype(F32))
            rows16 = pl.ds(pl.multiple_of(64 * i + 16 * d, 16), 16)
            empty = jnp.zeros((8, 32), F32)
            mix_c[rows16, :] = (jnp.concatenate([m[96:104], empty], axis=0) + ones8).astype(BF)
            mix_t[rows16, :] = (jnp.concatenate([m[104:112], empty], axis=0) + ones8).astype(BF)
            mix_n[rows16, :] = (m[112:128] + as_number(column32 == 24)).astype(BF)

    loop(0, 8, turn_early)
    ffn_out(0)
    loop(0, 4, lambda r: wait_ab_start_c(4, r))
    ffn_out(1)
    loop(0, 4, lambda r: wait_ab_start_c(5, r))
    wait_boxes(actw_in, r_act)
    act_mine = dot(actw_in[...].reshape(512, 256), as_number(hot_back(256, 128, (96 * me) % 128)).astype(BF))
    act_mine = jnp.where(lanes((512, 128), 1) == 96, 1.0, act_mine).astype(BF)
    loop(0, 4, lambda r: wait_c(4, r))
    ffn_out(2)

    out_rows = dot(act_mine, f4[:, :, :, 0:768].reshape(512, 768), FIRST)
    g_out[...] = out_rows[0:96]
    sums[...] = jnp.zeros_like(sums)
    sums[4:5, 0:768] = out_rows[96:97]

    def in_rows(i):
        columns = pl.ds(pl.multiple_of(768 + 768 * i, 256), 768)
        to = pl.ds(pl.multiple_of(768 * i, 256), 768)
        rows = dot(mix_n[...], f4[:, :, :, columns].reshape(512, 768), FIRST)
        g_in[:, to] = rows[0:24]
        sums[8:16, to] = rows[24:32]

    loop(0, 4, in_rows)
    ffn_out(3)
    loop(0, 4, lambda r: wait_c(5, r))
    rows = dot(mix_c[...], f5[:, :, :, 0:768].reshape(512, 768), FIRST)
    g_proj[...] = rows[0:24]
    sums[2:3, 0:768] = rows[24:25]
    rows = dot(mix_t[...], f5[:, :, :, 768:1536].reshape(512, 768), FIRST)
    g_qkv[:, 0:768] = rows[0:24]
    sums[0:1, 0:768] = rows[24:25]

    def value_rows(g):
        total = dot(early_in[4 * g][:, 0:96], spread(f5[g, 0, :, 0:768].astype(F32)[8:16]))
        for i in range(1, 4):
            total += dot(early_in[4 * g + i][:, 0:96], spread(f5[g, i, :, 0:768].astype(F32)[8:16]))
        unit0[0:32, :] += total

    unit0[0:64, :] = jnp.zeros((64, 768), F32)
    loop(0, 8, value_rows)
    wait_boxes(late_in, r_late)
    rest[...] = jnp.zeros_like(rest)

    def key_rows(g):
        total = dot(late_in[4 * g][:, 0:96], spread(f5[g, 0, :, 768:1536].astype(F32)[8:16]))
        extra = late_in[4 * g].astype(F32)
        for i in range(1, 4):
            total += dot(late_in[4 * g + i][:, 0:96], spread(f5[g, i, :, 768:1536].astype(F32)[8:16]))
            extra += late_in[4 * g + i].astype(F32)
        unit0[32:64, :] += total
        rest[...] += extra

    loop(0, 8, key_rows)
    g_qkv[:, 768:1536] = unit0[32:56, :]
    g_qkv[:, 1536:2304] = unit0[0:24, :]
    turned = jnp.transpose(rest[...])
    near = sums[0:8, pl.ds(pl.multiple_of(128 * ((24 * me) // 128), 128), 256)]
    stage[0:8, 0:24] = dot_exact(near, as_number(hot_back(256, 24, (24 * me) % 128)))
    for j, row in enumerate((1, 3, 5, 6, 7)):
        stage[row : row + 1, 0:24] = (turned[96 + j : 97 + j, :] + turned[104 + j : 105 + j, :])[:, 0:24]
    g_bias[...] = stage[0:6, 0:24]
    g_gain[...] = stage[6:8, 0:24]
    near = sums[8:16, pl.ds(pl.multiple_of(128 * ((96 * me) // 128), 128), 256)]
    g_fbias[...] = dot_exact(near, as_number(hot_back(256, 96, (96 * me) % 128)))[0:1]

    sent(4)
    sent(5)
    wait_boxes(actw_in, s_act)
    wait_boxes(late, s_late)
    token_copy.wait()
    for i in range(4):
        rows = pl.ds(256 * (i % 2), 256)
        pltpu.make_async_copy(nlow.at[pl.ds(256 * i, 256)], hidden_hbm.at[i // 2, rows], s_hid.at[i]).wait()


def hot_back(rows, columns, shift):
    row = lax.broadcasted_iota(jnp.int32, (rows, columns), 0)
    column = lax.broadcasted_iota(jnp.int32, (rows, columns), 1)
    return row == column + shift


def dot_exact(a, b, dims=((1,), (0,))):
    return lax.dot_general(a, b, (dims, ((), ())), preferred_element_type=F32, precision=HIGH)


def hand_over(*refs):
    n = len(refs) // 3
    here, there, held = refs[:n], refs[n : 2 * n], refs[2 * n : 3 * n]
    s_in, s_out = refs[3 * n :]
    parts = []
    for i in range(n):
        rows = here[i].shape[-2]
        cuts = range(0, rows, rows // 4) if rows == 512 else [0]
        for at in cuts:
            size = rows // len(cuts)
            where = (slice(None),) * (len(here[i].shape) - 2) + (pl.ds(at, size),)
            parts.append([ref[i].at[where] for ref in (here, held, there)])
    loads = [pltpu.make_async_copy(p[0], p[1], s_in.at[k]) for k, p in enumerate(parts)]
    stores = [pltpu.make_async_copy(p[1], p[2], s_out.at[k]) for k, p in enumerate(parts)]
    for load in loads:
        load.start()
    for load, store in zip(loads, stores):
        load.wait()
        store.start()
    for store in stores:
        store.wait()


def encoder_step(
    tokens, qkv_weight, proj_weight, ffn_in_weight, ffn_out_weight, bias_rows, ffn_bias, norm_gains, buckets, padding, dropout
):
    def vm(*shape):
        return pltpu.VMEM(shape, BF)

    def vf(*shape):
        return pltpu.VMEM(shape, F32)

    def sems(*shape):
        return pltpu.SemaphoreType.DMA(shape)

    one = pltpu.SemaphoreType.DMA
    inside = pl.BlockSpec(memory_space=pltpu.VMEM)
    anywhere = pl.BlockSpec(memory_space=pl.ANY)
    engine = [sems(6, 4)] * 6 + [sems(4)]
    out = pl.pallas_call(
        encoder_kernel,
        name="encoder_step",
        out_shape=[
            jax.ShapeDtypeStruct((2, 512, 768), BF),
            jax.ShapeDtypeStruct((1, 1), F32),
            jax.ShapeDtypeStruct((512, 768), F32),
            jax.ShapeDtypeStruct((24, 2304), F32),
            jax.ShapeDtypeStruct((24, 768), F32),
            jax.ShapeDtypeStruct((24, 3072), F32),
            jax.ShapeDtypeStruct((96, 768), F32),
            jax.ShapeDtypeStruct((6, 24), F32),
            jax.ShapeDtypeStruct((1, 96), F32),
            jax.ShapeDtypeStruct((2, 24), F32),
        ],
        in_specs=[inside] * 10 + [anywhere],
        out_specs=[anywhere, inside, anywhere] + [inside] * 7,
        scratch_shapes=[
            vm(768, PW), vm(768, 3072), vm(3072, 768),
            vm(4, 2, 2, 16, WIDE + SW), vm(4, 2, 2, 16, WIDE), vm(4, 2, 2, 16, WIDE),
            vm(8, 4, 16, 768), vm(8, 4, 16, 3840), vm(8, 4, 16, 1536),
            vm(8, 4, 16, SW), vf(16, SW), vf(16, 3328),
            pltpu.VMEM((2, 512, 768), jnp.int32), vm(512, 2304), vf(512, 512), vm(512, 768),
            vf(2, 512, 768), vm(1024, 768), vm(1024, 3072),
            vf(120, 768), vf(8, 512), vm(8, 512), vf(16, 3072), vm(16, 3200), vf(96, 512),
            vm(208, 512), vm(208, 768), vf(128, 768), vf(768, 128), vf(256, 768), vf(256, 768), vf(16, 3328),
            vm(32, 32, 128), vm(32, 32, 128), vm(32, 32, 128), vm(32, 32, 128), vm(32, 16, 256),
            vf(512, 768), vm(768, 512), vm(512, 256),
            vm(512, 32), vm(512, 32), vm(512, 32), vf(32, 128),
        ] + engine + engine + [one] * 6 + [sems(2), sems(4), one],
        compiler_params=pltpu.CompilerParams(
            collective_id=0, has_side_effects=True, vmem_limit_bytes=63 * 2**20
        ),
    )(
        qkv_weight, proj_weight, ffn_in_weight, ffn_out_weight, bias_rows, norm_gains,
        ffn_bias[None], tokens, buckets, padding[None], dropout,
    )
    out = pl.pallas_call(
        hand_over,
        name="hand_over",
        out_shape=[jax.ShapeDtypeStruct(o.shape, o.dtype) for o in out],
        in_specs=[anywhere] * 10,
        out_specs=[anywhere] * 10,
        scratch_shapes=[pltpu.VMEM(o.shape, o.dtype) for o in out] + [sems(16), sems(16)],
        compiler_params=pltpu.CompilerParams(vmem_limit_bytes=60 * 2**20),
    )(*out)
    hidden, loss, gtok, g_qkv, g_proj, g_in, g_out, g_bias, g_fbias, g_gain = out
    return (hidden, loss[0, 0], gtok, g_qkv, g_proj, g_in, g_out, g_bias, g_fbias[0], g_gain)


def solution(mesh):
    in_specs = (
        P(AXES, None),
        P(AXES, None),
        P(AXES, None),
        P(AXES, None),
        P(AXES, None),
        P(None, AXES),
        P(AXES),
        P(None, AXES),
        P(AXES, None),
        P(AXES),
        P(None, None, AXES, None),
    )
    out_specs = (
        P(None, AXES, None),
        P(),
        P(AXES, None),
        P(AXES, None),
        P(AXES, None),
        P(AXES, None),
        P(AXES, None),
        P(None, AXES),
        P(AXES),
        P(None, AXES),
    )
    grid_fits = mesh.shape["dp"] == 8 and mesh.shape["fsdp"] == 4
    return jax.shard_map(
        encoder_step if grid_fits else with_collectives, mesh=mesh, in_specs=in_specs, out_specs=out_specs, check_vma=False
    )
```

```python
import functools

import jax
import jax.numpy as jnp
from jax import lax
from jax.experimental import pallas as pl
from jax.experimental.pallas import tpu as pltpu
from jax.sharding import PartitionSpec as P

H = 12
HD = 64

NEGATIVE = -1e30
NORM_EPSILON = 1e-12
UNIT_EPSILON = 1e-06
SOFTMAX_TEMP = 0.05
KEEP_SCALE = 1.0 / 0.9
FULL_PRECISION = lax.Precision.HIGHEST
AXES = ("dp", "fsdp")
BF = jnp.bfloat16
F32 = jnp.float32


def dot(a, b, dims=((1,), (0,))):
    return lax.dot_general(a, b, (dims, ((), ())), preferred_element_type=F32)


def layer_norm(inputs, gain_vec, shift_vec):
    centre = inputs - jnp.mean(inputs, axis=-1, keepdims=True)
    spread = jnp.mean(centre * centre, axis=-1, keepdims=True)
    return centre * lax.rsqrt(spread + NORM_EPSILON) * gain_vec + shift_vec


def normalize(inputs):
    return inputs * lax.rsqrt(jnp.sum(inputs * inputs, axis=-1, keepdims=True) + UNIT_EPSILON)


def exact_gelu(inputs):
    return jax.nn.gelu(inputs, approximate=False)


def sentence_layout(bucket_row, pad_row, rows_here):
    row_ids = jnp.arange(rows_here, dtype=jnp.int32)
    starts = jnp.cumsum(bucket_row) - bucket_row
    used = bucket_row > 0
    member = (row_ids[:, None] >= starts[None, :]) & used[None, :]
    sentence = jnp.sum(member.astype(jnp.int32), axis=1)
    allowed = (sentence[:, None] == sentence[None, :]) & (pad_row[None, :] > 0)
    select = ((row_ids[None, :] == starts[:, None]) & used[:, None]).astype(jnp.float32)
    slot_allowed = (
        (sentence[None, :] == jnp.arange(1, bucket_row.shape[0] + 1)[:, None])
        & used[:, None]
        & (pad_row[None, :] > 0)
    )
    return (allowed, select, slot_allowed)


def gather(x, axis=0):
    return lax.all_gather(x, AXES, axis=axis, tiled=True)


def all_to_all(x):
    return lax.all_to_all(x, AXES, split_axis=0, concat_axis=0, tiled=True)


def with_collectives(
    tokens,
    qkv_weight,
    proj_weight,
    ffn_in_weight,
    ffn_out_weight,
    bias_rows,
    ffn_bias,
    norm_gains,
    buckets,
    padding,
    dropout,
):
    rows_here, width = tokens.shape
    slots = buckets.shape[1]
    hidden = ffn_in_weight.shape[1]
    small = bias_rows.shape[1]
    devices = width // small
    hidden_small = hidden // devices
    me = lax.axis_index(AXES)
    score_scale = HD ** (-0.5)
    used_slot = (buckets[0] > 0).astype(BF)

    params = jnp.concatenate(
        [bias_rows.reshape(-1), norm_gains.reshape(-1), ffn_bias, used_slot]
    )
    params_all = gather(params[None])
    qp = gather(jnp.concatenate([qkv_weight, proj_weight], axis=1))
    qkv_full, proj_full = qp[:, : 3 * width], qp[:, 3 * width :]
    in_full = gather(ffn_in_weight)
    out_full = gather(ffn_out_weight)
    rows8 = params_all[:, : 8 * small].reshape(devices, 8, small).transpose(1, 0, 2)
    rows8 = rows8.reshape(8, width).astype(F32)
    bias_f, gain_f = rows8[:6], rows8[6:]
    ffn_bias_f = params_all[:, 8 * small : 8 * small + hidden_small].reshape(-1).astype(F32)
    used_all = params_all[:, 8 * small + hidden_small :].reshape(-1)

    allowed, select, slot_allowed = sentence_layout(buckets[0], padding, rows_here)
    select_low = select.astype(BF)
    zero_row = jnp.zeros((width,), F32)
    qkv = (dot(tokens, qkv_full) + jnp.concatenate([bias_f[0], zero_row, bias_f[1]])).astype(BF)
    head_view = qkv.reshape(rows_here, 3, H, HD)
    queries, key_rows, value_rows = (head_view[:, 0], head_view[:, 1], head_view[:, 2])

    scores = (
        jnp.einsum("qhd,khd->hqk", queries, key_rows, preferred_element_type=F32) * score_scale
    )
    scores = jnp.where(allowed[None], scores, NEGATIVE)
    exp_scores = jnp.exp(scores - jnp.max(scores, axis=-1, keepdims=True))
    probability = (exp_scores / jnp.sum(exp_scores, axis=-1, keepdims=True)).astype(BF)
    context = jnp.einsum("hqk,khd->qhd", probability, value_rows, preferred_element_type=F32)
    context = context.reshape(rows_here, width).astype(BF)
    branch = dot(context, proj_full) + bias_f[2]
    keep_mask = dropout.astype(F32)
    mixed_one = tokens.astype(F32)[None] + branch[None] * keep_mask[:, 0] * KEEP_SCALE
    normed = layer_norm(mixed_one, gain_f[0], bias_f[3])
    normed_low = normed.astype(BF)
    preact = dot(normed_low.reshape(-1, width), in_full) + ffn_bias_f
    activation = exact_gelu(preact).astype(BF)
    ffn_out = (dot(activation, out_full) + bias_f[4]).reshape(normed.shape)
    mixed_two = normed + ffn_out * keep_mask[:, 1] * KEEP_SCALE
    hidden_out = layer_norm(mixed_two, gain_f[1], bias_f[5]).astype(BF)

    tokens_s = dot(select_low, tokens)
    qkv_s = dot(select_low, qkv).astype(BF)
    queries_s = qkv_s[:, :width].reshape(slots, H, HD)
    scores_s = (
        jnp.einsum("shd,khd->hsk", queries_s, key_rows, preferred_element_type=F32) * score_scale
    )
    scores_s = jnp.where(slot_allowed[None], scores_s, NEGATIVE)
    peak_s = jnp.max(scores_s, axis=-1, keepdims=True)
    exp_s = jnp.exp(scores_s - peak_s) * slot_allowed[None].astype(F32)
    probability_f = exp_s / jnp.maximum(jnp.sum(exp_s, axis=-1, keepdims=True), 1e-30)
    probability_s = probability_f.astype(BF)
    context_s = dot(select_low, context).astype(BF)
    branch_s = dot(context_s, proj_full) + bias_f[2]
    keep_s = jnp.einsum(
        "sr,vbrd->vbsd", select_low, dropout.astype(BF), preferred_element_type=F32
    )
    mixed_s = tokens_s[None] + branch_s[None] * keep_s[:, 0] * KEEP_SCALE
    normed_s, first_back = jax.vjp(layer_norm, mixed_s, gain_f[0], bias_f[3])
    normed_s_low = normed_s.astype(BF).reshape(2 * slots, width)
    preact_s = dot(normed_s_low, in_full) + ffn_bias_f
    activation_sf, gelu_back = jax.vjp(exact_gelu, preact_s)
    activation_s = activation_sf.astype(BF)
    ffn_out_s = (dot(activation_s, out_full) + bias_f[4]).reshape(normed_s.shape)
    mixed_two_s = normed_s + ffn_out_s * keep_s[:, 1] * KEEP_SCALE
    final_s, second_back = jax.vjp(layer_norm, mixed_two_s, gain_f[1], bias_f[5])
    used_f = used_slot.astype(F32)
    final_s = final_s * used_f[None, :, None]
    unit_s, unit_back = jax.vjp(normalize, final_s)
    unit_low = unit_s.astype(BF)

    unit_all = gather(unit_low.reshape(1, 2, slots, width))
    unit_0 = unit_all[:, 0].reshape(-1, width)
    unit_1 = unit_all[:, 1].reshape(-1, width)
    logits = dot(unit_0, unit_1, ((1,), (1,))) / SOFTMAX_TEMP
    logits = jnp.where(used_all[None, :] > 0, logits, NEGATIVE)
    total = unit_0.shape[0]
    ids = jnp.arange(total, dtype=jnp.int32)
    diagonal = ids[:, None] == ids[None, :]
    logit_peak = jnp.max(logits, axis=-1, keepdims=True)
    logit_total = logit_peak[:, 0] + jnp.log(jnp.sum(jnp.exp(logits - logit_peak), axis=-1))
    positive = jnp.sum(jnp.where(diagonal, logits, 0.0), axis=1)
    used_all_f = used_all.astype(F32)
    loss_mean = jnp.sum((logit_total - positive) * used_all_f) / jnp.sum(used_all_f)
    soft = jnp.exp(logits - logit_total[:, None])
    logit_gradient = ((soft - diagonal.astype(F32)) * used_all_f[:, None]).astype(BF)
    mine_rows = lax.dynamic_slice_in_dim(logit_gradient, me * slots, slots, 0)
    mine_columns = lax.dynamic_slice_in_dim(logit_gradient, me * slots, slots, 1)
    grad_unit = jnp.stack(
        [dot(mine_rows, unit_1), dot(mine_columns, unit_0, ((0,), (0,)))]
    ) / SOFTMAX_TEMP
    (grad_final,) = unit_back(grad_unit)
    grad_final = grad_final * used_f[None, :, None]
    grad_mixed_two, grad_gain_two, grad_shift_two = second_back(grad_final)
    grad_ffn = (grad_mixed_two * keep_s[:, 1] * KEEP_SCALE).astype(BF).reshape(-1, width)
    grad_shift_out = jnp.sum(grad_ffn.astype(F32), axis=0)
    grad_act = dot(grad_ffn, out_full, ((1,), (1,)))
    (grad_preact_f,) = gelu_back(grad_act)
    grad_preact = grad_preact_f.astype(BF)
    grad_hidden_bias = jnp.sum(grad_preact.astype(F32), axis=0)
    grad_normed = dot(grad_preact, in_full, ((1,), (1,))).reshape(normed_s.shape) + grad_mixed_two
    grad_mixed, grad_gain_one, grad_shift_one = first_back(grad_normed)
    grad_branch = jnp.sum(grad_mixed * keep_s[:, 0] * KEEP_SCALE, axis=0).astype(BF)
    grad_shift_proj = jnp.sum(grad_branch.astype(F32), axis=0)
    grad_context = dot(grad_branch, proj_full, ((1,), (1,))).astype(BF)
    grad_context_h = grad_context.reshape(slots, H, HD)
    grad_probs = jnp.einsum(
        "shd,khd->hsk", grad_context_h, value_rows, preferred_element_type=F32
    )
    inner = jnp.sum(probability_f * grad_probs, axis=-1, keepdims=True)
    grad_scores = (probability_f * (grad_probs - inner)).astype(BF)
    grad_queries = (
        (jnp.einsum("hsk,khd->shd", grad_scores, key_rows, preferred_element_type=F32) * score_scale)
        .reshape(slots, width)
        .astype(BF)
    )
    pairs = jnp.concatenate([grad_scores, probability_s], axis=0).reshape(2 * H * slots, rows_here)
    token_sums = dot(pairs, tokens).astype(BF)
    key_factor = (queries_s.astype(F32) * score_scale).astype(BF)
    back_w = qkv_full.reshape(width, 3, H, HD)
    through = jnp.concatenate(
        [
            jnp.einsum("shd,whd->hsw", key_factor, back_w[:, 1], preferred_element_type=F32),
            jnp.einsum("shd,whd->hsw", grad_context_h, back_w[:, 2], preferred_element_type=F32),
        ],
        axis=0,
    ).reshape(2 * H * slots, width)
    start_grad = jnp.sum(grad_mixed, axis=0) + dot(
        grad_queries, qkv_full[:, :width], ((1,), (1,))
    )
    grad_tokens = dot(pairs, through.astype(BF), ((0,), (0,))) + lax.dot_general(
        select, start_grad, (((0,), (0,)), ((), ())), precision=FULL_PRECISION
    )
    value_sum = jnp.sum(probability_s.astype(F32), axis=-1).T
    grad_shift_value = jnp.sum(value_sum[:, :, None] * grad_context_h.astype(F32), axis=0).reshape(-1)
    grad_shift_query = jnp.sum(grad_queries.astype(F32), axis=0)

    wide = gather(jnp.concatenate([grad_ffn, grad_preact], axis=1))
    gffn_all, gpre_all = wide[:, :width], wide[:, width:]
    narrow = gather(
        jnp.concatenate([grad_branch, key_factor.reshape(slots, width), grad_context, grad_queries], axis=1)
    )
    gbranch_all = narrow[:, :width]
    key_all = narrow[:, width : 2 * width].reshape(-1, H, HD)
    gctx_all = narrow[:, 2 * width : 3 * width].reshape(-1, H, HD)
    gq_all = narrow[:, 3 * width :]

    def cut(x, n):
        return x.reshape(x.shape[0], devices, n).transpose(1, 0, 2).reshape(devices, -1)

    bias_sums = jnp.concatenate(
        [
            jnp.stack(
                [
                    grad_shift_query,
                    grad_shift_value,
                    grad_shift_proj,
                    grad_shift_one,
                    grad_shift_out,
                    grad_shift_two,
                    grad_gain_one,
                    grad_gain_two,
                ]
            )
            .reshape(8, devices, small)
            .transpose(1, 0, 2)
            .reshape(devices, -1),
            grad_hidden_bias.reshape(devices, -1),
        ],
        axis=1,
    )
    high = bias_sums.astype(BF)
    lower = (bias_sums - high.astype(F32)).astype(BF)
    pieces = [
        cut(activation_s, hidden_small),
        cut(normed_s_low, small),
        cut(context_s, small),
        cut(tokens_s.astype(BF), small),
        cut(token_sums, small),
        high,
        lower,
    ]
    sizes = [p.shape[1] for p in pieces]
    received = all_to_all(jnp.concatenate(pieces, axis=1))
    ends = []
    at = 0
    for n in sizes:
        ends.append(received[:, at : at + n])
        at += n
    act_r = ends[0].reshape(-1, hidden_small)
    normed_r = ends[1].reshape(-1, small)
    ctx_r = ends[2].reshape(-1, small)
    tok_r = ends[3].reshape(-1, small)
    sums_r = ends[4].reshape(devices, 2, H, slots, small)
    bias_r = jnp.sum(ends[5].astype(F32) + ends[6].astype(F32), axis=0)

    grad_out_weight = dot(act_r, gffn_all, ((0,), (0,)))
    grad_in_weight = dot(normed_r, gpre_all, ((0,), (0,)))
    grad_proj = dot(ctx_r, gbranch_all, ((0,), (0,)))
    grad_q = dot(tok_r, gq_all, ((0,), (0,)))
    keys_r = sums_r[:, 0].transpose(1, 0, 2, 3).reshape(H, -1, small)
    values_r = sums_r[:, 1].transpose(1, 0, 2, 3).reshape(H, -1, small)
    grad_k = jnp.einsum("hnw,nhd->whd", keys_r, key_all, preferred_element_type=F32)
    grad_v = jnp.einsum("hnw,nhd->whd", values_r, gctx_all, preferred_element_type=F32)
    grad_qkv_weight = jnp.concatenate(
        [grad_q, grad_k.reshape(small, width), grad_v.reshape(small, width)], axis=1
    )
    bias8 = bias_r[: 8 * small].reshape(8, small)
    return (
        hidden_out,
        loss_mean,
        grad_tokens,
        grad_qkv_weight,
        grad_proj,
        grad_in_weight,
        grad_out_weight,
        bias8[:6],
        bias_r[8 * small :],
        bias8[6:],
    )


MESH = pl.DeviceIdType.MESH
PW, QW, SW = 3072, 1536, 256
WIDE = PW + QW
HIGH = lax.Precision.HIGHEST
LAST = ((1,), (1,))
FIRST = ((0,), (0,))
WHOLE = (WIDE + SW, WIDE, WIDE, 768, 768, 1536, 768)


def place():
    dp = lax.axis_index("dp")
    fs = lax.axis_index("fsdp")
    return dp // 2, dp % 2, fs // 2, fs % 2


def peer_z(z, r):
    return (z + r) % 2 + 2 * ((z // 2 + r // 2) % 2)


def hot(rows, columns, shift):
    row = lax.broadcasted_iota(jnp.int32, (rows, columns), 0)
    column = lax.broadcasted_iota(jnp.int32, (rows, columns), 1)
    return row + shift == column


def as_number(flags):
    return jnp.where(flags, 1.0, 0.0)


def tail_of(x):
    t = 1.0 / (1.0 + (0.3275911 * 0.7071067811865476) * jnp.abs(x))
    bell = jnp.exp(x * x * -0.5)
    poly = 0.5 * 1.061405429
    for c in (-1.453152027, 1.421413741, -0.284496736, 0.254829592):
        poly = poly * t + 0.5 * c
    return poly * t * bell, bell


def gelu(x):
    tail, _ = tail_of(x)
    return jnp.maximum(x, 0.0) - jnp.abs(x) * tail


def gelu_slope(x):
    tail, bell = tail_of(x)
    return jnp.where(x >= 0.0, 1.0 - tail, tail) + x * bell * 0.3989422804014327


def mean(x):
    return jnp.sum(x, axis=-1, keepdims=True) * (1.0 / x.shape[-1])


def standardize(x):
    centre = x - mean(x)
    scale = lax.rsqrt(mean(centre * centre) + NORM_EPSILON)
    return centre * scale, scale


def norm_back(grad_hat, hat, scale):
    return scale * (grad_hat - mean(grad_hat) - hat * mean(grad_hat * hat))


def encoder_kernel(
    qkv_ref, proj_ref, in_ref, out_ref, bias_ref, gain_ref, fbias_ref, tokens, buckets_ref, pad_ref, drop_hbm,
    hidden_hbm, loss_ref, gtok_hbm, g_qkv, g_proj, g_in, g_out, g_bias, g_fbias, g_gain,
    wqp, win, wout, l0, l1, l2, f3, f4, f5, f6, pb, stage, par,
    drop, qkv, madd, ctx, normed, nlow, act,
    cls, sm8, sel, pre_s, acts, p_f, pairs, through, mixer, mixer_t, unit0, unit1, sums,
    early, early_in, late, late_in, actw_in, gtok, keys_t, values1, mix_n, mix_c, mix_t, rest, slope,
    sz, sx, sy, sa, sb, sc, scp, rz, rx, ry, ra, rb, rc, rcp, s_early, r_early, s_act, r_act, s_late, r_late, s_drop, s_hid, s_tok,
):
    z, c, y, x = place()
    me = 8 * z + 4 * c + 2 * y + x
    land = (l0, l1, l2)
    full = (f3, f4, f5, f6)
    weights = (wqp, win, wout)
    lanes = functools.partial(lax.broadcasted_iota, jnp.int32)

    def dev(z_, c_, y_, x_):
        return (2 * z_ + c_, 2 * y_ + x_)

    def other(i):
        t = (me + i) % 32
        return t, (t // 4, t % 4)

    def loop(lo, hi, body):
        def step(i, carry):
            body(i)
            return carry

        lax.fori_loop(lo, hi, step, 0)

    bar = pltpu.get_barrier_semaphore()

    def greet(i):
        _, device = other(i)
        pl.semaphore_signal(bar, inc=1, device_id=device, device_id_type=MESH)

    loop(1, 32, greet)
    drop_copy = pltpu.make_async_copy(drop_hbm.at[:, 0], drop, s_drop.at[0])
    drop_copy.start()

    def slot(ph, zz, yy, xx):
        if ph < 3:
            return land[ph].at[zz, yy, xx]
        return full[ph - 3].at[2 * zz + c, 2 * yy + xx]

    def rcopy(ref, s, r, device):
        return pltpu.make_async_remote_copy(
            src_ref=ref, dst_ref=ref, send_sem=s, recv_sem=r, device_id=device, device_id_type=MESH
        )

    def cp_z(ph, r):
        return rcopy(slot(ph, z, y, x), sz.at[ph, r], rz.at[ph, r], dev(peer_z(z, r), c, y, x))

    def cp_x(ph, r):
        return rcopy(slot(ph, peer_z(z, r), y, x), sx.at[ph, r], rx.at[ph, r], dev(z, c, y, 1 - x))

    def cp_y(ph, r):
        return rcopy(slot(ph, peer_z(z, r), y, x), sy.at[ph, r], ry.at[ph, r], dev(z, c, 1 - y, x))

    def half(ph):
        return WHOLE[ph] // 256 * 128

    def cp_a(ph, r):
        ref = slot(ph, peer_z(z, r), y, 1 - x).at[:, 0 : half(ph)]
        return rcopy(ref, sa.at[ph, r], ra.at[ph, r], dev(z, c, 1 - y, x))

    def cp_b(ph, r):
        ref = slot(ph, peer_z(z, r), 1 - y, x).at[:, half(ph) : WHOLE[ph]]
        return rcopy(ref, sb.at[ph, r], rb.at[ph, r], dev(z, c, y, 1 - x))

    def cp_c(ph, r):
        group = 2 * peer_z(z, r) + c
        if ph < 3:
            n = 384 if ph == 2 else 96
            ref = weights[ph].at[pl.ds(pl.multiple_of(n * group, n), n)]
        else:
            ref = full[ph - 3].at[group]
        return rcopy(ref, sc.at[ph, r], rc.at[ph, r], dev(z, 1 - c, y, x))

    def cp_cp(r):
        return rcopy(pb.at[2 * peer_z(z, r) + c], scp.at[r], rcp.at[r], dev(z, 1 - c, y, x))

    def start_z(ph):
        loop(1, 4, lambda r: cp_z(ph, r).start())

    def start_xy(ph, r):
        cp_x(ph, r).start()
        cp_y(ph, r).start()

    def wait_z_start_xy(ph, r):
        cp_z(ph, r).wait_recv()
        start_xy(ph, r)

    def wait_xy_start_ab(ph, r):
        cp_x(ph, r).wait_recv()
        cp_a(ph, r).start()
        cp_y(ph, r).wait_recv()
        cp_b(ph, r).start()

    def merge(ph, r):
        zz = peer_z(z, r)
        group = 2 * zz + c
        if ph == 2:
            for yy in range(2):
                for xx in range(2):
                    base = 384 * group + 96 * (2 * yy + xx)
                    for j in range(6):
                        wout[pl.ds(pl.multiple_of(base + 16 * j, 16), 16), :] = l2[
                            zz, yy, xx, :, 768 * j : 768 * (j + 1)
                        ]
            return
        w = weights[ph]
        l = land[ph]
        spans = [(0, 2304, PW), (2304, 768, PW + 1152)] if ph == 0 else [(0, 3072, PW)]
        for yy in range(2):
            base = 96 * group + 48 * yy
            w[pl.ds(pl.multiple_of(base, 16), 16), :] = l[zz, yy, 0, :, 0:PW]
            w[pl.ds(pl.multiple_of(base + 32, 16), 16), :] = l[zz, yy, 1, :, 0:PW]
            middle = pl.ds(pl.multiple_of(base + 16, 16), 16)
            for at, n, qat in spans:
                qe = l[zz, yy, 0, :, qat : qat + n // 2].astype(F32)
                qo = l[zz, yy, 1, :, qat : qat + n // 2].astype(F32)
                w[middle, at : at + n // 2] = jnp.concatenate([qe[0:8], qo[0:8]], axis=0).astype(BF)
                w[middle, at + n // 2 : at + n] = jnp.concatenate([qe[8:16], qo[8:16]], axis=0).astype(BF)
        if ph == 0:
            for yy in range(2):
                for xx in range(2):
                    pb[group, 2 * yy + xx] = l0[zz, yy, xx, :, WIDE:]

    def wait_ab_start_c(ph, r):
        cp_a(ph, r).wait_recv()
        cp_b(ph, r).wait_recv()
        if ph < 3:
            merge(ph, r)
        cp_c(ph, r).start()
        if ph == 0:
            cp_cp(r).start()

    def wait_c(ph, r):
        cp_c(ph, r).wait_recv()
        if ph == 0:
            cp_cp(r).wait_recv()

    def pack(ph, parts):
        at, qat = 0, PW
        for ref in parts:
            v = ref[...].astype(F32)
            n = v.shape[1]
            p_rows = jnp.where(x == 0, v[0:16], v[8:24])
            q_rows = jnp.where(x == 0, v[16:24], v[0:8])
            land[ph][z, y, x, :, at : at + n] = p_rows.astype(BF)
            land[ph][z, y, x, :, qat : qat + n // 2] = jnp.concatenate(
                [q_rows[:, : n // 2], q_rows[:, n // 2 :]], axis=0
            ).astype(BF)
            at += n
            qat += n // 2

    pack(0, (qkv_ref, proj_ref))

    def put(v, shift):
        return dot(v.astype(BF), as_number(hot(v.shape[1], SW, shift)).astype(BF))

    bk = buckets_ref[...].astype(F32)
    stage[...] = jnp.zeros_like(stage)
    stage[0:6, :] = put(bias_ref[...], (24 * me) % 128)
    stage[6:8, :] = put(gain_ref[...], (24 * me) % 128)
    stage[8:9, :] = put(fbias_ref[...], (96 * me) % 128)
    stage[9:10, :] = put(as_number(bk > 0.0), (8 * me) % 128)
    l0[z, y, x, :, WIDE:] = stage[...].astype(BF)
    pl.semaphore_wait(bar, 31)

    start_z(0)
    start_xy(0, 0)
    pack(1, (in_ref,))
    for j in range(6):
        l2[z, y, x, :, 768 * j : 768 * (j + 1)] = out_ref[16 * j : 16 * (j + 1), :]

    row8, lane8 = lanes((8, 8), 0), lanes((8, 8), 1)
    bk_col = jnp.sum(jnp.where(row8 == lane8, bk, 0.0), axis=1, keepdims=True)
    starts_col = jnp.sum(jnp.where(lane8 < row8, bk, 0.0), axis=1, keepdims=True)
    starts_row = jnp.sum(jnp.where(row8 < lane8, bk_col, 0.0), axis=0, keepdims=True)
    used_mine = as_number(bk_col > 0.0)
    used16 = jnp.concatenate([used_mine, used_mine], axis=0)
    row_ids = lanes((512, 8), 0).astype(F32)
    column_ids = lanes((8, 512), 1).astype(F32)
    sent_row = jnp.sum(as_number((row_ids >= starts_row) & (bk > 0.0)), axis=1, keepdims=True)
    sent_col = jnp.sum(as_number((column_ids >= starts_col) & (bk_col > 0.0)), axis=0, keepdims=True)
    key_of = jnp.where(pad_ref[...] > 0, sent_col, 0.0)
    madd[...] = jnp.where(sent_row == key_of, 0.0, NEGATIVE)
    sm8[...] = as_number(key_of == (lanes((8, 512), 0) + 1).astype(F32))
    sel[...] = as_number((column_ids == starts_col) & (bk_col > 0.0)).astype(BF)

    wait_z_start_xy(0, 1)
    wait_xy_start_ab(0, 0)
    wait_z_start_xy(0, 2)
    wait_z_start_xy(0, 3)
    start_z(1)
    start_xy(1, 0)
    loop(1, 4, lambda r: wait_xy_start_ab(0, r))
    loop(1, 4, lambda r: wait_z_start_xy(1, r))
    start_z(2)
    start_xy(2, 0)
    loop(0, 4, lambda r: wait_ab_start_c(0, r))
    drop_copy.wait()
    loop(0, 4, lambda r: wait_c(0, r))
    par[...] = jnp.zeros_like(par)
    for d in range(32):
        w = pb[d // 4, d % 4].astype(F32)
        t, t2, t3 = 24 * d // 128, 96 * d // 128, 8 * d // 128
        par[0:8, 128 * t : 128 * t + 256] += w[0:8]
        par[8:9, 128 * t2 : 128 * t2 + 256] += w[8:9]
        par[9:10, 128 * t3 : 128 * t3 + 256] += w[9:10]

    def bias(i):
        return par[i : i + 1, 0:768]

    def gain(i):
        return par[6 + i : 7 + i, 0:768]

    def qkv_part(i):
        columns = pl.ds(pl.multiple_of(256 * i, 256), 256)
        inside = pl.ds(pl.multiple_of(256 * (i % 3), 256), 256)
        both = par[0:8, inside]
        part = jnp.where(i < 3, both[0:1], jnp.where(i < 6, 0.0, both[1:2]))
        qkv[:, columns] = (dot(tokens[...], wqp[:, columns]) + part).astype(BF)

    loop(0, 9, qkv_part)
    loop(0, 4, lambda r: wait_xy_start_ab(1, r))
    loop(1, 4, lambda r: wait_z_start_xy(2, r))

    left = lanes((1, 128), 1) < 64
    left_scale = jnp.where(left, HD**-0.5, 0.0)
    right_scale = jnp.where(left, 0.0, HD**-0.5)

    def turn_keys(i):
        columns = pl.ds(pl.multiple_of(768 + 128 * i, 128), 128)
        keys_t[pl.ds(pl.multiple_of(128 * i, 128), 128), :] = jnp.transpose(qkv[:, columns].astype(F32)).astype(BF)

    loop(0, 6, turn_keys)
    values1[:, 128:256] = jnp.ones((512, 128), BF)

    def attend(pair):
        def columns(part):
            return pl.ds(pl.multiple_of(768 * part + 128 * pair, 128), 128)

        values1[:, 0:128] = qkv[:, columns(2)]

        q = qkv[:, columns(0)].astype(F32)
        results = []
        for scale in (left_scale, right_scale):
            s = dot((q * scale).astype(BF), keys_t[columns(0), :]) + madd[...]
            e = jnp.exp(s - jnp.max(s, axis=-1, keepdims=True)).astype(BF)
            both = dot(e, values1[...])
            results.append(both[:, 0:128] * (1.0 / both[:, 128:256]))
        ctx[:, columns(0)] = jnp.where(left, results[0], results[1]).astype(BF)

    loop(0, 6, attend)

    def first_norm(i):
        rows = pl.ds(pl.multiple_of(128 * i, 128), 128)
        branch = (dot(ctx[rows, :], wqp[:, 2304:3072]) + bias(2)) * KEEP_SCALE
        token_rows = tokens[rows, :].astype(F32)
        for v in range(2):
            hat, _ = standardize(token_rows + branch * drop[v, rows, :].astype(F32))
            n = hat * gain(0) + bias(3)
            normed[v, rows, :] = n
            nlow[pl.ds(pl.multiple_of(512 * v + 128 * i, 128), 128), :] = n.astype(BF)

    loop(0, 4, first_norm)
    loop(0, 4, lambda r: wait_ab_start_c(1, r))
    wait_xy_start_ab(2, 0)

    TOK, QRY, CTX, KEEP1, KEEP2, HAT1, NRM, HAT2, FIN = 0, 8, 16, 24, 40, 56, 72, 88, 104
    pick = sel[...]
    cls[TOK : TOK + 8, :] = dot(pick, tokens[...])
    cls[QRY : QRY + 8, :] = dot(pick, qkv[:, 0:768]) * HD**-0.5
    cls[CTX : CTX + 8, :] = dot(pick, ctx[...])
    for v in range(2):
        cls[KEEP1 + 8 * v : KEEP1 + 8 * v + 8, :] = dot(pick, drop[v].astype(F32).astype(BF)) * KEEP_SCALE
    drop_copy = pltpu.make_async_copy(drop_hbm.at[:, 1], drop, s_drop.at[1])
    drop_copy.start()

    def twice(v):
        return jnp.concatenate([v, v], axis=0)

    head = lax.broadcasted_iota(jnp.int32, (12, 8, 768), 0) * 64
    lane = lax.broadcasted_iota(jnp.int32, (12, 8, 768), 2)
    own_head = (lane >= head) & (lane < head + 64)

    def spread(rows8):
        return jnp.where(own_head, rows8[None], 0.0).reshape(96, 768).astype(BF)

    def gathered(rows96):
        return jnp.sum(jnp.where(own_head, rows96.reshape(12, 8, 768), 0.0), axis=0)

    branch_s = dot(cls[CTX : CTX + 8, :].astype(BF), wqp[:, 2304:3072]) + bias(2)
    hat1, scale1 = standardize(twice(cls[TOK : TOK + 8, :]) + twice(branch_s) * cls[KEEP1 : KEEP1 + 16, :])
    normed_s = hat1 * gain(0) + bias(3)
    cls[HAT1 : HAT1 + 16, :] = hat1
    cls[NRM : NRM + 16, :] = normed_s
    f6[2 * z + c, 2 * y + x] = normed_s.astype(BF)
    start_z(6)
    query_big = spread(cls[QRY : QRY + 8, :])
    seen = jnp.broadcast_to(sm8[...][None], (12, 8, 512)).reshape(96, 512)
    s = jnp.where(seen > 0.0, dot(query_big, qkv[:, 768:1536], LAST), NEGATIVE)
    e = jnp.exp(s - jnp.max(s, axis=-1, keepdims=True)) * seen
    prob = e * (1.0 / jnp.maximum(jnp.sum(e, axis=-1, keepdims=True), 1e-30))
    p_f[...] = prob
    pairs[96:192, :] = prob.astype(BF)
    pairs[192:208, :] = twice(pick.astype(F32)).astype(BF)
    mixer[0:96, :] = dot(prob.astype(BF), tokens[...])
    mixer[96:104, :] = cls[CTX : CTX + 8, :]
    mixer[104:112, :] = cls[TOK : TOK + 8, :]
    mixer[112:128, :] = normed_s

    def send_mixer(box, box_in, s_sem, r_sem):
        mixer_t[...] = jnp.transpose(mixer[...])

        def cut(t):
            v = mixer_t[pl.ds(pl.multiple_of(24 * t, 8), 24), :]
            box[t] = jnp.concatenate([v, jnp.zeros((8, 128), F32)], axis=0).astype(BF)

        loop(0, 32, cut)
        box_in[me] = box[me]

        def send(i):
            t, device = other(i)
            pltpu.make_async_remote_copy(
                src_ref=box.at[t],
                dst_ref=box_in.at[me],
                send_sem=s_sem,
                recv_sem=r_sem,
                device_id=device,
                device_id_type=MESH,
            ).start()

        loop(1, 32, send)

    def wait_boxes(ref, sem):
        part = ref.at[pl.ds(0, 31)]
        pltpu.make_async_copy(part, part, sem).wait()

    send_mixer(early, early_in, s_early, r_early)

    loop(0, 4, lambda r: wait_c(1, r))
    wait_xy_start_ab(2, 1)

    def ffn_in(i):
        columns = pl.ds(pl.multiple_of(256 * i, 256), 256)
        act[:, columns] = gelu(dot(nlow[...], win[:, columns]) + par[8:9, columns]).astype(BF)

    loop(0, 3, ffn_in)
    wait_xy_start_ab(2, 2)
    loop(3, 6, ffn_in)
    drop_copy.wait()
    for v in range(2):
        cls[KEEP2 + 8 * v : KEEP2 + 8 * v + 8, :] = dot(pick, drop[v].astype(F32).astype(BF)) * KEEP_SCALE
    preact_s = dot(cls[NRM : NRM + 16, :].astype(BF), win[...]) + par[8:9, 0:3072]
    pre_s[...] = preact_s
    acts[:, 0:3072] = gelu(preact_s).astype(BF)
    acts[:, 3072:3200] = jnp.zeros((16, 128), BF)

    def window(t):
        return acts.at[:, pl.ds(pl.multiple_of(128 * ((96 * t) // 128), 128), 256)]

    def send_act(i):
        t, device = other(i)
        pltpu.make_async_remote_copy(
            src_ref=window(t),
            dst_ref=actw_in.at[me],
            send_sem=s_act,
            recv_sem=r_act,
            device_id=device,
            device_id_type=MESH,
        ).start()

    loop(1, 32, send_act)
    actw_in[me] = window(me)[...]

    wait_xy_start_ab(2, 3)
    start_xy(6, 0)
    loop(1, 4, lambda r: wait_z_start_xy(6, r))
    loop(6, 8, ffn_in)

    loop(0, 4, lambda r: wait_ab_start_c(2, r))
    loop(0, 4, lambda r: wait_c(2, r))
    keep2 = cls[KEEP2 : KEEP2 + 16, :]
    ffn_s = dot(acts[:, 0:3072], wout[...]) + bias(4)
    hat2, scale2 = standardize(cls[NRM : NRM + 16, :] + ffn_s * keep2)
    final_s = (hat2 * gain(1) + bias(5)) * used16
    length = lax.rsqrt(jnp.sum(final_s * final_s, axis=-1, keepdims=True) + UNIT_EPSILON)
    cls[HAT2 : HAT2 + 16, :] = hat2
    cls[FIN : FIN + 16, :] = final_s
    f3[2 * z + c, 2 * y + x] = (final_s * length).astype(BF)
    start_z(3)
    start_xy(3, 0)

    def ffn_out(i):
        v = i // 2
        rows = pl.ds(pl.multiple_of(256 * (i % 2), 256), 256)
        flat = pl.ds(pl.multiple_of(256 * i, 256), 256)
        out = dot(act[flat, :], wout[...]) + bias(4)
        hat, _ = standardize(normed[v, rows, :] + out * (drop[v, rows, :].astype(F32) * KEEP_SCALE))
        nlow[flat, :] = (hat * gain(1) + bias(5)).astype(BF)
        pltpu.make_async_copy(nlow.at[flat], hidden_hbm.at[v, rows], s_hid.at[i]).start()

    loop(8, 10, ffn_in)
    loop(1, 4, lambda r: wait_z_start_xy(3, r))
    loop(0, 4, lambda r: wait_xy_start_ab(6, r))
    loop(10, 12, ffn_in)
    loop(0, 4, lambda r: wait_xy_start_ab(3, r))
    loop(0, 4, lambda r: wait_ab_start_c(6, r))
    ffn_out(0)
    loop(0, 4, lambda r: wait_ab_start_c(3, r))
    loop(0, 4, lambda r: wait_c(6, r))

    def slopes(i):
        columns = pl.ds(pl.multiple_of(512 * i, 512), 512)
        preact = dot(f6[...].reshape(512, 768), win[:, columns]) + par[8:9, columns]
        slope[:, columns] = gelu_slope(preact).astype(BF)

    slopes(0)
    loop(0, 4, lambda r: wait_c(3, r))

    def sent(ph):
        def of(r):
            for copy in (cp_x, cp_y, cp_a, cp_b, cp_c):
                copy(ph, r).wait_send()
            if ph == 0:
                cp_cp(r).wait_send()

        def to_peers(r):
            of(r)
            cp_z(ph, r).wait_send()

        of(0)
        loop(1, 4, to_peers)

    def part_units(i):
        v = f3[i // 4, i % 4].astype(F32)
        rows = pl.ds(pl.multiple_of(8 * i, 8), 8)
        unit0[rows, :] = v[0:8]
        unit1[rows, :] = v[8:16]

    loop(0, 32, part_units)
    u0, u1 = unit0[...].astype(BF), unit1[...].astype(BF)
    mine = pl.ds(pl.multiple_of(8 * me, 8), 8)
    u0_mine, u1_mine = unit0[mine, :].astype(BF), unit1[mine, :].astype(BF)
    used_row = par[9:10, 0:256]
    eye = hot(256, 256, 0)
    used_col = jnp.sum(jnp.where(eye, used_row, 0.0), axis=1, keepdims=True)
    by_column = jnp.where(used_col > 0.0, dot(u1, u0, LAST) * (1.0 / SOFTMAX_TEMP), NEGATIVE)
    peak = jnp.max(by_column, axis=0, keepdims=True)
    total = peak + jnp.log(jnp.sum(jnp.exp(by_column - peak), axis=0, keepdims=True))
    positive = jnp.sum(jnp.where(eye, by_column, 0.0), axis=0, keepdims=True)
    loss_sum = jnp.sum((total - positive) * used_row, axis=1, keepdims=True)
    loss_ref[...] = loss_sum / jnp.sum(used_row, axis=1, keepdims=True)
    target = as_number(hot(8, 256, 8 * me))
    mine_1 = jnp.where(used_mine > 0.0, dot(u1_mine, u0, LAST) * (1.0 / SOFTMAX_TEMP), NEGATIVE)
    grad_1 = ((jnp.exp(mine_1 - total) - target) * used_row).astype(BF)
    mine_0 = jnp.where(used_row > 0.0, dot(u0_mine, u1, LAST) * (1.0 / SOFTMAX_TEMP), NEGATIVE)
    peak_0 = jnp.max(mine_0, axis=1, keepdims=True)
    total_0 = peak_0 + jnp.log(jnp.sum(jnp.exp(mine_0 - peak_0), axis=1, keepdims=True))
    grad_0 = ((jnp.exp(mine_0 - total_0) - target) * used_mine).astype(BF)
    grad_unit = jnp.concatenate([dot(grad_0, u1), dot(grad_1, u0)], axis=0) * (1.0 / SOFTMAX_TEMP)
    final_s = cls[FIN : FIN + 16, :]
    hat2 = cls[HAT2 : HAT2 + 16, :]
    pull = jnp.sum(grad_unit * final_s, axis=-1, keepdims=True)
    grad_final = (grad_unit - final_s * (pull * length * length)) * length * used16

    grad_mixed_two = norm_back(grad_final * gain(1), hat2, scale2)
    grad_ffn = (grad_mixed_two * cls[KEEP2 : KEEP2 + 16, :]).astype(BF)
    f4[2 * z + c, 2 * y + x] = grad_ffn
    start_z(4)
    start_xy(4, 0)
    grad_pre = (dot(grad_ffn, wout[...], LAST) * gelu_slope(pre_s[...])).astype(BF)
    grad_normed = dot(grad_pre, win[...], LAST) + grad_mixed_two
    hat1 = cls[HAT1 : HAT1 + 16, :]
    grad_mixed = norm_back(grad_normed * gain(0), hat1, scale1)
    dropped = grad_mixed * cls[KEEP1 : KEEP1 + 16, :]
    grad_branch = (dropped[0:8] + dropped[8:16]).astype(BF)
    grad_ctx = dot(grad_branch, wqp[:, 2304:3072], LAST).astype(BF)
    loop(1, 4, lambda r: wait_z_start_xy(4, r))
    grad_big = spread(grad_ctx.astype(F32))
    query_big = spread(cls[QRY : QRY + 8, :])
    grad_probs = dot(grad_big, qkv[:, 1536:2304], LAST)
    prob = p_f[...]
    weighted = prob * grad_probs
    grad_scores = (weighted - prob * jnp.sum(weighted, axis=-1, keepdims=True)).astype(BF)
    pairs[0:96, :] = grad_scores
    grad_q = (gathered(dot(grad_scores, qkv[:, 768:1536])) * HD**-0.5).astype(BF)
    own5 = f5.at[2 * z + c, 2 * y + x]
    own5[:, 0:768] = jnp.concatenate([grad_branch.astype(F32), grad_ctx.astype(F32)], axis=0).astype(BF)
    own5[:, 768:1536] = jnp.concatenate([grad_q.astype(F32), cls[QRY : QRY + 8, :]], axis=0).astype(BF)
    start_z(5)
    start_xy(5, 0)
    wait_boxes(early, s_early)
    mixer[0:96, :] = dot(grad_scores, tokens[...])
    value_sum = jnp.sum(pairs[96:192, :].astype(F32), axis=-1, keepdims=True)
    own_sums = [
        jnp.sum(value_sum * grad_big.astype(F32), axis=0, keepdims=True),
        jnp.sum(grad_normed, axis=0, keepdims=True),
        jnp.sum(grad_final, axis=0, keepdims=True),
        jnp.sum(grad_normed * hat1, axis=0, keepdims=True),
        jnp.sum(grad_final * hat2, axis=0, keepdims=True),
    ]
    mixer[96:128, :] = jnp.zeros((32, 768), F32)
    for j, v in enumerate(own_sums):
        upper = v.astype(BF).astype(F32)
        mixer[96 + j : 97 + j, :] = upper
        mixer[104 + j : 105 + j, :] = v - upper
    send_mixer(late, late_in, s_late, r_late)
    loop(0, 4, lambda r: wait_xy_start_ab(4, r))
    loop(1, 4, lambda r: wait_z_start_xy(5, r))
    loop(1, 3, slopes)
    loop(0, 4, lambda r: wait_ab_start_c(4, r))
    loop(3, 4, slopes)
    loop(0, 4, lambda r: wait_xy_start_ab(5, r))
    loop(4, 6, slopes)
    for ph in (0, 1, 2, 3, 6):
        sent(ph)

    through[0:96, :] = dot(query_big, wqp[:, 768:1536], LAST).astype(BF)
    through[96:192, :] = dot(grad_big, wqp[:, 1536:2304], LAST).astype(BF)
    start_grad = grad_mixed[0:8] + grad_mixed[8:16] + dot(grad_q, wqp[:, 0:768], LAST)
    upper = start_grad.astype(BF).astype(F32)
    through[192:208, :] = jnp.concatenate([upper, start_grad - upper], axis=0).astype(BF)

    def token_grad(i):
        columns = pl.ds(pl.multiple_of(256 * i, 256), 256)
        gtok[:, columns] = dot(pairs[...], through[:, columns], FIRST)

    loop(0, 3, token_grad)
    token_copy = pltpu.make_async_copy(gtok, gtok_hbm, s_tok)
    token_copy.start()
    wait_boxes(early_in, r_early)

    column32 = lanes((16, 32), 1)
    first8 = lanes((16, 32), 0) < 8
    ones8 = as_number(first8 & (column32 == 24))

    def turn_early(i):
        for d in range(4):
            m = jnp.transpose(early_in[4 * i + d].astype(F32))
            rows16 = pl.ds(pl.multiple_of(64 * i + 16 * d, 16), 16)
            empty = jnp.zeros((8, 32), F32)
            mix_c[rows16, :] = (jnp.concatenate([m[96:104], empty], axis=0) + ones8).astype(BF)
            mix_t[rows16, :] = (jnp.concatenate([m[104:112], empty], axis=0) + ones8).astype(BF)
            mix_n[rows16, :] = (m[112:128] + as_number(column32 == 24)).astype(BF)

    loop(0, 8, turn_early)
    loop(0, 4, lambda r: wait_ab_start_c(5, r))
    wait_boxes(actw_in, r_act)
    act_mine = dot(actw_in[...].reshape(512, 256), as_number(hot_back(256, 128, (96 * me) % 128)).astype(BF))
    act_mine = jnp.where(lanes((512, 128), 1) == 96, 1.0, act_mine).astype(BF)
    loop(0, 4, lambda r: wait_c(4, r))
    ffn_out(1)

    out_rows = dot(act_mine, f4[...].reshape(512, 768), FIRST)
    g_out[...] = out_rows[0:96]
    sums[...] = jnp.zeros_like(sums)
    sums[4:5, 0:768] = out_rows[96:97]

    def in_rows(i):
        to = pl.ds(pl.multiple_of(768 * i, 256), 768)
        grad_act = dot(f4[...].reshape(512, 768), wout[to, :], LAST)
        rows = dot(mix_n[...], (grad_act * slope[:, to].astype(F32)).astype(BF), FIRST)
        g_in[:, to] = rows[0:24]
        sums[8:16, to] = rows[24:32]

    loop(0, 4, in_rows)
    ffn_out(2)
    ffn_out(3)
    loop(0, 4, lambda r: wait_c(5, r))
    rows = dot(mix_c[...], f5[:, :, :, 0:768].reshape(512, 768), FIRST)
    g_proj[...] = rows[0:24]
    sums[2:3, 0:768] = rows[24:25]
    rows = dot(mix_t[...], f5[:, :, :, 768:1536].reshape(512, 768), FIRST)
    g_qkv[:, 0:768] = rows[0:24]
    sums[0:1, 0:768] = rows[24:25]

    def value_rows(g):
        total = dot(early_in[4 * g][:, 0:96], spread(f5[g, 0, :, 0:768].astype(F32)[8:16]))
        for i in range(1, 4):
            total += dot(early_in[4 * g + i][:, 0:96], spread(f5[g, i, :, 0:768].astype(F32)[8:16]))
        unit0[0:32, :] += total

    unit0[0:64, :] = jnp.zeros((64, 768), F32)
    loop(0, 8, value_rows)
    wait_boxes(late_in, r_late)
    rest[...] = jnp.zeros_like(rest)

    def key_rows(g):
        total = dot(late_in[4 * g][:, 0:96], spread(f5[g, 0, :, 768:1536].astype(F32)[8:16]))
        extra = late_in[4 * g].astype(F32)
        for i in range(1, 4):
            total += dot(late_in[4 * g + i][:, 0:96], spread(f5[g, i, :, 768:1536].astype(F32)[8:16]))
            extra += late_in[4 * g + i].astype(F32)
        unit0[32:64, :] += total
        rest[...] += extra

    loop(0, 8, key_rows)
    g_qkv[:, 768:1536] = unit0[32:56, :]
    g_qkv[:, 1536:2304] = unit0[0:24, :]
    turned = jnp.transpose(rest[...])
    near = sums[0:8, pl.ds(pl.multiple_of(128 * ((24 * me) // 128), 128), 256)]
    stage[0:8, 0:24] = dot_exact(near, as_number(hot_back(256, 24, (24 * me) % 128)))
    for j, row in enumerate((1, 3, 5, 6, 7)):
        stage[row : row + 1, 0:24] = (turned[96 + j : 97 + j, :] + turned[104 + j : 105 + j, :])[:, 0:24]
    g_bias[...] = stage[0:6, 0:24]
    g_gain[...] = stage[6:8, 0:24]
    near = sums[8:16, pl.ds(pl.multiple_of(128 * ((96 * me) // 128), 128), 256)]
    g_fbias[...] = dot_exact(near, as_number(hot_back(256, 96, (96 * me) % 128)))[0:1]

    sent(4)
    sent(5)
    wait_boxes(actw_in, s_act)
    wait_boxes(late, s_late)
    token_copy.wait()
    for i in range(4):
        rows = pl.ds(256 * (i % 2), 256)
        pltpu.make_async_copy(nlow.at[pl.ds(256 * i, 256)], hidden_hbm.at[i // 2, rows], s_hid.at[i]).wait()


def hot_back(rows, columns, shift):
    row = lax.broadcasted_iota(jnp.int32, (rows, columns), 0)
    column = lax.broadcasted_iota(jnp.int32, (rows, columns), 1)
    return row == column + shift


def dot_exact(a, b, dims=((1,), (0,))):
    return lax.dot_general(a, b, (dims, ((), ())), preferred_element_type=F32, precision=HIGH)


def hand_over(*refs):
    n = len(refs) // 3
    here, there, held = refs[:n], refs[n : 2 * n], refs[2 * n : 3 * n]
    s_in, s_out = refs[3 * n :]
    parts = []
    for i in range(n):
        rows = here[i].shape[-2]
        cuts = range(0, rows, rows // 4) if rows == 512 else [0]
        for at in cuts:
            size = rows // len(cuts)
            where = (slice(None),) * (len(here[i].shape) - 2) + (pl.ds(at, size),)
            parts.append([ref[i].at[where] for ref in (here, held, there)])
    loads = [pltpu.make_async_copy(p[0], p[1], s_in.at[k]) for k, p in enumerate(parts)]
    stores = [pltpu.make_async_copy(p[1], p[2], s_out.at[k]) for k, p in enumerate(parts)]
    for load in loads:
        load.start()
    for load, store in zip(loads, stores):
        load.wait()
        store.start()
    for store in stores:
        store.wait()


def encoder_step(
    tokens, qkv_weight, proj_weight, ffn_in_weight, ffn_out_weight, bias_rows, ffn_bias, norm_gains, buckets, padding, dropout
):
    def vm(*shape):
        return pltpu.VMEM(shape, BF)

    def vf(*shape):
        return pltpu.VMEM(shape, F32)

    def sems(*shape):
        return pltpu.SemaphoreType.DMA(shape)

    one = pltpu.SemaphoreType.DMA
    inside = pl.BlockSpec(memory_space=pltpu.VMEM)
    anywhere = pl.BlockSpec(memory_space=pl.ANY)
    engine = [sems(7, 4)] * 6 + [sems(4)]
    out = pl.pallas_call(
        encoder_kernel,
        name="encoder_step",
        out_shape=[
            jax.ShapeDtypeStruct((2, 512, 768), BF),
            jax.ShapeDtypeStruct((1, 1), F32),
            jax.ShapeDtypeStruct((512, 768), F32),
            jax.ShapeDtypeStruct((24, 2304), F32),
            jax.ShapeDtypeStruct((24, 768), F32),
            jax.ShapeDtypeStruct((24, 3072), F32),
            jax.ShapeDtypeStruct((96, 768), F32),
            jax.ShapeDtypeStruct((6, 24), F32),
            jax.ShapeDtypeStruct((1, 96), F32),
            jax.ShapeDtypeStruct((2, 24), F32),
        ],
        in_specs=[inside] * 10 + [anywhere],
        out_specs=[anywhere, inside, anywhere] + [inside] * 7,
        scratch_shapes=[
            vm(768, PW), vm(768, 3072), vm(3072, 768),
            vm(4, 2, 2, 16, WIDE + SW), vm(4, 2, 2, 16, WIDE), vm(4, 2, 2, 16, WIDE),
            vm(8, 4, 16, 768), vm(8, 4, 16, 768), vm(8, 4, 16, 1536), vm(8, 4, 16, 768),
            vm(8, 4, 16, SW), vf(16, SW), vf(16, 3328),
            pltpu.VMEM((2, 512, 768), jnp.int32), vm(512, 2304), vf(512, 512), vm(512, 768),
            vf(2, 512, 768), vm(1024, 768), vm(1024, 3072),
            vf(120, 768), vf(8, 512), vm(8, 512), vf(16, 3072), vm(16, 3200), vf(96, 512),
            vm(208, 512), vm(208, 768), vf(128, 768), vf(768, 128), vf(256, 768), vf(256, 768), vf(16, 3328),
            vm(32, 32, 128), vm(32, 32, 128), vm(32, 32, 128), vm(32, 32, 128), vm(32, 16, 256),
            vf(512, 768), vm(768, 512), vm(512, 256),
            vm(512, 32), vm(512, 32), vm(512, 32), vf(32, 128), vm(512, 3072),
        ] + engine + engine + [one] * 6 + [sems(2), sems(4), one],
        compiler_params=pltpu.CompilerParams(
            collective_id=0, has_side_effects=True, vmem_limit_bytes=63 * 2**20
        ),
    )(
        qkv_weight, proj_weight, ffn_in_weight, ffn_out_weight, bias_rows, norm_gains,
        ffn_bias[None], tokens, buckets, padding[None], dropout,
    )
    out = pl.pallas_call(
        hand_over,
        name="hand_over",
        out_shape=[jax.ShapeDtypeStruct(o.shape, o.dtype) for o in out],
        in_specs=[anywhere] * 10,
        out_specs=[anywhere] * 10,
        scratch_shapes=[pltpu.VMEM(o.shape, o.dtype) for o in out] + [sems(16), sems(16)],
        compiler_params=pltpu.CompilerParams(vmem_limit_bytes=60 * 2**20),
    )(*out)
    hidden, loss, gtok, g_qkv, g_proj, g_in, g_out, g_bias, g_fbias, g_gain = out
    return (hidden, loss[0, 0], gtok, g_qkv, g_proj, g_in, g_out, g_bias, g_fbias[0], g_gain)


def solution(mesh):
    in_specs = (
        P(AXES, None),
        P(AXES, None),
        P(AXES, None),
        P(AXES, None),
        P(AXES, None),
        P(None, AXES),
        P(AXES),
        P(None, AXES),
        P(AXES, None),
        P(AXES),
        P(None, None, AXES, None),
    )
    out_specs = (
        P(None, AXES, None),
        P(),
        P(AXES, None),
        P(AXES, None),
        P(AXES, None),
        P(AXES, None),
        P(AXES, None),
        P(None, AXES),
        P(AXES),
        P(None, AXES),
    )
    grid_fits = mesh.shape["dp"] == 8 and mesh.shape["fsdp"] == 4
    return jax.shard_map(
        encoder_step if grid_fits else with_collectives, mesh=mesh, in_specs=in_specs, out_specs=out_specs, check_vma=False
    )
```

```python
import functools

import jax
import jax.numpy as jnp
from jax import lax
from jax.experimental import pallas as pl
from jax.experimental.pallas import tpu as pltpu
from jax.sharding import PartitionSpec as P

H = 12
HD = 64

NEGATIVE = -1e30
NORM_EPSILON = 1e-12
UNIT_EPSILON = 1e-06
SOFTMAX_TEMP = 0.05
KEEP_SCALE = 1.0 / 0.9
FULL_PRECISION = lax.Precision.HIGHEST
AXES = ("dp", "fsdp")
BF = jnp.bfloat16
F32 = jnp.float32


def dot(a, b, dims=((1,), (0,))):
    return lax.dot_general(a, b, (dims, ((), ())), preferred_element_type=F32)


def layer_norm(inputs, gain_vec, shift_vec):
    centre = inputs - jnp.mean(inputs, axis=-1, keepdims=True)
    spread = jnp.mean(centre * centre, axis=-1, keepdims=True)
    return centre * lax.rsqrt(spread + NORM_EPSILON) * gain_vec + shift_vec


def normalize(inputs):
    return inputs * lax.rsqrt(jnp.sum(inputs * inputs, axis=-1, keepdims=True) + UNIT_EPSILON)


def exact_gelu(inputs):
    return jax.nn.gelu(inputs, approximate=False)


def sentence_layout(bucket_row, pad_row, rows_here):
    row_ids = jnp.arange(rows_here, dtype=jnp.int32)
    starts = jnp.cumsum(bucket_row) - bucket_row
    used = bucket_row > 0
    member = (row_ids[:, None] >= starts[None, :]) & used[None, :]
    sentence = jnp.sum(member.astype(jnp.int32), axis=1)
    allowed = (sentence[:, None] == sentence[None, :]) & (pad_row[None, :] > 0)
    select = ((row_ids[None, :] == starts[:, None]) & used[:, None]).astype(jnp.float32)
    slot_allowed = (
        (sentence[None, :] == jnp.arange(1, bucket_row.shape[0] + 1)[:, None])
        & used[:, None]
        & (pad_row[None, :] > 0)
    )
    return (allowed, select, slot_allowed)


def gather(x, axis=0):
    return lax.all_gather(x, AXES, axis=axis, tiled=True)


def all_to_all(x):
    return lax.all_to_all(x, AXES, split_axis=0, concat_axis=0, tiled=True)


def with_collectives(
    tokens,
    qkv_weight,
    proj_weight,
    ffn_in_weight,
    ffn_out_weight,
    bias_rows,
    ffn_bias,
    norm_gains,
    buckets,
    padding,
    dropout,
):
    rows_here, width = tokens.shape
    slots = buckets.shape[1]
    hidden = ffn_in_weight.shape[1]
    small = bias_rows.shape[1]
    devices = width // small
    hidden_small = hidden // devices
    me = lax.axis_index(AXES)
    score_scale = HD ** (-0.5)
    used_slot = (buckets[0] > 0).astype(BF)

    params = jnp.concatenate(
        [bias_rows.reshape(-1), norm_gains.reshape(-1), ffn_bias, used_slot]
    )
    params_all = gather(params[None])
    qp = gather(jnp.concatenate([qkv_weight, proj_weight], axis=1))
    qkv_full, proj_full = qp[:, : 3 * width], qp[:, 3 * width :]
    in_full = gather(ffn_in_weight)
    out_full = gather(ffn_out_weight)
    rows8 = params_all[:, : 8 * small].reshape(devices, 8, small).transpose(1, 0, 2)
    rows8 = rows8.reshape(8, width).astype(F32)
    bias_f, gain_f = rows8[:6], rows8[6:]
    ffn_bias_f = params_all[:, 8 * small : 8 * small + hidden_small].reshape(-1).astype(F32)
    used_all = params_all[:, 8 * small + hidden_small :].reshape(-1)

    allowed, select, slot_allowed = sentence_layout(buckets[0], padding, rows_here)
    select_low = select.astype(BF)
    zero_row = jnp.zeros((width,), F32)
    qkv = (dot(tokens, qkv_full) + jnp.concatenate([bias_f[0], zero_row, bias_f[1]])).astype(BF)
    head_view = qkv.reshape(rows_here, 3, H, HD)
    queries, key_rows, value_rows = (head_view[:, 0], head_view[:, 1], head_view[:, 2])

    scores = (
        jnp.einsum("qhd,khd->hqk", queries, key_rows, preferred_element_type=F32) * score_scale
    )
    scores = jnp.where(allowed[None], scores, NEGATIVE)
    exp_scores = jnp.exp(scores - jnp.max(scores, axis=-1, keepdims=True))
    probability = (exp_scores / jnp.sum(exp_scores, axis=-1, keepdims=True)).astype(BF)
    context = jnp.einsum("hqk,khd->qhd", probability, value_rows, preferred_element_type=F32)
    context = context.reshape(rows_here, width).astype(BF)
    branch = dot(context, proj_full) + bias_f[2]
    keep_mask = dropout.astype(F32)
    mixed_one = tokens.astype(F32)[None] + branch[None] * keep_mask[:, 0] * KEEP_SCALE
    normed = layer_norm(mixed_one, gain_f[0], bias_f[3])
    normed_low = normed.astype(BF)
    preact = dot(normed_low.reshape(-1, width), in_full) + ffn_bias_f
    activation = exact_gelu(preact).astype(BF)
    ffn_out = (dot(activation, out_full) + bias_f[4]).reshape(normed.shape)
    mixed_two = normed + ffn_out * keep_mask[:, 1] * KEEP_SCALE
    hidden_out = layer_norm(mixed_two, gain_f[1], bias_f[5]).astype(BF)

    tokens_s = dot(select_low, tokens)
    qkv_s = dot(select_low, qkv).astype(BF)
    queries_s = qkv_s[:, :width].reshape(slots, H, HD)
    scores_s = (
        jnp.einsum("shd,khd->hsk", queries_s, key_rows, preferred_element_type=F32) * score_scale
    )
    scores_s = jnp.where(slot_allowed[None], scores_s, NEGATIVE)
    peak_s = jnp.max(scores_s, axis=-1, keepdims=True)
    exp_s = jnp.exp(scores_s - peak_s) * slot_allowed[None].astype(F32)
    probability_f = exp_s / jnp.maximum(jnp.sum(exp_s, axis=-1, keepdims=True), 1e-30)
    probability_s = probability_f.astype(BF)
    context_s = dot(select_low, context).astype(BF)
    branch_s = dot(context_s, proj_full) + bias_f[2]
    keep_s = jnp.einsum(
        "sr,vbrd->vbsd", select_low, dropout.astype(BF), preferred_element_type=F32
    )
    mixed_s = tokens_s[None] + branch_s[None] * keep_s[:, 0] * KEEP_SCALE
    normed_s, first_back = jax.vjp(layer_norm, mixed_s, gain_f[0], bias_f[3])
    normed_s_low = normed_s.astype(BF).reshape(2 * slots, width)
    preact_s = dot(normed_s_low, in_full) + ffn_bias_f
    activation_sf, gelu_back = jax.vjp(exact_gelu, preact_s)
    activation_s = activation_sf.astype(BF)
    ffn_out_s = (dot(activation_s, out_full) + bias_f[4]).reshape(normed_s.shape)
    mixed_two_s = normed_s + ffn_out_s * keep_s[:, 1] * KEEP_SCALE
    final_s, second_back = jax.vjp(layer_norm, mixed_two_s, gain_f[1], bias_f[5])
    used_f = used_slot.astype(F32)
    final_s = final_s * used_f[None, :, None]
    unit_s, unit_back = jax.vjp(normalize, final_s)
    unit_low = unit_s.astype(BF)

    unit_all = gather(unit_low.reshape(1, 2, slots, width))
    unit_0 = unit_all[:, 0].reshape(-1, width)
    unit_1 = unit_all[:, 1].reshape(-1, width)
    logits = dot(unit_0, unit_1, ((1,), (1,))) / SOFTMAX_TEMP
    logits = jnp.where(used_all[None, :] > 0, logits, NEGATIVE)
    total = unit_0.shape[0]
    ids = jnp.arange(total, dtype=jnp.int32)
    diagonal = ids[:, None] == ids[None, :]
    logit_peak = jnp.max(logits, axis=-1, keepdims=True)
    logit_total = logit_peak[:, 0] + jnp.log(jnp.sum(jnp.exp(logits - logit_peak), axis=-1))
    positive = jnp.sum(jnp.where(diagonal, logits, 0.0), axis=1)
    used_all_f = used_all.astype(F32)
    loss_mean = jnp.sum((logit_total - positive) * used_all_f) / jnp.sum(used_all_f)
    soft = jnp.exp(logits - logit_total[:, None])
    logit_gradient = ((soft - diagonal.astype(F32)) * used_all_f[:, None]).astype(BF)
    mine_rows = lax.dynamic_slice_in_dim(logit_gradient, me * slots, slots, 0)
    mine_columns = lax.dynamic_slice_in_dim(logit_gradient, me * slots, slots, 1)
    grad_unit = jnp.stack(
        [dot(mine_rows, unit_1), dot(mine_columns, unit_0, ((0,), (0,)))]
    ) / SOFTMAX_TEMP
    (grad_final,) = unit_back(grad_unit)
    grad_final = grad_final * used_f[None, :, None]
    grad_mixed_two, grad_gain_two, grad_shift_two = second_back(grad_final)
    grad_ffn = (grad_mixed_two * keep_s[:, 1] * KEEP_SCALE).astype(BF).reshape(-1, width)
    grad_shift_out = jnp.sum(grad_ffn.astype(F32), axis=0)
    grad_act = dot(grad_ffn, out_full, ((1,), (1,)))
    (grad_preact_f,) = gelu_back(grad_act)
    grad_preact = grad_preact_f.astype(BF)
    grad_hidden_bias = jnp.sum(grad_preact.astype(F32), axis=0)
    grad_normed = dot(grad_preact, in_full, ((1,), (1,))).reshape(normed_s.shape) + grad_mixed_two
    grad_mixed, grad_gain_one, grad_shift_one = first_back(grad_normed)
    grad_branch = jnp.sum(grad_mixed * keep_s[:, 0] * KEEP_SCALE, axis=0).astype(BF)
    grad_shift_proj = jnp.sum(grad_branch.astype(F32), axis=0)
    grad_context = dot(grad_branch, proj_full, ((1,), (1,))).astype(BF)
    grad_context_h = grad_context.reshape(slots, H, HD)
    grad_probs = jnp.einsum(
        "shd,khd->hsk", grad_context_h, value_rows, preferred_element_type=F32
    )
    inner = jnp.sum(probability_f * grad_probs, axis=-1, keepdims=True)
    grad_scores = (probability_f * (grad_probs - inner)).astype(BF)
    grad_queries = (
        (jnp.einsum("hsk,khd->shd", grad_scores, key_rows, preferred_element_type=F32) * score_scale)
        .reshape(slots, width)
        .astype(BF)
    )
    pairs = jnp.concatenate([grad_scores, probability_s], axis=0).reshape(2 * H * slots, rows_here)
    token_sums = dot(pairs, tokens).astype(BF)
    key_factor = (queries_s.astype(F32) * score_scale).astype(BF)
    back_w = qkv_full.reshape(width, 3, H, HD)
    through = jnp.concatenate(
        [
            jnp.einsum("shd,whd->hsw", key_factor, back_w[:, 1], preferred_element_type=F32),
            jnp.einsum("shd,whd->hsw", grad_context_h, back_w[:, 2], preferred_element_type=F32),
        ],
        axis=0,
    ).reshape(2 * H * slots, width)
    start_grad = jnp.sum(grad_mixed, axis=0) + dot(
        grad_queries, qkv_full[:, :width], ((1,), (1,))
    )
    grad_tokens = dot(pairs, through.astype(BF), ((0,), (0,))) + lax.dot_general(
        select, start_grad, (((0,), (0,)), ((), ())), precision=FULL_PRECISION
    )
    value_sum = jnp.sum(probability_s.astype(F32), axis=-1).T
    grad_shift_value = jnp.sum(value_sum[:, :, None] * grad_context_h.astype(F32), axis=0).reshape(-1)
    grad_shift_query = jnp.sum(grad_queries.astype(F32), axis=0)

    wide = gather(jnp.concatenate([grad_ffn, grad_preact], axis=1))
    gffn_all, gpre_all = wide[:, :width], wide[:, width:]
    narrow = gather(
        jnp.concatenate([grad_branch, key_factor.reshape(slots, width), grad_context, grad_queries], axis=1)
    )
    gbranch_all = narrow[:, :width]
    key_all = narrow[:, width : 2 * width].reshape(-1, H, HD)
    gctx_all = narrow[:, 2 * width : 3 * width].reshape(-1, H, HD)
    gq_all = narrow[:, 3 * width :]

    def cut(x, n):
        return x.reshape(x.shape[0], devices, n).transpose(1, 0, 2).reshape(devices, -1)

    bias_sums = jnp.concatenate(
        [
            jnp.stack(
                [
                    grad_shift_query,
                    grad_shift_value,
                    grad_shift_proj,
                    grad_shift_one,
                    grad_shift_out,
                    grad_shift_two,
                    grad_gain_one,
                    grad_gain_two,
                ]
            )
            .reshape(8, devices, small)
            .transpose(1, 0, 2)
            .reshape(devices, -1),
            grad_hidden_bias.reshape(devices, -1),
        ],
        axis=1,
    )
    high = bias_sums.astype(BF)
    lower = (bias_sums - high.astype(F32)).astype(BF)
    pieces = [
        cut(activation_s, hidden_small),
        cut(normed_s_low, small),
        cut(context_s, small),
        cut(tokens_s.astype(BF), small),
        cut(token_sums, small),
        high,
        lower,
    ]
    sizes = [p.shape[1] for p in pieces]
    received = all_to_all(jnp.concatenate(pieces, axis=1))
    ends = []
    at = 0
    for n in sizes:
        ends.append(received[:, at : at + n])
        at += n
    act_r = ends[0].reshape(-1, hidden_small)
    normed_r = ends[1].reshape(-1, small)
    ctx_r = ends[2].reshape(-1, small)
    tok_r = ends[3].reshape(-1, small)
    sums_r = ends[4].reshape(devices, 2, H, slots, small)
    bias_r = jnp.sum(ends[5].astype(F32) + ends[6].astype(F32), axis=0)

    grad_out_weight = dot(act_r, gffn_all, ((0,), (0,)))
    grad_in_weight = dot(normed_r, gpre_all, ((0,), (0,)))
    grad_proj = dot(ctx_r, gbranch_all, ((0,), (0,)))
    grad_q = dot(tok_r, gq_all, ((0,), (0,)))
    keys_r = sums_r[:, 0].transpose(1, 0, 2, 3).reshape(H, -1, small)
    values_r = sums_r[:, 1].transpose(1, 0, 2, 3).reshape(H, -1, small)
    grad_k = jnp.einsum("hnw,nhd->whd", keys_r, key_all, preferred_element_type=F32)
    grad_v = jnp.einsum("hnw,nhd->whd", values_r, gctx_all, preferred_element_type=F32)
    grad_qkv_weight = jnp.concatenate(
        [grad_q, grad_k.reshape(small, width), grad_v.reshape(small, width)], axis=1
    )
    bias8 = bias_r[: 8 * small].reshape(8, small)
    return (
        hidden_out,
        loss_mean,
        grad_tokens,
        grad_qkv_weight,
        grad_proj,
        grad_in_weight,
        grad_out_weight,
        bias8[:6],
        bias_r[8 * small :],
        bias8[6:],
    )


MESH = pl.DeviceIdType.MESH
PW, QW, SW = 3072, 1536, 256
WIDE = PW + QW
HIGH = lax.Precision.HIGHEST
LAST = ((1,), (1,))
FIRST = ((0,), (0,))
WHOLE = (WIDE + SW, WIDE, WIDE, 768, 768, 1536, 768)


def place():
    dp = lax.axis_index("dp")
    fs = lax.axis_index("fsdp")
    return dp // 2, dp % 2, fs // 2, fs % 2


def peer_z(z, r):
    return (z + r) % 2 + 2 * ((z // 2 + r // 2) % 2)


def hot(rows, columns, shift):
    row = lax.broadcasted_iota(jnp.int32, (rows, columns), 0)
    column = lax.broadcasted_iota(jnp.int32, (rows, columns), 1)
    return row + shift == column


def as_number(flags):
    return jnp.where(flags, 1.0, 0.0)


def tail_of(x):
    t = 1.0 / (1.0 + (0.3275911 * 0.7071067811865476) * jnp.abs(x))
    bell = jnp.exp(x * x * -0.5)
    poly = 0.5 * 1.061405429
    for c in (-1.453152027, 1.421413741, -0.284496736, 0.254829592):
        poly = poly * t + 0.5 * c
    return poly * t * bell, bell


def gelu(x):
    tail, _ = tail_of(x)
    return jnp.maximum(x, 0.0) - jnp.abs(x) * tail


def gelu_slope(x):
    tail, bell = tail_of(x)
    return jnp.where(x >= 0.0, 1.0 - tail, tail) + x * bell * 0.3989422804014327


def mean(x):
    return jnp.sum(x, axis=-1, keepdims=True) * (1.0 / x.shape[-1])


def standardize(x):
    centre = x - mean(x)
    scale = lax.rsqrt(mean(centre * centre) + NORM_EPSILON)
    return centre * scale, scale


def norm_back(grad_hat, hat, scale):
    return scale * (grad_hat - mean(grad_hat) - hat * mean(grad_hat * hat))


def encoder_kernel(
    qkv_ref, proj_ref, in_ref, out_ref, bias_ref, gain_ref, fbias_ref, tokens, buckets_ref, pad_ref, drop_hbm,
    hidden_hbm, loss_ref, gtok_hbm, g_qkv, g_proj, g_in, g_out, g_bias, g_fbias, g_gain,
    wqp, win, wout, l0, l1, l2, f3, f4, f5, f6, pb, stage, par,
    drop, qkv, madd, ctx, normed, nlow, act,
    cls, sm8, sel, pre_s, acts, p_f, pairs, through, mixer, mixer_t, unit0, unit1, sums,
    early, early_in, late, late_in, actw_in, gtok, keys_t, values1, mix_n, mix_c, mix_t, rest, slope, mix_o, half_s, half_r,
    sz, sx, sy, sa, sb, sc, scp, rz, rx, ry, ra, rb, rc, rcp, s_early, r_early, s_act, r_act, s_late, r_late, s_drop, s_hid, s_tok, s_mix, r_mix, s_half, r_half,
):
    z, c, y, x = place()
    me = 8 * z + 4 * c + 2 * y + x
    land = (l0, l1, l2)
    full = (f3, f4, f5, f6)
    weights = (wqp, win, wout)
    lanes = functools.partial(lax.broadcasted_iota, jnp.int32)

    def dev(z_, c_, y_, x_):
        return (2 * z_ + c_, 2 * y_ + x_)

    def other(i):
        t = (me + i) % 32
        return t, (t // 4, t % 4)

    def loop(lo, hi, body):
        def step(i, carry):
            body(i)
            return carry

        lax.fori_loop(lo, hi, step, 0)

    bar = pltpu.get_barrier_semaphore()

    def greet(i):
        _, device = other(i)
        pl.semaphore_signal(bar, inc=1, device_id=device, device_id_type=MESH)

    loop(1, 32, greet)
    drop_copy = pltpu.make_async_copy(drop_hbm.at[:, 0], drop, s_drop.at[0])
    drop_copy.start()

    def slot(ph, zz, yy, xx):
        if ph < 3:
            return land[ph].at[zz, yy, xx]
        return full[ph - 3].at[2 * zz + c, 2 * yy + xx]

    def rcopy(ref, s, r, device):
        return pltpu.make_async_remote_copy(
            src_ref=ref, dst_ref=ref, send_sem=s, recv_sem=r, device_id=device, device_id_type=MESH
        )

    def cp_z(ph, r):
        return rcopy(slot(ph, z, y, x), sz.at[ph, r], rz.at[ph, r], dev(peer_z(z, r), c, y, x))

    def cp_x(ph, r):
        return rcopy(slot(ph, peer_z(z, r), y, x), sx.at[ph, r], rx.at[ph, r], dev(z, c, y, 1 - x))

    def cp_y(ph, r):
        return rcopy(slot(ph, peer_z(z, r), y, x), sy.at[ph, r], ry.at[ph, r], dev(z, c, 1 - y, x))

    def half(ph):
        return WHOLE[ph] // 256 * 128

    def cp_a(ph, r):
        ref = slot(ph, peer_z(z, r), y, 1 - x).at[:, 0 : half(ph)]
        return rcopy(ref, sa.at[ph, r], ra.at[ph, r], dev(z, c, 1 - y, x))

    def cp_b(ph, r):
        ref = slot(ph, peer_z(z, r), 1 - y, x).at[:, half(ph) : WHOLE[ph]]
        return rcopy(ref, sb.at[ph, r], rb.at[ph, r], dev(z, c, y, 1 - x))

    def cp_c(ph, r):
        group = 2 * peer_z(z, r) + c
        if ph < 3:
            n = 384 if ph == 2 else 96
            ref = weights[ph].at[pl.ds(pl.multiple_of(n * group, n), n)]
        else:
            ref = full[ph - 3].at[group]
        return rcopy(ref, sc.at[ph, r], rc.at[ph, r], dev(z, 1 - c, y, x))

    def cp_cp(r):
        return rcopy(pb.at[2 * peer_z(z, r) + c], scp.at[r], rcp.at[r], dev(z, 1 - c, y, x))

    def start_z(ph):
        loop(1, 4, lambda r: cp_z(ph, r).start())

    def start_xy(ph, r):
        cp_x(ph, r).start()
        cp_y(ph, r).start()

    def wait_z_start_xy(ph, r):
        cp_z(ph, r).wait_recv()
        start_xy(ph, r)

    def wait_xy_start_ab(ph, r):
        cp_x(ph, r).wait_recv()
        cp_a(ph, r).start()
        cp_y(ph, r).wait_recv()
        cp_b(ph, r).start()

    def merge(ph, r):
        zz = peer_z(z, r)
        group = 2 * zz + c
        if ph == 2:
            for yy in range(2):
                for xx in range(2):
                    base = 384 * group + 96 * (2 * yy + xx)
                    for j in range(6):
                        wout[pl.ds(pl.multiple_of(base + 16 * j, 16), 16), :] = l2[
                            zz, yy, xx, :, 768 * j : 768 * (j + 1)
                        ]
            return
        w = weights[ph]
        l = land[ph]
        spans = [(0, 2304, PW), (2304, 768, PW + 1152)] if ph == 0 else [(0, 3072, PW)]
        for yy in range(2):
            base = 96 * group + 48 * yy
            w[pl.ds(pl.multiple_of(base, 16), 16), :] = l[zz, yy, 0, :, 0:PW]
            w[pl.ds(pl.multiple_of(base + 32, 16), 16), :] = l[zz, yy, 1, :, 0:PW]
            middle = pl.ds(pl.multiple_of(base + 16, 16), 16)
            for at, n, qat in spans:
                qe = l[zz, yy, 0, :, qat : qat + n // 2].astype(F32)
                qo = l[zz, yy, 1, :, qat : qat + n // 2].astype(F32)
                w[middle, at : at + n // 2] = jnp.concatenate([qe[0:8], qo[0:8]], axis=0).astype(BF)
                w[middle, at + n // 2 : at + n] = jnp.concatenate([qe[8:16], qo[8:16]], axis=0).astype(BF)
        if ph == 0:
            for yy in range(2):
                for xx in range(2):
                    pb[group, 2 * yy + xx] = l0[zz, yy, xx, :, WIDE:]

    def wait_ab_start_c(ph, r):
        cp_a(ph, r).wait_recv()
        cp_b(ph, r).wait_recv()
        if ph < 3:
            merge(ph, r)
        cp_c(ph, r).start()
        if ph == 0:
            cp_cp(r).start()

    def wait_c(ph, r):
        cp_c(ph, r).wait_recv()
        if ph == 0:
            cp_cp(r).wait_recv()

    def pack(ph, parts):
        at, qat = 0, PW
        for ref in parts:
            v = ref[...].astype(F32)
            n = v.shape[1]
            p_rows = jnp.where(x == 0, v[0:16], v[8:24])
            q_rows = jnp.where(x == 0, v[16:24], v[0:8])
            land[ph][z, y, x, :, at : at + n] = p_rows.astype(BF)
            land[ph][z, y, x, :, qat : qat + n // 2] = jnp.concatenate(
                [q_rows[:, : n // 2], q_rows[:, n // 2 :]], axis=0
            ).astype(BF)
            at += n
            qat += n // 2

    pack(0, (qkv_ref, proj_ref))

    def put(v, shift):
        return dot(v.astype(BF), as_number(hot(v.shape[1], SW, shift)).astype(BF))

    bk = buckets_ref[...].astype(F32)
    stage[...] = jnp.zeros_like(stage)
    stage[0:6, :] = put(bias_ref[...], (24 * me) % 128)
    stage[6:8, :] = put(gain_ref[...], (24 * me) % 128)
    stage[8:9, :] = put(fbias_ref[...], (96 * me) % 128)
    stage[9:10, :] = put(as_number(bk > 0.0), (8 * me) % 128)
    l0[z, y, x, :, WIDE:] = stage[...].astype(BF)
    pl.semaphore_wait(bar, 31)

    start_z(0)
    start_xy(0, 0)
    pack(1, (in_ref,))
    for j in range(6):
        l2[z, y, x, :, 768 * j : 768 * (j + 1)] = out_ref[16 * j : 16 * (j + 1), :]

    start_xy(1, 0)

    row8, lane8 = lanes((8, 8), 0), lanes((8, 8), 1)
    bk_col = jnp.sum(jnp.where(row8 == lane8, bk, 0.0), axis=1, keepdims=True)
    starts_col = jnp.sum(jnp.where(lane8 < row8, bk, 0.0), axis=1, keepdims=True)
    starts_row = jnp.sum(jnp.where(row8 < lane8, bk_col, 0.0), axis=0, keepdims=True)
    used_mine = as_number(bk_col > 0.0)
    used16 = jnp.concatenate([used_mine, used_mine], axis=0)
    row_ids = lanes((512, 8), 0).astype(F32)
    column_ids = lanes((8, 512), 1).astype(F32)
    sent_row = jnp.sum(as_number((row_ids >= starts_row) & (bk > 0.0)), axis=1, keepdims=True)
    sent_col = jnp.sum(as_number((column_ids >= starts_col) & (bk_col > 0.0)), axis=0, keepdims=True)
    key_of = jnp.where(pad_ref[...] > 0, sent_col, 0.0)
    madd[...] = jnp.where(sent_row == key_of, 0.0, NEGATIVE)
    sm8[...] = as_number(key_of == (lanes((8, 512), 0) + 1).astype(F32))
    sel[...] = as_number((column_ids == starts_col) & (bk_col > 0.0)).astype(BF)

    wait_z_start_xy(0, 1)
    wait_xy_start_ab(0, 0)
    wait_z_start_xy(0, 2)
    wait_z_start_xy(0, 3)
    start_z(1)
    loop(1, 4, lambda r: wait_xy_start_ab(0, r))
    loop(1, 4, lambda r: wait_z_start_xy(1, r))
    start_z(2)
    start_xy(2, 0)
    loop(0, 4, lambda r: wait_ab_start_c(0, r))
    drop_copy.wait()
    loop(0, 4, lambda r: wait_c(0, r))
    par[...] = jnp.zeros_like(par)
    for d in range(32):
        w = pb[d // 4, d % 4].astype(F32)
        t, t2, t3 = 24 * d // 128, 96 * d // 128, 8 * d // 128
        par[0:8, 128 * t : 128 * t + 256] += w[0:8]
        par[8:9, 128 * t2 : 128 * t2 + 256] += w[8:9]
        par[9:10, 128 * t3 : 128 * t3 + 256] += w[9:10]

    def bias(i):
        return par[i : i + 1, 0:768]

    def gain(i):
        return par[6 + i : 7 + i, 0:768]

    def qkv_part(i):
        columns = pl.ds(pl.multiple_of(256 * i, 256), 256)
        inside = pl.ds(pl.multiple_of(256 * (i % 3), 256), 256)
        both = par[0:8, inside]
        part = jnp.where(i < 3, both[0:1], jnp.where(i < 6, 0.0, both[1:2]))
        qkv[:, columns] = (dot(tokens[...], wqp[:, columns]) + part).astype(BF)

    loop(0, 9, qkv_part)
    loop(0, 4, lambda r: wait_xy_start_ab(1, r))
    loop(1, 4, lambda r: wait_z_start_xy(2, r))

    left = lanes((1, 128), 1) < 64
    left_scale = jnp.where(left, HD**-0.5, 0.0)
    right_scale = jnp.where(left, 0.0, HD**-0.5)

    def turn_keys(i):
        columns = pl.ds(pl.multiple_of(768 + 128 * i, 128), 128)
        keys_t[pl.ds(pl.multiple_of(128 * i, 128), 128), :] = jnp.transpose(qkv[:, columns].astype(F32)).astype(BF)

    loop(0, 6, turn_keys)
    values1[:, 128:256] = jnp.ones((512, 128), BF)

    def attend(pair):
        def columns(part):
            return pl.ds(pl.multiple_of(768 * part + 128 * pair, 128), 128)

        values1[:, 0:128] = qkv[:, columns(2)]

        q = qkv[:, columns(0)].astype(F32)
        results = []
        for scale in (left_scale, right_scale):
            s = dot((q * scale).astype(BF), keys_t[columns(0), :]) + madd[...]
            e = jnp.exp(s - jnp.max(s, axis=-1, keepdims=True)).astype(BF)
            both = dot(e, values1[...])
            results.append(both[:, 0:128] * (1.0 / both[:, 128:256]))
        ctx[:, columns(0)] = jnp.where(left, results[0], results[1]).astype(BF)

    loop(0, 6, attend)
    wait_xy_start_ab(2, 0)

    def first_norm(i):
        rows = pl.ds(pl.multiple_of(128 * i, 128), 128)
        branch = (dot(ctx[rows, :], wqp[:, 2304:3072]) + bias(2)) * KEEP_SCALE
        token_rows = tokens[rows, :].astype(F32)
        for v in range(2):
            hat, _ = standardize(token_rows + branch * drop[v, rows, :].astype(F32))
            n = hat * gain(0) + bias(3)
            normed[v, rows, :] = n
            nlow[pl.ds(pl.multiple_of(512 * v + 128 * i, 128), 128), :] = n.astype(BF)

    loop(0, 4, first_norm)
    loop(0, 4, lambda r: wait_ab_start_c(1, r))
    wait_xy_start_ab(2, 1)

    TOK, QRY, CTX, KEEP1, KEEP2, HAT1, NRM, HAT2, FIN = 0, 8, 16, 24, 40, 56, 72, 88, 104
    pick = sel[...]
    cls[TOK : TOK + 8, :] = dot(pick, tokens[...])
    cls[QRY : QRY + 8, :] = dot(pick, qkv[:, 0:768]) * HD**-0.5
    cls[CTX : CTX + 8, :] = dot(pick, ctx[...])
    for v in range(2):
        cls[KEEP1 + 8 * v : KEEP1 + 8 * v + 8, :] = dot(pick, drop[v].astype(F32).astype(BF)) * KEEP_SCALE
    drop_copy = pltpu.make_async_copy(drop_hbm.at[:, 1], drop, s_drop.at[1])
    drop_copy.start()

    def twice(v):
        return jnp.concatenate([v, v], axis=0)

    head = lax.broadcasted_iota(jnp.int32, (12, 8, 768), 0) * 64
    lane = lax.broadcasted_iota(jnp.int32, (12, 8, 768), 2)
    own_head = (lane >= head) & (lane < head + 64)

    def spread(rows8):
        return jnp.where(own_head, rows8[None], 0.0).reshape(96, 768).astype(BF)

    def gathered(rows96):
        return jnp.sum(jnp.where(own_head, rows96.reshape(12, 8, 768), 0.0), axis=0)

    branch_s = dot(cls[CTX : CTX + 8, :].astype(BF), wqp[:, 2304:3072]) + bias(2)
    hat1, scale1 = standardize(twice(cls[TOK : TOK + 8, :]) + twice(branch_s) * cls[KEEP1 : KEEP1 + 16, :])
    normed_s = hat1 * gain(0) + bias(3)
    cls[HAT1 : HAT1 + 16, :] = hat1
    cls[NRM : NRM + 16, :] = normed_s
    f6[2 * z + c, 2 * y + x] = normed_s.astype(BF)
    start_z(6)
    query_big = spread(cls[QRY : QRY + 8, :])
    seen = jnp.broadcast_to(sm8[...][None], (12, 8, 512)).reshape(96, 512)
    s = jnp.where(seen > 0.0, dot(query_big, qkv[:, 768:1536], LAST), NEGATIVE)
    e = jnp.exp(s - jnp.max(s, axis=-1, keepdims=True)) * seen
    prob = e * (1.0 / jnp.maximum(jnp.sum(e, axis=-1, keepdims=True), 1e-30))
    p_f[...] = prob
    pairs[96:192, :] = prob.astype(BF)
    pairs[192:208, :] = twice(pick.astype(F32)).astype(BF)
    wait_xy_start_ab(2, 2)
    mixer[0:96, :] = dot(prob.astype(BF), tokens[...])
    mixer[96:104, :] = cls[CTX : CTX + 8, :]
    mixer[104:112, :] = cls[TOK : TOK + 8, :]
    mixer[112:128, :] = normed_s

    def send_mixer(box, box_in, s_sem, r_sem):
        mixer_t[...] = jnp.transpose(mixer[...])

        def cut(t):
            v = mixer_t[pl.ds(pl.multiple_of(24 * t, 8), 24), :]
            box[t] = jnp.concatenate([v, jnp.zeros((8, 128), F32)], axis=0).astype(BF)

        loop(0, 32, cut)
        box_in[me] = box[me]

        def send(i):
            t, device = other(i)
            pltpu.make_async_remote_copy(
                src_ref=box.at[t],
                dst_ref=box_in.at[me],
                send_sem=s_sem,
                recv_sem=r_sem,
                device_id=device,
                device_id_type=MESH,
            ).start()

        loop(1, 32, send)

    def wait_boxes(ref, sem):
        part = ref.at[pl.ds(0, 31)]
        pltpu.make_async_copy(part, part, sem).wait()

    send_mixer(early, early_in, s_early, r_early)

    loop(0, 4, lambda r: wait_c(1, r))

    def ffn_in(i):
        columns = pl.ds(pl.multiple_of(256 * i, 256), 256)
        act[:, columns] = gelu(dot(nlow[...], win[:, columns]) + par[8:9, columns]).astype(BF)

    loop(0, 2, ffn_in)
    wait_xy_start_ab(2, 3)
    start_xy(6, 0)
    loop(1, 4, lambda r: wait_z_start_xy(6, r))
    drop_copy.wait()
    for v in range(2):
        cls[KEEP2 + 8 * v : KEEP2 + 8 * v + 8, :] = dot(pick, drop[v].astype(F32).astype(BF)) * KEEP_SCALE
    preact_s = dot(cls[NRM : NRM + 16, :].astype(BF), win[...]) + par[8:9, 0:3072]
    pre_s[...] = preact_s
    acts[:, 0:3072] = gelu(preact_s).astype(BF)
    acts[:, 3072:3200] = jnp.zeros((16, 128), BF)

    def window(t):
        return acts.at[:, pl.ds(pl.multiple_of(128 * ((96 * t) // 128), 128), 256)]

    def send_act(i):
        t, device = other(i)
        pltpu.make_async_remote_copy(
            src_ref=window(t),
            dst_ref=actw_in.at[me],
            send_sem=s_act,
            recv_sem=r_act,
            device_id=device,
            device_id_type=MESH,
        ).start()

    loop(1, 32, send_act)
    actw_in[me] = window(me)[...]

    loop(2, 5, ffn_in)

    column32 = lanes((16, 32), 1)
    first8 = lanes((16, 32), 0) < 8
    ones8 = as_number(first8 & (column32 == 24))

    def turn_early(i):
        for d in range(4):
            m = jnp.transpose(early_in[4 * i + d].astype(F32))
            rows16 = pl.ds(pl.multiple_of(64 * i + 16 * d, 16), 16)
            empty = jnp.zeros((8, 32), F32)
            mix_c[rows16, :] = (jnp.concatenate([m[96:104], empty], axis=0) + ones8).astype(BF)
            mix_t[rows16, :] = (jnp.concatenate([m[104:112], empty], axis=0) + ones8).astype(BF)
            mix_n[rows16, :] = (m[112:128] + as_number(column32 == 24)).astype(BF)

    mix_copy = pltpu.make_async_remote_copy(
        src_ref=mix_n,
        dst_ref=mix_o,
        send_sem=s_mix,
        recv_sem=r_mix,
        device_id=dev(z, 1 - c, y, x),
        device_id_type=MESH,
    )
    half_copy = pltpu.make_async_remote_copy(
        src_ref=half_s,
        dst_ref=half_r,
        send_sem=s_half,
        recv_sem=r_half,
        device_id=dev(z, 1 - c, y, x),
        device_id_type=MESH,
    )

    def turn_all_early():
        loop(0, 8, turn_early)
        mix_copy.start()

    loop(0, 4, lambda r: wait_ab_start_c(2, r))
    loop(0, 4, lambda r: wait_c(2, r))
    keep2 = cls[KEEP2 : KEEP2 + 16, :]
    ffn_s = dot(acts[:, 0:3072], wout[...]) + bias(4)
    hat2, scale2 = standardize(cls[NRM : NRM + 16, :] + ffn_s * keep2)
    final_s = (hat2 * gain(1) + bias(5)) * used16
    length = lax.rsqrt(jnp.sum(final_s * final_s, axis=-1, keepdims=True) + UNIT_EPSILON)
    cls[HAT2 : HAT2 + 16, :] = hat2
    cls[FIN : FIN + 16, :] = final_s
    f3[2 * z + c, 2 * y + x] = (final_s * length).astype(BF)
    start_z(3)
    start_xy(3, 0)

    def ffn_out(i):
        v = i // 2
        rows = pl.ds(pl.multiple_of(256 * (i % 2), 256), 256)
        flat = pl.ds(pl.multiple_of(256 * i, 256), 256)
        out = dot(act[flat, :], wout[...]) + bias(4)
        hat, _ = standardize(normed[v, rows, :] + out * (drop[v, rows, :].astype(F32) * KEEP_SCALE))
        nlow[flat, :] = (hat * gain(1) + bias(5)).astype(BF)
        pltpu.make_async_copy(nlow.at[flat], hidden_hbm.at[v, rows], s_hid.at[i]).start()

    wait_boxes(early_in, r_early)
    turn_all_early()
    loop(5, 7, ffn_in)
    loop(1, 4, lambda r: wait_z_start_xy(3, r))
    loop(0, 4, lambda r: wait_xy_start_ab(6, r))
    loop(7, 9, ffn_in)
    loop(0, 4, lambda r: wait_xy_start_ab(3, r))
    loop(0, 4, lambda r: wait_ab_start_c(6, r))
    loop(9, 11, ffn_in)
    loop(0, 4, lambda r: wait_ab_start_c(3, r))
    loop(0, 4, lambda r: wait_c(6, r))

    def slopes(i):
        columns = pl.ds(pl.multiple_of(1536 * c + 512 * i, 512), 512)
        preact = dot(f6[...].reshape(512, 768), win[:, columns]) + par[8:9, columns]
        slope[:, pl.ds(pl.multiple_of(512 * i, 512), 512)] = gelu_slope(preact).astype(BF)

    slopes(0)
    loop(0, 4, lambda r: wait_c(3, r))

    def sent(ph):
        def of(r):
            for copy in (cp_x, cp_y, cp_a, cp_b, cp_c):
                copy(ph, r).wait_send()
            if ph == 0:
                cp_cp(r).wait_send()

        def to_peers(r):
            of(r)
            cp_z(ph, r).wait_send()

        of(0)
        loop(1, 4, to_peers)

    def part_units(i):
        v = f3[i // 4, i % 4].astype(F32)
        rows = pl.ds(pl.multiple_of(8 * i, 8), 8)
        unit0[rows, :] = v[0:8]
        unit1[rows, :] = v[8:16]

    loop(0, 32, part_units)
    u0, u1 = unit0[...].astype(BF), unit1[...].astype(BF)
    mine = pl.ds(pl.multiple_of(8 * me, 8), 8)
    u0_mine, u1_mine = unit0[mine, :].astype(BF), unit1[mine, :].astype(BF)
    used_row = par[9:10, 0:256]
    eye = hot(256, 256, 0)
    used_col = jnp.sum(jnp.where(eye, used_row, 0.0), axis=1, keepdims=True)
    by_column = jnp.where(used_col > 0.0, dot(u1, u0, LAST) * (1.0 / SOFTMAX_TEMP), NEGATIVE)
    peak = jnp.max(by_column, axis=0, keepdims=True)
    total = peak + jnp.log(jnp.sum(jnp.exp(by_column - peak), axis=0, keepdims=True))
    positive = jnp.sum(jnp.where(eye, by_column, 0.0), axis=0, keepdims=True)
    loss_sum = jnp.sum((total - positive) * used_row, axis=1, keepdims=True)
    loss_ref[...] = loss_sum / jnp.sum(used_row, axis=1, keepdims=True)
    target = as_number(hot(8, 256, 8 * me))
    mine_1 = jnp.where(used_mine > 0.0, dot(u1_mine, u0, LAST) * (1.0 / SOFTMAX_TEMP), NEGATIVE)
    grad_1 = ((jnp.exp(mine_1 - total) - target) * used_row).astype(BF)
    mine_0 = jnp.where(used_row > 0.0, dot(u0_mine, u1, LAST) * (1.0 / SOFTMAX_TEMP), NEGATIVE)
    peak_0 = jnp.max(mine_0, axis=1, keepdims=True)
    total_0 = peak_0 + jnp.log(jnp.sum(jnp.exp(mine_0 - peak_0), axis=1, keepdims=True))
    grad_0 = ((jnp.exp(mine_0 - total_0) - target) * used_mine).astype(BF)
    grad_unit = jnp.concatenate([dot(grad_0, u1), dot(grad_1, u0)], axis=0) * (1.0 / SOFTMAX_TEMP)
    final_s = cls[FIN : FIN + 16, :]
    hat2 = cls[HAT2 : HAT2 + 16, :]
    pull = jnp.sum(grad_unit * final_s, axis=-1, keepdims=True)
    grad_final = (grad_unit - final_s * (pull * length * length)) * length * used16

    grad_mixed_two = norm_back(grad_final * gain(1), hat2, scale2)
    grad_ffn = (grad_mixed_two * cls[KEEP2 : KEEP2 + 16, :]).astype(BF)
    f4[2 * z + c, 2 * y + x] = grad_ffn
    start_z(4)
    start_xy(4, 0)
    grad_pre = (dot(grad_ffn, wout[...], LAST) * gelu_slope(pre_s[...])).astype(BF)
    grad_normed = dot(grad_pre, win[...], LAST) + grad_mixed_two
    hat1 = cls[HAT1 : HAT1 + 16, :]
    grad_mixed = norm_back(grad_normed * gain(0), hat1, scale1)
    dropped = grad_mixed * cls[KEEP1 : KEEP1 + 16, :]
    grad_branch = (dropped[0:8] + dropped[8:16]).astype(BF)
    grad_ctx = dot(grad_branch, wqp[:, 2304:3072], LAST).astype(BF)
    loop(1, 4, lambda r: wait_z_start_xy(4, r))
    grad_big = spread(grad_ctx.astype(F32))
    query_big = spread(cls[QRY : QRY + 8, :])
    grad_probs = dot(grad_big, qkv[:, 1536:2304], LAST)
    prob = p_f[...]
    weighted = prob * grad_probs
    grad_scores = (weighted - prob * jnp.sum(weighted, axis=-1, keepdims=True)).astype(BF)
    pairs[0:96, :] = grad_scores
    grad_q = (gathered(dot(grad_scores, qkv[:, 768:1536])) * HD**-0.5).astype(BF)
    own5 = f5.at[2 * z + c, 2 * y + x]
    own5[:, 0:768] = jnp.concatenate([grad_branch.astype(F32), grad_ctx.astype(F32)], axis=0).astype(BF)
    own5[:, 768:1536] = jnp.concatenate([grad_q.astype(F32), cls[QRY : QRY + 8, :]], axis=0).astype(BF)
    start_z(5)
    start_xy(5, 0)
    wait_boxes(early, s_early)
    mixer[0:96, :] = dot(grad_scores, tokens[...])
    value_sum = jnp.sum(pairs[96:192, :].astype(F32), axis=-1, keepdims=True)
    own_sums = [
        jnp.sum(value_sum * grad_big.astype(F32), axis=0, keepdims=True),
        jnp.sum(grad_normed, axis=0, keepdims=True),
        jnp.sum(grad_final, axis=0, keepdims=True),
        jnp.sum(grad_normed * hat1, axis=0, keepdims=True),
        jnp.sum(grad_final * hat2, axis=0, keepdims=True),
    ]
    mixer[96:128, :] = jnp.zeros((32, 768), F32)
    for j, v in enumerate(own_sums):
        upper = v.astype(BF).astype(F32)
        mixer[96 + j : 97 + j, :] = upper
        mixer[104 + j : 105 + j, :] = v - upper
    send_mixer(late, late_in, s_late, r_late)
    slopes(1)
    loop(0, 4, lambda r: wait_xy_start_ab(4, r))
    slopes(2)
    loop(1, 4, lambda r: wait_z_start_xy(5, r))
    loop(0, 4, lambda r: wait_ab_start_c(4, r))
    loop(11, 12, ffn_in)
    ffn_out(0)
    loop(0, 4, lambda r: wait_xy_start_ab(5, r))
    for ph in (0, 1, 2, 3, 6):
        sent(ph)

    through[0:96, :] = dot(query_big, wqp[:, 768:1536], LAST).astype(BF)
    through[96:192, :] = dot(grad_big, wqp[:, 1536:2304], LAST).astype(BF)
    start_grad = grad_mixed[0:8] + grad_mixed[8:16] + dot(grad_q, wqp[:, 0:768], LAST)
    upper = start_grad.astype(BF).astype(F32)
    through[192:208, :] = jnp.concatenate([upper, start_grad - upper], axis=0).astype(BF)

    def token_grad(i):
        columns = pl.ds(pl.multiple_of(256 * i, 256), 256)
        gtok[:, columns] = dot(pairs[...], through[:, columns], FIRST)

    loop(0, 3, token_grad)
    token_copy = pltpu.make_async_copy(gtok, gtok_hbm, s_tok)
    token_copy.start()
    loop(0, 4, lambda r: wait_ab_start_c(5, r))
    wait_boxes(actw_in, r_act)
    act_mine = dot(actw_in[...].reshape(512, 256), as_number(hot_back(256, 128, (96 * me) % 128)).astype(BF))
    act_mine = jnp.where(lanes((512, 128), 1) == 96, 1.0, act_mine).astype(BF)
    loop(0, 4, lambda r: wait_c(4, r))
    ffn_out(1)

    out_rows = dot(act_mine, f4[...].reshape(512, 768), FIRST)
    g_out[...] = out_rows[0:96]
    sums[...] = jnp.zeros_like(sums)
    sums[4:5, 0:768] = out_rows[96:97]

    mix_copy.wait_recv()

    def in_rows(i):
        here = pl.ds(pl.multiple_of(768 * i, 256), 768)
        to = pl.ds(pl.multiple_of(1536 * c + 768 * i, 256), 768)
        grad_act = dot(f4[...].reshape(512, 768), wout[to, :], LAST)
        grad_pre = (grad_act * slope[:, here].astype(F32)).astype(BF)
        rows = dot(mix_n[...], grad_pre, FIRST)
        g_in[:, to] = rows[0:24]
        sums[8:16, to] = rows[24:32]
        half_s[:, here] = dot(mix_o[...], grad_pre, FIRST)

    loop(0, 2, in_rows)
    half_copy.start()
    ffn_out(2)
    ffn_out(3)
    half_copy.wait_recv()
    there = pl.ds(pl.multiple_of(1536 * (1 - c), 256), 1536)
    g_in[:, there] = half_r[0:24, :]
    sums[8:16, there] = half_r[24:32, :]
    loop(0, 4, lambda r: wait_c(5, r))
    rows = dot(mix_c[...], f5[:, :, :, 0:768].reshape(512, 768), FIRST)
    g_proj[...] = rows[0:24]
    sums[2:3, 0:768] = rows[24:25]
    rows = dot(mix_t[...], f5[:, :, :, 768:1536].reshape(512, 768), FIRST)
    g_qkv[:, 0:768] = rows[0:24]
    sums[0:1, 0:768] = rows[24:25]

    def value_rows(g):
        total = dot(early_in[4 * g][:, 0:96], spread(f5[g, 0, :, 0:768].astype(F32)[8:16]))
        for i in range(1, 4):
            total += dot(early_in[4 * g + i][:, 0:96], spread(f5[g, i, :, 0:768].astype(F32)[8:16]))
        unit0[0:32, :] += total

    unit0[0:64, :] = jnp.zeros((64, 768), F32)
    loop(0, 8, value_rows)
    wait_boxes(late_in, r_late)
    rest[...] = jnp.zeros_like(rest)

    def key_rows(g):
        total = dot(late_in[4 * g][:, 0:96], spread(f5[g, 0, :, 768:1536].astype(F32)[8:16]))
        extra = late_in[4 * g].astype(F32)
        for i in range(1, 4):
            total += dot(late_in[4 * g + i][:, 0:96], spread(f5[g, i, :, 768:1536].astype(F32)[8:16]))
            extra += late_in[4 * g + i].astype(F32)
        unit0[32:64, :] += total
        rest[...] += extra

    loop(0, 8, key_rows)
    g_qkv[:, 768:1536] = unit0[32:56, :]
    g_qkv[:, 1536:2304] = unit0[0:24, :]
    turned = jnp.transpose(rest[...])
    near = sums[0:8, pl.ds(pl.multiple_of(128 * ((24 * me) // 128), 128), 256)]
    stage[0:8, 0:24] = dot_exact(near, as_number(hot_back(256, 24, (24 * me) % 128)))
    for j, row in enumerate((1, 3, 5, 6, 7)):
        stage[row : row + 1, 0:24] = (turned[96 + j : 97 + j, :] + turned[104 + j : 105 + j, :])[:, 0:24]
    g_bias[...] = stage[0:6, 0:24]
    g_gain[...] = stage[6:8, 0:24]
    near = sums[8:16, pl.ds(pl.multiple_of(128 * ((96 * me) // 128), 128), 256)]
    g_fbias[...] = dot_exact(near, as_number(hot_back(256, 96, (96 * me) % 128)))[0:1]

    sent(4)
    sent(5)
    mix_copy.wait_send()
    half_copy.wait_send()
    wait_boxes(actw_in, s_act)
    wait_boxes(late, s_late)
    token_copy.wait()
    for i in range(4):
        rows = pl.ds(256 * (i % 2), 256)
        pltpu.make_async_copy(nlow.at[pl.ds(256 * i, 256)], hidden_hbm.at[i // 2, rows], s_hid.at[i]).wait()


def hot_back(rows, columns, shift):
    row = lax.broadcasted_iota(jnp.int32, (rows, columns), 0)
    column = lax.broadcasted_iota(jnp.int32, (rows, columns), 1)
    return row == column + shift


def dot_exact(a, b, dims=((1,), (0,))):
    return lax.dot_general(a, b, (dims, ((), ())), preferred_element_type=F32, precision=HIGH)


def hand_over(*refs):
    n = len(refs) // 3
    here, there, held = refs[:n], refs[n : 2 * n], refs[2 * n : 3 * n]
    s_in, s_out = refs[3 * n :]
    parts = []
    for i in range(n):
        rows = here[i].shape[-2]
        cuts = range(0, rows, rows // 4) if rows == 512 else [0]
        for at in cuts:
            size = rows // len(cuts)
            where = (slice(None),) * (len(here[i].shape) - 2) + (pl.ds(at, size),)
            parts.append([ref[i].at[where] for ref in (here, held, there)])
    loads = [pltpu.make_async_copy(p[0], p[1], s_in.at[k]) for k, p in enumerate(parts)]
    stores = [pltpu.make_async_copy(p[1], p[2], s_out.at[k]) for k, p in enumerate(parts)]
    for load in loads:
        load.start()
    for load, store in zip(loads, stores):
        load.wait()
        store.start()
    for store in stores:
        store.wait()


def encoder_step(
    tokens, qkv_weight, proj_weight, ffn_in_weight, ffn_out_weight, bias_rows, ffn_bias, norm_gains, buckets, padding, dropout
):
    def vm(*shape):
        return pltpu.VMEM(shape, BF)

    def vf(*shape):
        return pltpu.VMEM(shape, F32)

    def sems(*shape):
        return pltpu.SemaphoreType.DMA(shape)

    one = pltpu.SemaphoreType.DMA
    inside = pl.BlockSpec(memory_space=pltpu.VMEM)
    anywhere = pl.BlockSpec(memory_space=pl.ANY)
    engine = [sems(7, 4)] * 6 + [sems(4)]
    out = pl.pallas_call(
        encoder_kernel,
        name="encoder_step",
        out_shape=[
            jax.ShapeDtypeStruct((2, 512, 768), BF),
            jax.ShapeDtypeStruct((1, 1), F32),
            jax.ShapeDtypeStruct((512, 768), F32),
            jax.ShapeDtypeStruct((24, 2304), F32),
            jax.ShapeDtypeStruct((24, 768), F32),
            jax.ShapeDtypeStruct((24, 3072), F32),
            jax.ShapeDtypeStruct((96, 768), F32),
            jax.ShapeDtypeStruct((6, 24), F32),
            jax.ShapeDtypeStruct((1, 96), F32),
            jax.ShapeDtypeStruct((2, 24), F32),
        ],
        in_specs=[inside] * 10 + [anywhere],
        out_specs=[anywhere, inside, anywhere] + [inside] * 7,
        scratch_shapes=[
            vm(768, PW), vm(768, 3072), vm(3072, 768),
            vm(4, 2, 2, 16, WIDE + SW), vm(4, 2, 2, 16, WIDE), vm(4, 2, 2, 16, WIDE),
            vm(8, 4, 16, 768), vm(8, 4, 16, 768), vm(8, 4, 16, 1536), vm(8, 4, 16, 768),
            vm(8, 4, 16, SW), vf(16, SW), vf(16, 3328),
            pltpu.VMEM((2, 512, 768), jnp.int32), vm(512, 2304), vf(512, 512), vm(512, 768),
            vf(2, 512, 768), vm(1024, 768), vm(1024, 3072),
            vf(120, 768), vf(8, 512), vm(8, 512), vf(16, 3072), vm(16, 3200), vf(96, 512),
            vm(208, 512), vm(208, 768), vf(128, 768), vf(768, 128), vf(256, 768), vf(256, 768), vf(16, 3328),
            vm(32, 32, 128), vm(32, 32, 128), vm(32, 32, 128), vm(32, 32, 128), vm(32, 16, 256),
            vf(512, 768), vm(768, 512), vm(512, 256),
            vm(512, 32), vm(512, 32), vm(512, 32), vf(32, 128), vm(512, 1536), vm(512, 32), vf(32, 1536), vf(32, 1536),
        ] + engine + engine + [one] * 6 + [sems(2), sems(4)] + [one] * 5,
        compiler_params=pltpu.CompilerParams(
            collective_id=0, has_side_effects=True, vmem_limit_bytes=63 * 2**20
        ),
    )(
        qkv_weight, proj_weight, ffn_in_weight, ffn_out_weight, bias_rows, norm_gains,
        ffn_bias[None], tokens, buckets, padding[None], dropout,
    )
    out = pl.pallas_call(
        hand_over,
        name="hand_over",
        out_shape=[jax.ShapeDtypeStruct(o.shape, o.dtype) for o in out],
        in_specs=[anywhere] * 10,
        out_specs=[anywhere] * 10,
        scratch_shapes=[pltpu.VMEM(o.shape, o.dtype) for o in out] + [sems(16), sems(16)],
        compiler_params=pltpu.CompilerParams(vmem_limit_bytes=60 * 2**20),
    )(*out)
    hidden, loss, gtok, g_qkv, g_proj, g_in, g_out, g_bias, g_fbias, g_gain = out
    return (hidden, loss[0, 0], gtok, g_qkv, g_proj, g_in, g_out, g_bias, g_fbias[0], g_gain)


def solution(mesh):
    in_specs = (
        P(AXES, None),
        P(AXES, None),
        P(AXES, None),
        P(AXES, None),
        P(AXES, None),
        P(None, AXES),
        P(AXES),
        P(None, AXES),
        P(AXES, None),
        P(AXES),
        P(None, None, AXES, None),
    )
    out_specs = (
        P(None, AXES, None),
        P(),
        P(AXES, None),
        P(AXES, None),
        P(AXES, None),
        P(AXES, None),
        P(AXES, None),
        P(None, AXES),
        P(AXES),
        P(None, AXES),
    )
    grid_fits = mesh.shape["dp"] == 8 and mesh.shape["fsdp"] == 4
    return jax.shard_map(
        encoder_step if grid_fits else with_collectives, mesh=mesh, in_specs=in_specs, out_specs=out_specs, check_vma=False
    )
```

```python
import functools

import jax
import jax.numpy as jnp
from jax import lax
from jax.experimental import pallas as pl
from jax.experimental.pallas import tpu as pltpu
from jax.sharding import PartitionSpec as P

H = 12
HD = 64

NEGATIVE = -1e30
NORM_EPSILON = 1e-12
UNIT_EPSILON = 1e-06
SOFTMAX_TEMP = 0.05
KEEP_SCALE = 1.0 / 0.9
FULL_PRECISION = lax.Precision.HIGHEST
AXES = ("dp", "fsdp")
BF = jnp.bfloat16
F32 = jnp.float32


def dot(a, b, dims=((1,), (0,))):
    return lax.dot_general(a, b, (dims, ((), ())), preferred_element_type=F32)


def layer_norm(inputs, gain_vec, shift_vec):
    centre = inputs - jnp.mean(inputs, axis=-1, keepdims=True)
    spread = jnp.mean(centre * centre, axis=-1, keepdims=True)
    return centre * lax.rsqrt(spread + NORM_EPSILON) * gain_vec + shift_vec


def normalize(inputs):
    return inputs * lax.rsqrt(jnp.sum(inputs * inputs, axis=-1, keepdims=True) + UNIT_EPSILON)


def exact_gelu(inputs):
    return jax.nn.gelu(inputs, approximate=False)


def sentence_layout(bucket_row, pad_row, rows_here):
    row_ids = jnp.arange(rows_here, dtype=jnp.int32)
    starts = jnp.cumsum(bucket_row) - bucket_row
    used = bucket_row > 0
    member = (row_ids[:, None] >= starts[None, :]) & used[None, :]
    sentence = jnp.sum(member.astype(jnp.int32), axis=1)
    allowed = (sentence[:, None] == sentence[None, :]) & (pad_row[None, :] > 0)
    select = ((row_ids[None, :] == starts[:, None]) & used[:, None]).astype(jnp.float32)
    slot_allowed = (
        (sentence[None, :] == jnp.arange(1, bucket_row.shape[0] + 1)[:, None])
        & used[:, None]
        & (pad_row[None, :] > 0)
    )
    return (allowed, select, slot_allowed)


def gather(x, axis=0):
    return lax.all_gather(x, AXES, axis=axis, tiled=True)


def all_to_all(x):
    return lax.all_to_all(x, AXES, split_axis=0, concat_axis=0, tiled=True)


def with_collectives(
    tokens,
    qkv_weight,
    proj_weight,
    ffn_in_weight,
    ffn_out_weight,
    bias_rows,
    ffn_bias,
    norm_gains,
    buckets,
    padding,
    dropout,
):
    rows_here, width = tokens.shape
    slots = buckets.shape[1]
    hidden = ffn_in_weight.shape[1]
    small = bias_rows.shape[1]
    devices = width // small
    hidden_small = hidden // devices
    me = lax.axis_index(AXES)
    score_scale = HD ** (-0.5)
    used_slot = (buckets[0] > 0).astype(BF)

    params = jnp.concatenate(
        [bias_rows.reshape(-1), norm_gains.reshape(-1), ffn_bias, used_slot]
    )
    params_all = gather(params[None])
    qp = gather(jnp.concatenate([qkv_weight, proj_weight], axis=1))
    qkv_full, proj_full = qp[:, : 3 * width], qp[:, 3 * width :]
    in_full = gather(ffn_in_weight)
    out_full = gather(ffn_out_weight)
    rows8 = params_all[:, : 8 * small].reshape(devices, 8, small).transpose(1, 0, 2)
    rows8 = rows8.reshape(8, width).astype(F32)
    bias_f, gain_f = rows8[:6], rows8[6:]
    ffn_bias_f = params_all[:, 8 * small : 8 * small + hidden_small].reshape(-1).astype(F32)
    used_all = params_all[:, 8 * small + hidden_small :].reshape(-1)

    allowed, select, slot_allowed = sentence_layout(buckets[0], padding, rows_here)
    select_low = select.astype(BF)
    zero_row = jnp.zeros((width,), F32)
    qkv = (dot(tokens, qkv_full) + jnp.concatenate([bias_f[0], zero_row, bias_f[1]])).astype(BF)
    head_view = qkv.reshape(rows_here, 3, H, HD)
    queries, key_rows, value_rows = (head_view[:, 0], head_view[:, 1], head_view[:, 2])

    scores = (
        jnp.einsum("qhd,khd->hqk", queries, key_rows, preferred_element_type=F32) * score_scale
    )
    scores = jnp.where(allowed[None], scores, NEGATIVE)
    exp_scores = jnp.exp(scores - jnp.max(scores, axis=-1, keepdims=True))
    probability = (exp_scores / jnp.sum(exp_scores, axis=-1, keepdims=True)).astype(BF)
    context = jnp.einsum("hqk,khd->qhd", probability, value_rows, preferred_element_type=F32)
    context = context.reshape(rows_here, width).astype(BF)
    branch = dot(context, proj_full) + bias_f[2]
    keep_mask = dropout.astype(F32)
    mixed_one = tokens.astype(F32)[None] + branch[None] * keep_mask[:, 0] * KEEP_SCALE
    normed = layer_norm(mixed_one, gain_f[0], bias_f[3])
    normed_low = normed.astype(BF)
    preact = dot(normed_low.reshape(-1, width), in_full) + ffn_bias_f
    activation = exact_gelu(preact).astype(BF)
    ffn_out = (dot(activation, out_full) + bias_f[4]).reshape(normed.shape)
    mixed_two = normed + ffn_out * keep_mask[:, 1] * KEEP_SCALE
    hidden_out = layer_norm(mixed_two, gain_f[1], bias_f[5]).astype(BF)

    tokens_s = dot(select_low, tokens)
    qkv_s = dot(select_low, qkv).astype(BF)
    queries_s = qkv_s[:, :width].reshape(slots, H, HD)
    scores_s = (
        jnp.einsum("shd,khd->hsk", queries_s, key_rows, preferred_element_type=F32) * score_scale
    )
    scores_s = jnp.where(slot_allowed[None], scores_s, NEGATIVE)
    peak_s = jnp.max(scores_s, axis=-1, keepdims=True)
    exp_s = jnp.exp(scores_s - peak_s) * slot_allowed[None].astype(F32)
    probability_f = exp_s / jnp.maximum(jnp.sum(exp_s, axis=-1, keepdims=True), 1e-30)
    probability_s = probability_f.astype(BF)
    context_s = dot(select_low, context).astype(BF)
    branch_s = dot(context_s, proj_full) + bias_f[2]
    keep_s = jnp.einsum(
        "sr,vbrd->vbsd", select_low, dropout.astype(BF), preferred_element_type=F32
    )
    mixed_s = tokens_s[None] + branch_s[None] * keep_s[:, 0] * KEEP_SCALE
    normed_s, first_back = jax.vjp(layer_norm, mixed_s, gain_f[0], bias_f[3])
    normed_s_low = normed_s.astype(BF).reshape(2 * slots, width)
    preact_s = dot(normed_s_low, in_full) + ffn_bias_f
    activation_sf, gelu_back = jax.vjp(exact_gelu, preact_s)
    activation_s = activation_sf.astype(BF)
    ffn_out_s = (dot(activation_s, out_full) + bias_f[4]).reshape(normed_s.shape)
    mixed_two_s = normed_s + ffn_out_s * keep_s[:, 1] * KEEP_SCALE
    final_s, second_back = jax.vjp(layer_norm, mixed_two_s, gain_f[1], bias_f[5])
    used_f = used_slot.astype(F32)
    final_s = final_s * used_f[None, :, None]
    unit_s, unit_back = jax.vjp(normalize, final_s)
    unit_low = unit_s.astype(BF)

    unit_all = gather(unit_low.reshape(1, 2, slots, width))
    unit_0 = unit_all[:, 0].reshape(-1, width)
    unit_1 = unit_all[:, 1].reshape(-1, width)
    logits = dot(unit_0, unit_1, ((1,), (1,))) / SOFTMAX_TEMP
    logits = jnp.where(used_all[None, :] > 0, logits, NEGATIVE)
    total = unit_0.shape[0]
    ids = jnp.arange(total, dtype=jnp.int32)
    diagonal = ids[:, None] == ids[None, :]
    logit_peak = jnp.max(logits, axis=-1, keepdims=True)
    logit_total = logit_peak[:, 0] + jnp.log(jnp.sum(jnp.exp(logits - logit_peak), axis=-1))
    positive = jnp.sum(jnp.where(diagonal, logits, 0.0), axis=1)
    used_all_f = used_all.astype(F32)
    loss_mean = jnp.sum((logit_total - positive) * used_all_f) / jnp.sum(used_all_f)
    soft = jnp.exp(logits - logit_total[:, None])
    logit_gradient = ((soft - diagonal.astype(F32)) * used_all_f[:, None]).astype(BF)
    mine_rows = lax.dynamic_slice_in_dim(logit_gradient, me * slots, slots, 0)
    mine_columns = lax.dynamic_slice_in_dim(logit_gradient, me * slots, slots, 1)
    grad_unit = jnp.stack(
        [dot(mine_rows, unit_1), dot(mine_columns, unit_0, ((0,), (0,)))]
    ) / SOFTMAX_TEMP
    (grad_final,) = unit_back(grad_unit)
    grad_final = grad_final * used_f[None, :, None]
    grad_mixed_two, grad_gain_two, grad_shift_two = second_back(grad_final)
    grad_ffn = (grad_mixed_two * keep_s[:, 1] * KEEP_SCALE).astype(BF).reshape(-1, width)
    grad_shift_out = jnp.sum(grad_ffn.astype(F32), axis=0)
    grad_act = dot(grad_ffn, out_full, ((1,), (1,)))
    (grad_preact_f,) = gelu_back(grad_act)
    grad_preact = grad_preact_f.astype(BF)
    grad_hidden_bias = jnp.sum(grad_preact.astype(F32), axis=0)
    grad_normed = dot(grad_preact, in_full, ((1,), (1,))).reshape(normed_s.shape) + grad_mixed_two
    grad_mixed, grad_gain_one, grad_shift_one = first_back(grad_normed)
    grad_branch = jnp.sum(grad_mixed * keep_s[:, 0] * KEEP_SCALE, axis=0).astype(BF)
    grad_shift_proj = jnp.sum(grad_branch.astype(F32), axis=0)
    grad_context = dot(grad_branch, proj_full, ((1,), (1,))).astype(BF)
    grad_context_h = grad_context.reshape(slots, H, HD)
    grad_probs = jnp.einsum(
        "shd,khd->hsk", grad_context_h, value_rows, preferred_element_type=F32
    )
    inner = jnp.sum(probability_f * grad_probs, axis=-1, keepdims=True)
    grad_scores = (probability_f * (grad_probs - inner)).astype(BF)
    grad_queries = (
        (jnp.einsum("hsk,khd->shd", grad_scores, key_rows, preferred_element_type=F32) * score_scale)
        .reshape(slots, width)
        .astype(BF)
    )
    pairs = jnp.concatenate([grad_scores, probability_s], axis=0).reshape(2 * H * slots, rows_here)
    token_sums = dot(pairs, tokens).astype(BF)
    key_factor = (queries_s.astype(F32) * score_scale).astype(BF)
    back_w = qkv_full.reshape(width, 3, H, HD)
    through = jnp.concatenate(
        [
            jnp.einsum("shd,whd->hsw", key_factor, back_w[:, 1], preferred_element_type=F32),
            jnp.einsum("shd,whd->hsw", grad_context_h, back_w[:, 2], preferred_element_type=F32),
        ],
        axis=0,
    ).reshape(2 * H * slots, width)
    start_grad = jnp.sum(grad_mixed, axis=0) + dot(
        grad_queries, qkv_full[:, :width], ((1,), (1,))
    )
    grad_tokens = dot(pairs, through.astype(BF), ((0,), (0,))) + lax.dot_general(
        select, start_grad, (((0,), (0,)), ((), ())), precision=FULL_PRECISION
    )
    value_sum = jnp.sum(probability_s.astype(F32), axis=-1).T
    grad_shift_value = jnp.sum(value_sum[:, :, None] * grad_context_h.astype(F32), axis=0).reshape(-1)
    grad_shift_query = jnp.sum(grad_queries.astype(F32), axis=0)

    wide = gather(jnp.concatenate([grad_ffn, grad_preact], axis=1))
    gffn_all, gpre_all = wide[:, :width], wide[:, width:]
    narrow = gather(
        jnp.concatenate([grad_branch, key_factor.reshape(slots, width), grad_context, grad_queries], axis=1)
    )
    gbranch_all = narrow[:, :width]
    key_all = narrow[:, width : 2 * width].reshape(-1, H, HD)
    gctx_all = narrow[:, 2 * width : 3 * width].reshape(-1, H, HD)
    gq_all = narrow[:, 3 * width :]

    def cut(x, n):
        return x.reshape(x.shape[0], devices, n).transpose(1, 0, 2).reshape(devices, -1)

    bias_sums = jnp.concatenate(
        [
            jnp.stack(
                [
                    grad_shift_query,
                    grad_shift_value,
                    grad_shift_proj,
                    grad_shift_one,
                    grad_shift_out,
                    grad_shift_two,
                    grad_gain_one,
                    grad_gain_two,
                ]
            )
            .reshape(8, devices, small)
            .transpose(1, 0, 2)
            .reshape(devices, -1),
            grad_hidden_bias.reshape(devices, -1),
        ],
        axis=1,
    )
    high = bias_sums.astype(BF)
    lower = (bias_sums - high.astype(F32)).astype(BF)
    pieces = [
        cut(activation_s, hidden_small),
        cut(normed_s_low, small),
        cut(context_s, small),
        cut(tokens_s.astype(BF), small),
        cut(token_sums, small),
        high,
        lower,
    ]
    sizes = [p.shape[1] for p in pieces]
    received = all_to_all(jnp.concatenate(pieces, axis=1))
    ends = []
    at = 0
    for n in sizes:
        ends.append(received[:, at : at + n])
        at += n
    act_r = ends[0].reshape(-1, hidden_small)
    normed_r = ends[1].reshape(-1, small)
    ctx_r = ends[2].reshape(-1, small)
    tok_r = ends[3].reshape(-1, small)
    sums_r = ends[4].reshape(devices, 2, H, slots, small)
    bias_r = jnp.sum(ends[5].astype(F32) + ends[6].astype(F32), axis=0)

    grad_out_weight = dot(act_r, gffn_all, ((0,), (0,)))
    grad_in_weight = dot(normed_r, gpre_all, ((0,), (0,)))
    grad_proj = dot(ctx_r, gbranch_all, ((0,), (0,)))
    grad_q = dot(tok_r, gq_all, ((0,), (0,)))
    keys_r = sums_r[:, 0].transpose(1, 0, 2, 3).reshape(H, -1, small)
    values_r = sums_r[:, 1].transpose(1, 0, 2, 3).reshape(H, -1, small)
    grad_k = jnp.einsum("hnw,nhd->whd", keys_r, key_all, preferred_element_type=F32)
    grad_v = jnp.einsum("hnw,nhd->whd", values_r, gctx_all, preferred_element_type=F32)
    grad_qkv_weight = jnp.concatenate(
        [grad_q, grad_k.reshape(small, width), grad_v.reshape(small, width)], axis=1
    )
    bias8 = bias_r[: 8 * small].reshape(8, small)
    return (
        hidden_out,
        loss_mean,
        grad_tokens,
        grad_qkv_weight,
        grad_proj,
        grad_in_weight,
        grad_out_weight,
        bias8[:6],
        bias_r[8 * small :],
        bias8[6:],
    )


MESH = pl.DeviceIdType.MESH
PW, QW, SW = 3072, 1536, 256
WIDE = PW + QW
HIGH = lax.Precision.HIGHEST
LAST = ((1,), (1,))
FIRST = ((0,), (0,))
WHOLE = (WIDE + SW, WIDE, WIDE, 768, 768, 1536, 768)


def place():
    dp = lax.axis_index("dp")
    fs = lax.axis_index("fsdp")
    return dp // 2, dp % 2, fs // 2, fs % 2


def peer_z(z, r):
    return (z + r) % 2 + 2 * ((z // 2 + r // 2) % 2)


def hot(rows, columns, shift):
    row = lax.broadcasted_iota(jnp.int32, (rows, columns), 0)
    column = lax.broadcasted_iota(jnp.int32, (rows, columns), 1)
    return row + shift == column


def as_number(flags):
    return jnp.where(flags, 1.0, 0.0)


def tail_of(x):
    t = 1.0 / (1.0 + (0.3275911 * 0.7071067811865476) * jnp.abs(x))
    bell = jnp.exp(x * x * -0.5)
    poly = 0.5 * 1.061405429
    for c in (-1.453152027, 1.421413741, -0.284496736, 0.254829592):
        poly = poly * t + 0.5 * c
    return poly * t * bell, bell


def gelu(x):
    tail, _ = tail_of(x)
    return jnp.maximum(x, 0.0) - jnp.abs(x) * tail


def gelu_slope(x):
    tail, bell = tail_of(x)
    return jnp.where(x >= 0.0, 1.0 - tail, tail) + x * bell * 0.3989422804014327


def mean(x):
    return jnp.sum(x, axis=-1, keepdims=True) * (1.0 / x.shape[-1])


def standardize(x):
    centre = x - mean(x)
    scale = lax.rsqrt(mean(centre * centre) + NORM_EPSILON)
    return centre * scale, scale


def norm_back(grad_hat, hat, scale):
    return scale * (grad_hat - mean(grad_hat) - hat * mean(grad_hat * hat))


def encoder_kernel(
    qkv_ref, proj_ref, in_ref, out_hbm, bias_ref, gain_ref, fbias_ref, tokens_hbm, buckets_ref, pad_ref, drop_hbm,
    hidden_hbm, loss_ref, gtok_hbm, g_qkv, g_proj, g_in_hbm, g_out_hbm, g_bias, g_fbias, g_gain,
    wqp, win, wout, l0, l1, l2, f3, f4, f5, f6, pb, stage, par,
    drop, qkv, madd, ctx, normed, nlow, act,
    cls, sm8, sel, pre_s, acts, p_f, pairs, through, mixer, mixer_t, unit0, unit1, sums,
    early, early_in, late, late_in, actw_in, gtok, keys_t, values1, mix_n, mix_c, mix_t, rest, slope, mix_o, half_s, half_r, tokens, out_ref, g_in, g_out,
    sz, sx, sy, sa, sb, sc, scp, rz, rx, ry, ra, rb, rc, rcp, s_early, r_early, s_act, r_act, s_late, r_late, s_drop, s_hid, s_tok, s_mix, r_mix, s_half, r_half, s_own,
):
    z, c, y, x = place()
    me = 8 * z + 4 * c + 2 * y + x
    land = (l0, l1, l2)
    full = (f3, f4, f5, f6)
    weights = (wqp, win, wout)
    lanes = functools.partial(lax.broadcasted_iota, jnp.int32)

    def dev(z_, c_, y_, x_):
        return (2 * z_ + c_, 2 * y_ + x_)

    def other(i):
        t = (me + i) % 32
        return t, (t // 4, t % 4)

    def loop(lo, hi, body):
        def step(i, carry):
            body(i)
            return carry

        lax.fori_loop(lo, hi, step, 0)

    bar = pltpu.get_barrier_semaphore()

    def greet(i):
        _, device = other(i)
        pl.semaphore_signal(bar, inc=1, device_id=device, device_id_type=MESH)

    loop(1, 32, greet)
    out_copy = pltpu.make_async_copy(out_hbm, out_ref, s_own.at[0])
    out_copy.start()
    tokens_copy = pltpu.make_async_copy(tokens_hbm, tokens, s_own.at[1])
    tokens_copy.start()
    drop_copy = pltpu.make_async_copy(drop_hbm.at[:, 0], drop, s_drop.at[0])
    drop_copy.start()

    def slot(ph, zz, yy, xx):
        if ph < 3:
            return land[ph].at[zz, yy, xx]
        return full[ph - 3].at[2 * zz + c, 2 * yy + xx]

    def rcopy(ref, s, r, device):
        return pltpu.make_async_remote_copy(
            src_ref=ref, dst_ref=ref, send_sem=s, recv_sem=r, device_id=device, device_id_type=MESH
        )

    def cp_z(ph, r):
        return rcopy(slot(ph, z, y, x), sz.at[ph, r], rz.at[ph, r], dev(peer_z(z, r), c, y, x))

    def cp_x(ph, r):
        return rcopy(slot(ph, peer_z(z, r), y, x), sx.at[ph, r], rx.at[ph, r], dev(z, c, y, 1 - x))

    def cp_y(ph, r):
        return rcopy(slot(ph, peer_z(z, r), y, x), sy.at[ph, r], ry.at[ph, r], dev(z, c, 1 - y, x))

    def half(ph):
        return WHOLE[ph] // 256 * 128

    def cp_a(ph, r):
        ref = slot(ph, peer_z(z, r), y, 1 - x).at[:, 0 : half(ph)]
        return rcopy(ref, sa.at[ph, r], ra.at[ph, r], dev(z, c, 1 - y, x))

    def cp_b(ph, r):
        ref = slot(ph, peer_z(z, r), 1 - y, x).at[:, half(ph) : WHOLE[ph]]
        return rcopy(ref, sb.at[ph, r], rb.at[ph, r], dev(z, c, y, 1 - x))

    def cp_c(ph, r):
        group = 2 * peer_z(z, r) + c
        if ph < 3:
            n = 384 if ph == 2 else 96
            ref = weights[ph].at[pl.ds(pl.multiple_of(n * group, n), n)]
        else:
            ref = full[ph - 3].at[group]
        return rcopy(ref, sc.at[ph, r], rc.at[ph, r], dev(z, 1 - c, y, x))

    def cp_cp(r):
        return rcopy(pb.at[2 * peer_z(z, r) + c], scp.at[r], rcp.at[r], dev(z, 1 - c, y, x))

    def start_z(ph):
        loop(1, 4, lambda r: cp_z(ph, r).start())

    def start_xy(ph, r):
        cp_x(ph, r).start()
        cp_y(ph, r).start()

    def wait_z_start_xy(ph, r):
        cp_z(ph, r).wait_recv()
        start_xy(ph, r)

    def wait_xy_start_ab(ph, r):
        cp_x(ph, r).wait_recv()
        cp_a(ph, r).start()
        cp_y(ph, r).wait_recv()
        cp_b(ph, r).start()

    def merge(ph, r):
        zz = peer_z(z, r)
        group = 2 * zz + c
        if ph == 2:
            for yy in range(2):
                for xx in range(2):
                    base = 384 * group + 96 * (2 * yy + xx)
                    for j in range(6):
                        wout[pl.ds(pl.multiple_of(base + 16 * j, 16), 16), :] = l2[
                            zz, yy, xx, :, 768 * j : 768 * (j + 1)
                        ]
            return
        w = weights[ph]
        l = land[ph]
        spans = [(0, 2304, PW), (2304, 768, PW + 1152)] if ph == 0 else [(0, 3072, PW)]
        for yy in range(2):
            base = 96 * group + 48 * yy
            w[pl.ds(pl.multiple_of(base, 16), 16), :] = l[zz, yy, 0, :, 0:PW]
            w[pl.ds(pl.multiple_of(base + 32, 16), 16), :] = l[zz, yy, 1, :, 0:PW]
            middle = pl.ds(pl.multiple_of(base + 16, 16), 16)
            for at, n, qat in spans:
                qe = l[zz, yy, 0, :, qat : qat + n // 2].astype(F32)
                qo = l[zz, yy, 1, :, qat : qat + n // 2].astype(F32)
                w[middle, at : at + n // 2] = jnp.concatenate([qe[0:8], qo[0:8]], axis=0).astype(BF)
                w[middle, at + n // 2 : at + n] = jnp.concatenate([qe[8:16], qo[8:16]], axis=0).astype(BF)
        if ph == 0:
            for yy in range(2):
                for xx in range(2):
                    pb[group, 2 * yy + xx] = l0[zz, yy, xx, :, WIDE:]

    def wait_ab_start_c(ph, r):
        cp_a(ph, r).wait_recv()
        cp_b(ph, r).wait_recv()
        if ph < 3:
            merge(ph, r)
        cp_c(ph, r).start()
        if ph == 0:
            cp_cp(r).start()

    def wait_c(ph, r):
        cp_c(ph, r).wait_recv()
        if ph == 0:
            cp_cp(r).wait_recv()

    def pack(ph, parts):
        at, qat = 0, PW
        for ref in parts:
            v = ref[...].astype(F32)
            n = v.shape[1]
            p_rows = jnp.where(x == 0, v[0:16], v[8:24])
            q_rows = jnp.where(x == 0, v[16:24], v[0:8])
            land[ph][z, y, x, :, at : at + n] = p_rows.astype(BF)
            land[ph][z, y, x, :, qat : qat + n // 2] = jnp.concatenate(
                [q_rows[:, : n // 2], q_rows[:, n // 2 :]], axis=0
            ).astype(BF)
            at += n
            qat += n // 2

    pack(0, (qkv_ref, proj_ref))

    def put(v, shift):
        return dot(v.astype(BF), as_number(hot(v.shape[1], SW, shift)).astype(BF))

    bk = buckets_ref[...].astype(F32)
    stage[...] = jnp.zeros_like(stage)
    stage[0:6, :] = put(bias_ref[...], (24 * me) % 128)
    stage[6:8, :] = put(gain_ref[...], (24 * me) % 128)
    stage[8:9, :] = put(fbias_ref[...], (96 * me) % 128)
    stage[9:10, :] = put(as_number(bk > 0.0), (8 * me) % 128)
    l0[z, y, x, :, WIDE:] = stage[...].astype(BF)
    pl.semaphore_wait(bar, 31)

    start_z(0)
    start_xy(0, 0)
    pack(1, (in_ref,))
    out_copy.wait()
    for j in range(6):
        l2[z, y, x, :, 768 * j : 768 * (j + 1)] = out_ref[16 * j : 16 * (j + 1), :]

    start_xy(1, 0)

    row8, lane8 = lanes((8, 8), 0), lanes((8, 8), 1)
    bk_col = jnp.sum(jnp.where(row8 == lane8, bk, 0.0), axis=1, keepdims=True)
    starts_col = jnp.sum(jnp.where(lane8 < row8, bk, 0.0), axis=1, keepdims=True)
    starts_row = jnp.sum(jnp.where(row8 < lane8, bk_col, 0.0), axis=0, keepdims=True)
    used_mine = as_number(bk_col > 0.0)
    used16 = jnp.concatenate([used_mine, used_mine], axis=0)
    row_ids = lanes((512, 8), 0).astype(F32)
    column_ids = lanes((8, 512), 1).astype(F32)
    sent_row = jnp.sum(as_number((row_ids >= starts_row) & (bk > 0.0)), axis=1, keepdims=True)
    sent_col = jnp.sum(as_number((column_ids >= starts_col) & (bk_col > 0.0)), axis=0, keepdims=True)
    key_of = jnp.where(pad_ref[...] > 0, sent_col, 0.0)
    madd[...] = jnp.where(sent_row == key_of, 0.0, NEGATIVE)
    sm8[...] = as_number(key_of == (lanes((8, 512), 0) + 1).astype(F32))
    sel[...] = as_number((column_ids == starts_col) & (bk_col > 0.0)).astype(BF)

    wait_z_start_xy(0, 1)
    wait_xy_start_ab(0, 0)
    wait_z_start_xy(0, 2)
    wait_z_start_xy(0, 3)
    start_z(1)
    loop(1, 4, lambda r: wait_xy_start_ab(0, r))
    loop(1, 4, lambda r: wait_z_start_xy(1, r))
    start_z(2)
    start_xy(2, 0)
    loop(0, 4, lambda r: wait_ab_start_c(0, r))
    tokens_copy.wait()
    drop_copy.wait()
    loop(0, 4, lambda r: wait_c(0, r))
    par[...] = jnp.zeros_like(par)
    for d in range(32):
        w = pb[d // 4, d % 4].astype(F32)
        t, t2, t3 = 24 * d // 128, 96 * d // 128, 8 * d // 128
        par[0:8, 128 * t : 128 * t + 256] += w[0:8]
        par[8:9, 128 * t2 : 128 * t2 + 256] += w[8:9]
        par[9:10, 128 * t3 : 128 * t3 + 256] += w[9:10]

    def bias(i):
        return par[i : i + 1, 0:768]

    def gain(i):
        return par[6 + i : 7 + i, 0:768]

    def qkv_part(i):
        columns = pl.ds(pl.multiple_of(256 * i, 256), 256)
        inside = pl.ds(pl.multiple_of(256 * (i % 3), 256), 256)
        both = par[0:8, inside]
        part = jnp.where(i < 3, both[0:1], jnp.where(i < 6, 0.0, both[1:2]))
        qkv[:, columns] = (dot(tokens[...], wqp[:, columns]) + part).astype(BF)

    loop(0, 9, qkv_part)
    loop(0, 4, lambda r: wait_xy_start_ab(1, r))
    loop(1, 4, lambda r: wait_z_start_xy(2, r))

    left = lanes((1, 128), 1) < 64
    left_scale = jnp.where(left, HD**-0.5, 0.0)
    right_scale = jnp.where(left, 0.0, HD**-0.5)

    def turn_keys(i):
        columns = pl.ds(pl.multiple_of(768 + 128 * i, 128), 128)
        keys_t[pl.ds(pl.multiple_of(128 * i, 128), 128), :] = jnp.transpose(qkv[:, columns].astype(F32)).astype(BF)

    loop(0, 6, turn_keys)
    values1[:, 128:256] = jnp.ones((512, 128), BF)

    def attend(pair):
        def columns(part):
            return pl.ds(pl.multiple_of(768 * part + 128 * pair, 128), 128)

        values1[:, 0:128] = qkv[:, columns(2)]

        q = qkv[:, columns(0)].astype(F32)
        results = []
        for scale in (left_scale, right_scale):
            s = dot((q * scale).astype(BF), keys_t[columns(0), :]) + madd[...]
            e = jnp.exp(s - jnp.max(s, axis=-1, keepdims=True)).astype(BF)
            both = dot(e, values1[...])
            results.append(both[:, 0:128] * (1.0 / both[:, 128:256]))
        ctx[:, columns(0)] = jnp.where(left, results[0], results[1]).astype(BF)

    loop(0, 6, attend)
    wait_xy_start_ab(2, 0)

    def first_norm(i):
        rows = pl.ds(pl.multiple_of(128 * i, 128), 128)
        branch = (dot(ctx[rows, :], wqp[:, 2304:3072]) + bias(2)) * KEEP_SCALE
        token_rows = tokens[rows, :].astype(F32)
        for v in range(2):
            hat, _ = standardize(token_rows + branch * drop[v, rows, :].astype(F32))
            n = hat * gain(0) + bias(3)
            normed[v, rows, :] = n
            nlow[pl.ds(pl.multiple_of(512 * v + 128 * i, 128), 128), :] = n.astype(BF)

    loop(0, 4, first_norm)
    loop(0, 4, lambda r: wait_ab_start_c(1, r))
    wait_xy_start_ab(2, 1)

    TOK, QRY, CTX, KEEP1, KEEP2, HAT1, NRM, HAT2, FIN = 0, 8, 16, 24, 40, 56, 72, 88, 104
    pick = sel[...]
    cls[TOK : TOK + 8, :] = dot(pick, tokens[...])
    cls[QRY : QRY + 8, :] = dot(pick, qkv[:, 0:768]) * HD**-0.5
    cls[CTX : CTX + 8, :] = dot(pick, ctx[...])
    for v in range(2):
        cls[KEEP1 + 8 * v : KEEP1 + 8 * v + 8, :] = dot(pick, drop[v].astype(F32).astype(BF)) * KEEP_SCALE
    drop_copy = pltpu.make_async_copy(drop_hbm.at[:, 1], drop, s_drop.at[1])
    drop_copy.start()

    def twice(v):
        return jnp.concatenate([v, v], axis=0)

    head = lax.broadcasted_iota(jnp.int32, (12, 8, 768), 0) * 64
    lane = lax.broadcasted_iota(jnp.int32, (12, 8, 768), 2)
    own_head = (lane >= head) & (lane < head + 64)

    def spread(rows8):
        return jnp.where(own_head, rows8[None], 0.0).reshape(96, 768).astype(BF)

    def gathered(rows96):
        return jnp.sum(jnp.where(own_head, rows96.reshape(12, 8, 768), 0.0), axis=0)

    branch_s = dot(cls[CTX : CTX + 8, :].astype(BF), wqp[:, 2304:3072]) + bias(2)
    hat1, scale1 = standardize(twice(cls[TOK : TOK + 8, :]) + twice(branch_s) * cls[KEEP1 : KEEP1 + 16, :])
    normed_s = hat1 * gain(0) + bias(3)
    cls[HAT1 : HAT1 + 16, :] = hat1
    cls[NRM : NRM + 16, :] = normed_s
    f6[2 * z + c, 2 * y + x] = normed_s.astype(BF)
    start_z(6)
    query_big = spread(cls[QRY : QRY + 8, :])
    seen = jnp.broadcast_to(sm8[...][None], (12, 8, 512)).reshape(96, 512)
    s = jnp.where(seen > 0.0, dot(query_big, qkv[:, 768:1536], LAST), NEGATIVE)
    e = jnp.exp(s - jnp.max(s, axis=-1, keepdims=True)) * seen
    prob = e * (1.0 / jnp.maximum(jnp.sum(e, axis=-1, keepdims=True), 1e-30))
    p_f[...] = prob
    pairs[96:192, :] = prob.astype(BF)
    pairs[192:208, :] = twice(pick.astype(F32)).astype(BF)
    wait_xy_start_ab(2, 2)
    mixer[0:96, :] = dot(prob.astype(BF), tokens[...])
    mixer[96:104, :] = cls[CTX : CTX + 8, :]
    mixer[104:112, :] = cls[TOK : TOK + 8, :]
    mixer[112:128, :] = normed_s

    def send_mixer(box, box_in, s_sem, r_sem):
        mixer_t[...] = jnp.transpose(mixer[...])

        def cut(t):
            v = mixer_t[pl.ds(pl.multiple_of(24 * t, 8), 24), :]
            box[t] = jnp.concatenate([v, jnp.zeros((8, 128), F32)], axis=0).astype(BF)

        loop(0, 32, cut)
        box_in[me] = box[me]

        def send(i):
            t, device = other(i)
            pltpu.make_async_remote_copy(
                src_ref=box.at[t],
                dst_ref=box_in.at[me],
                send_sem=s_sem,
                recv_sem=r_sem,
                device_id=device,
                device_id_type=MESH,
            ).start()

        loop(1, 32, send)

    def wait_boxes(ref, sem):
        part = ref.at[pl.ds(0, 31)]
        pltpu.make_async_copy(part, part, sem).wait()

    send_mixer(early, early_in, s_early, r_early)

    loop(0, 4, lambda r: wait_c(1, r))

    def ffn_in(i):
        columns = pl.ds(pl.multiple_of(256 * i, 256), 256)
        act[:, columns] = gelu(dot(nlow[...], win[:, columns]) + par[8:9, columns]).astype(BF)

    loop(0, 2, ffn_in)
    wait_xy_start_ab(2, 3)
    start_xy(6, 0)
    loop(1, 4, lambda r: wait_z_start_xy(6, r))
    drop_copy.wait()
    for v in range(2):
        cls[KEEP2 + 8 * v : KEEP2 + 8 * v + 8, :] = dot(pick, drop[v].astype(F32).astype(BF)) * KEEP_SCALE
    preact_s = dot(cls[NRM : NRM + 16, :].astype(BF), win[...]) + par[8:9, 0:3072]
    pre_s[...] = preact_s
    acts[:, 0:3072] = gelu(preact_s).astype(BF)
    acts[:, 3072:3200] = jnp.zeros((16, 128), BF)

    def window(t):
        return acts.at[:, pl.ds(pl.multiple_of(128 * ((96 * t) // 128), 128), 256)]

    def send_act(i):
        t, device = other(i)
        pltpu.make_async_remote_copy(
            src_ref=window(t),
            dst_ref=actw_in.at[me],
            send_sem=s_act,
            recv_sem=r_act,
            device_id=device,
            device_id_type=MESH,
        ).start()

    loop(1, 32, send_act)
    actw_in[me] = window(me)[...]

    loop(2, 5, ffn_in)

    column32 = lanes((16, 32), 1)
    first8 = lanes((16, 32), 0) < 8
    ones8 = as_number(first8 & (column32 == 24))

    def turn_early(i):
        for d in range(4):
            m = jnp.transpose(early_in[4 * i + d].astype(F32))
            rows16 = pl.ds(pl.multiple_of(64 * i + 16 * d, 16), 16)
            empty = jnp.zeros((8, 32), F32)
            mix_c[rows16, :] = (jnp.concatenate([m[96:104], empty], axis=0) + ones8).astype(BF)
            mix_t[rows16, :] = (jnp.concatenate([m[104:112], empty], axis=0) + ones8).astype(BF)
            mix_n[rows16, :] = (m[112:128] + as_number(column32 == 24)).astype(BF)

    mix_copy = pltpu.make_async_remote_copy(
        src_ref=mix_n,
        dst_ref=mix_o,
        send_sem=s_mix,
        recv_sem=r_mix,
        device_id=dev(z, 1 - c, y, x),
        device_id_type=MESH,
    )
    half_copy = pltpu.make_async_remote_copy(
        src_ref=half_s,
        dst_ref=half_r,
        send_sem=s_half,
        recv_sem=r_half,
        device_id=dev(z, 1 - c, y, x),
        device_id_type=MESH,
    )

    def turn_all_early():
        loop(0, 8, turn_early)
        mix_copy.start()

    loop(0, 4, lambda r: wait_ab_start_c(2, r))
    loop(0, 4, lambda r: wait_c(2, r))
    keep2 = cls[KEEP2 : KEEP2 + 16, :]
    ffn_s = dot(acts[:, 0:3072], wout[...]) + bias(4)
    hat2, scale2 = standardize(cls[NRM : NRM + 16, :] + ffn_s * keep2)
    final_s = (hat2 * gain(1) + bias(5)) * used16
    length = lax.rsqrt(jnp.sum(final_s * final_s, axis=-1, keepdims=True) + UNIT_EPSILON)
    cls[HAT2 : HAT2 + 16, :] = hat2
    cls[FIN : FIN + 16, :] = final_s
    f3[2 * z + c, 2 * y + x] = (final_s * length).astype(BF)
    start_z(3)
    start_xy(3, 0)

    def ffn_out(i):
        v = i // 2
        rows = pl.ds(pl.multiple_of(256 * (i % 2), 256), 256)
        flat = pl.ds(pl.multiple_of(256 * i, 256), 256)
        out = dot(act[flat, :], wout[...]) + bias(4)
        hat, _ = standardize(normed[v, rows, :] + out * (drop[v, rows, :].astype(F32) * KEEP_SCALE))
        nlow[flat, :] = (hat * gain(1) + bias(5)).astype(BF)
        pltpu.make_async_copy(nlow.at[flat], hidden_hbm.at[v, rows], s_hid.at[i]).start()

    wait_boxes(early_in, r_early)
    turn_all_early()
    loop(5, 7, ffn_in)
    loop(1, 4, lambda r: wait_z_start_xy(3, r))
    loop(0, 4, lambda r: wait_xy_start_ab(6, r))
    loop(7, 9, ffn_in)
    loop(0, 4, lambda r: wait_xy_start_ab(3, r))
    loop(0, 4, lambda r: wait_ab_start_c(6, r))
    loop(9, 11, ffn_in)
    loop(0, 4, lambda r: wait_ab_start_c(3, r))
    loop(0, 4, lambda r: wait_c(6, r))

    def slopes(i):
        columns = pl.ds(pl.multiple_of(1536 * c + 512 * i, 512), 512)
        preact = dot(f6[...].reshape(512, 768), win[:, columns]) + par[8:9, columns]
        slope[:, pl.ds(pl.multiple_of(512 * i, 512), 512)] = gelu_slope(preact).astype(BF)

    slopes(0)
    loop(0, 4, lambda r: wait_c(3, r))

    def sent(ph):
        def of(r):
            for copy in (cp_x, cp_y, cp_a, cp_b, cp_c):
                copy(ph, r).wait_send()
            if ph == 0:
                cp_cp(r).wait_send()

        def to_peers(r):
            of(r)
            cp_z(ph, r).wait_send()

        of(0)
        loop(1, 4, to_peers)

    def part_units(i):
        v = f3[i // 4, i % 4].astype(F32)
        rows = pl.ds(pl.multiple_of(8 * i, 8), 8)
        unit0[rows, :] = v[0:8]
        unit1[rows, :] = v[8:16]

    loop(0, 32, part_units)
    u0, u1 = unit0[...].astype(BF), unit1[...].astype(BF)
    mine = pl.ds(pl.multiple_of(8 * me, 8), 8)
    u0_mine, u1_mine = unit0[mine, :].astype(BF), unit1[mine, :].astype(BF)
    used_row = par[9:10, 0:256]
    eye = hot(256, 256, 0)
    used_col = jnp.sum(jnp.where(eye, used_row, 0.0), axis=1, keepdims=True)
    by_column = jnp.where(used_col > 0.0, dot(u1, u0, LAST) * (1.0 / SOFTMAX_TEMP), NEGATIVE)
    peak = jnp.max(by_column, axis=0, keepdims=True)
    total = peak + jnp.log(jnp.sum(jnp.exp(by_column - peak), axis=0, keepdims=True))
    positive = jnp.sum(jnp.where(eye, by_column, 0.0), axis=0, keepdims=True)
    loss_sum = jnp.sum((total - positive) * used_row, axis=1, keepdims=True)
    loss_ref[...] = loss_sum / jnp.sum(used_row, axis=1, keepdims=True)
    target = as_number(hot(8, 256, 8 * me))
    mine_1 = jnp.where(used_mine > 0.0, dot(u1_mine, u0, LAST) * (1.0 / SOFTMAX_TEMP), NEGATIVE)
    grad_1 = ((jnp.exp(mine_1 - total) - target) * used_row).astype(BF)
    mine_0 = jnp.where(used_row > 0.0, dot(u0_mine, u1, LAST) * (1.0 / SOFTMAX_TEMP), NEGATIVE)
    peak_0 = jnp.max(mine_0, axis=1, keepdims=True)
    total_0 = peak_0 + jnp.log(jnp.sum(jnp.exp(mine_0 - peak_0), axis=1, keepdims=True))
    grad_0 = ((jnp.exp(mine_0 - total_0) - target) * used_mine).astype(BF)
    grad_unit = jnp.concatenate([dot(grad_0, u1), dot(grad_1, u0)], axis=0) * (1.0 / SOFTMAX_TEMP)
    final_s = cls[FIN : FIN + 16, :]
    hat2 = cls[HAT2 : HAT2 + 16, :]
    pull = jnp.sum(grad_unit * final_s, axis=-1, keepdims=True)
    grad_final = (grad_unit - final_s * (pull * length * length)) * length * used16

    grad_mixed_two = norm_back(grad_final * gain(1), hat2, scale2)
    grad_ffn = (grad_mixed_two * cls[KEEP2 : KEEP2 + 16, :]).astype(BF)
    f4[2 * z + c, 2 * y + x] = grad_ffn
    start_z(4)
    start_xy(4, 0)
    grad_pre = (dot(grad_ffn, wout[...], LAST) * gelu_slope(pre_s[...])).astype(BF)
    grad_normed = dot(grad_pre, win[...], LAST) + grad_mixed_two
    hat1 = cls[HAT1 : HAT1 + 16, :]
    grad_mixed = norm_back(grad_normed * gain(0), hat1, scale1)
    dropped = grad_mixed * cls[KEEP1 : KEEP1 + 16, :]
    grad_branch = (dropped[0:8] + dropped[8:16]).astype(BF)
    grad_ctx = dot(grad_branch, wqp[:, 2304:3072], LAST).astype(BF)
    loop(1, 4, lambda r: wait_z_start_xy(4, r))
    grad_big = spread(grad_ctx.astype(F32))
    query_big = spread(cls[QRY : QRY + 8, :])
    grad_probs = dot(grad_big, qkv[:, 1536:2304], LAST)
    prob = p_f[...]
    weighted = prob * grad_probs
    grad_scores = (weighted - prob * jnp.sum(weighted, axis=-1, keepdims=True)).astype(BF)
    pairs[0:96, :] = grad_scores
    grad_q = (gathered(dot(grad_scores, qkv[:, 768:1536])) * HD**-0.5).astype(BF)
    own5 = f5.at[2 * z + c, 2 * y + x]
    own5[:, 0:768] = jnp.concatenate([grad_branch.astype(F32), grad_ctx.astype(F32)], axis=0).astype(BF)
    own5[:, 768:1536] = jnp.concatenate([grad_q.astype(F32), cls[QRY : QRY + 8, :]], axis=0).astype(BF)
    start_z(5)
    start_xy(5, 0)
    wait_boxes(early, s_early)
    mixer[0:96, :] = dot(grad_scores, tokens[...])
    value_sum = jnp.sum(pairs[96:192, :].astype(F32), axis=-1, keepdims=True)
    own_sums = [
        jnp.sum(value_sum * grad_big.astype(F32), axis=0, keepdims=True),
        jnp.sum(grad_normed, axis=0, keepdims=True),
        jnp.sum(grad_final, axis=0, keepdims=True),
        jnp.sum(grad_normed * hat1, axis=0, keepdims=True),
        jnp.sum(grad_final * hat2, axis=0, keepdims=True),
    ]
    mixer[96:128, :] = jnp.zeros((32, 768), F32)
    for j, v in enumerate(own_sums):
        upper = v.astype(BF).astype(F32)
        mixer[96 + j : 97 + j, :] = upper
        mixer[104 + j : 105 + j, :] = v - upper
    send_mixer(late, late_in, s_late, r_late)
    slopes(1)
    loop(0, 4, lambda r: wait_xy_start_ab(4, r))
    slopes(2)
    loop(1, 4, lambda r: wait_z_start_xy(5, r))
    loop(0, 4, lambda r: wait_ab_start_c(4, r))
    loop(11, 12, ffn_in)
    ffn_out(0)
    loop(0, 4, lambda r: wait_xy_start_ab(5, r))
    for ph in (0, 1, 2, 3, 6):
        sent(ph)

    through[0:96, :] = dot(query_big, wqp[:, 768:1536], LAST).astype(BF)
    through[96:192, :] = dot(grad_big, wqp[:, 1536:2304], LAST).astype(BF)
    start_grad = grad_mixed[0:8] + grad_mixed[8:16] + dot(grad_q, wqp[:, 0:768], LAST)
    upper = start_grad.astype(BF).astype(F32)
    through[192:208, :] = jnp.concatenate([upper, start_grad - upper], axis=0).astype(BF)

    def token_grad(i):
        columns = pl.ds(pl.multiple_of(256 * i, 256), 256)
        gtok[:, columns] = dot(pairs[...], through[:, columns], FIRST)

    loop(0, 3, token_grad)
    token_copy = pltpu.make_async_copy(gtok, gtok_hbm, s_tok)
    token_copy.start()
    loop(0, 4, lambda r: wait_ab_start_c(5, r))
    wait_boxes(actw_in, r_act)
    act_mine = dot(actw_in[...].reshape(512, 256), as_number(hot_back(256, 128, (96 * me) % 128)).astype(BF))
    act_mine = jnp.where(lanes((512, 128), 1) == 96, 1.0, act_mine).astype(BF)
    loop(0, 4, lambda r: wait_c(4, r))
    ffn_out(1)

    out_rows = dot(act_mine, f4[...].reshape(512, 768), FIRST)
    g_out[...] = out_rows[0:96]
    g_out_copy = pltpu.make_async_copy(g_out, g_out_hbm, s_own.at[2])
    g_out_copy.start()
    sums[...] = jnp.zeros_like(sums)
    sums[4:5, 0:768] = out_rows[96:97]

    mix_copy.wait_recv()

    def in_rows(i):
        here = pl.ds(pl.multiple_of(768 * i, 256), 768)
        to = pl.ds(pl.multiple_of(1536 * c + 768 * i, 256), 768)
        grad_act = dot(f4[...].reshape(512, 768), wout[to, :], LAST)
        grad_pre = (grad_act * slope[:, here].astype(F32)).astype(BF)
        rows = dot(mix_n[...], grad_pre, FIRST)
        g_in[:, to] = rows[0:24]
        sums[8:16, to] = rows[24:32]
        half_s[:, here] = dot(mix_o[...], grad_pre, FIRST)

    loop(0, 2, in_rows)
    half_copy.start()
    ffn_out(2)
    ffn_out(3)
    half_copy.wait_recv()
    there = pl.ds(pl.multiple_of(1536 * (1 - c), 256), 1536)
    g_in[:, there] = half_r[0:24, :]
    sums[8:16, there] = half_r[24:32, :]
    g_in_copy = pltpu.make_async_copy(g_in, g_in_hbm, s_own.at[3])
    g_in_copy.start()
    loop(0, 4, lambda r: wait_c(5, r))
    rows = dot(mix_c[...], f5[:, :, :, 0:768].reshape(512, 768), FIRST)
    g_proj[...] = rows[0:24]
    sums[2:3, 0:768] = rows[24:25]
    rows = dot(mix_t[...], f5[:, :, :, 768:1536].reshape(512, 768), FIRST)
    g_qkv[:, 0:768] = rows[0:24]
    sums[0:1, 0:768] = rows[24:25]

    def value_rows(g):
        total = dot(early_in[4 * g][:, 0:96], spread(f5[g, 0, :, 0:768].astype(F32)[8:16]))
        for i in range(1, 4):
            total += dot(early_in[4 * g + i][:, 0:96], spread(f5[g, i, :, 0:768].astype(F32)[8:16]))
        unit0[0:32, :] += total

    unit0[0:64, :] = jnp.zeros((64, 768), F32)
    loop(0, 8, value_rows)
    wait_boxes(late_in, r_late)
    rest[...] = jnp.zeros_like(rest)

    def key_rows(g):
        total = dot(late_in[4 * g][:, 0:96], spread(f5[g, 0, :, 768:1536].astype(F32)[8:16]))
        extra = late_in[4 * g].astype(F32)
        for i in range(1, 4):
            total += dot(late_in[4 * g + i][:, 0:96], spread(f5[g, i, :, 768:1536].astype(F32)[8:16]))
            extra += late_in[4 * g + i].astype(F32)
        unit0[32:64, :] += total
        rest[...] += extra

    loop(0, 8, key_rows)
    g_qkv[:, 768:1536] = unit0[32:56, :]
    g_qkv[:, 1536:2304] = unit0[0:24, :]
    turned = jnp.transpose(rest[...])
    near = sums[0:8, pl.ds(pl.multiple_of(128 * ((24 * me) // 128), 128), 256)]
    stage[0:8, 0:24] = dot_exact(near, as_number(hot_back(256, 24, (24 * me) % 128)))
    for j, row in enumerate((1, 3, 5, 6, 7)):
        stage[row : row + 1, 0:24] = (turned[96 + j : 97 + j, :] + turned[104 + j : 105 + j, :])[:, 0:24]
    g_bias[...] = stage[0:6, 0:24]
    g_gain[...] = stage[6:8, 0:24]
    near = sums[8:16, pl.ds(pl.multiple_of(128 * ((96 * me) // 128), 128), 256)]
    g_fbias[...] = dot_exact(near, as_number(hot_back(256, 96, (96 * me) % 128)))[0:1]

    sent(4)
    sent(5)
    mix_copy.wait_send()
    half_copy.wait_send()
    wait_boxes(actw_in, s_act)
    wait_boxes(late, s_late)
    token_copy.wait()
    g_out_copy.wait()
    g_in_copy.wait()
    for i in range(4):
        rows = pl.ds(256 * (i % 2), 256)
        pltpu.make_async_copy(nlow.at[pl.ds(256 * i, 256)], hidden_hbm.at[i // 2, rows], s_hid.at[i]).wait()


def hot_back(rows, columns, shift):
    row = lax.broadcasted_iota(jnp.int32, (rows, columns), 0)
    column = lax.broadcasted_iota(jnp.int32, (rows, columns), 1)
    return row == column + shift


def dot_exact(a, b, dims=((1,), (0,))):
    return lax.dot_general(a, b, (dims, ((), ())), preferred_element_type=F32, precision=HIGH)


def hand_over(*refs):
    n = len(refs) // 3
    here, there, held = refs[:n], refs[n : 2 * n], refs[2 * n : 3 * n]
    s_in, s_out = refs[3 * n :]
    parts = []
    for i in range(n):
        rows = here[i].shape[-2]
        cuts = range(0, rows, rows // 4) if rows == 512 else [0]
        for at in cuts:
            size = rows // len(cuts)
            where = (slice(None),) * (len(here[i].shape) - 2) + (pl.ds(at, size),)
            parts.append([ref[i].at[where] for ref in (here, held, there)])
    loads = [pltpu.make_async_copy(p[0], p[1], s_in.at[k]) for k, p in enumerate(parts)]
    stores = [pltpu.make_async_copy(p[1], p[2], s_out.at[k]) for k, p in enumerate(parts)]
    for load in loads:
        load.start()
    for load, store in zip(loads, stores):
        load.wait()
        store.start()
    for store in stores:
        store.wait()


def encoder_step(
    tokens, qkv_weight, proj_weight, ffn_in_weight, ffn_out_weight, bias_rows, ffn_bias, norm_gains, buckets, padding, dropout
):
    def vm(*shape):
        return pltpu.VMEM(shape, BF)

    def vf(*shape):
        return pltpu.VMEM(shape, F32)

    def sems(*shape):
        return pltpu.SemaphoreType.DMA(shape)

    one = pltpu.SemaphoreType.DMA
    inside = pl.BlockSpec(memory_space=pltpu.VMEM)
    anywhere = pl.BlockSpec(memory_space=pl.ANY)
    engine = [sems(7, 4)] * 6 + [sems(4)]
    out = pl.pallas_call(
        encoder_kernel,
        name="encoder_step",
        out_shape=[
            jax.ShapeDtypeStruct((2, 512, 768), BF),
            jax.ShapeDtypeStruct((1, 1), F32),
            jax.ShapeDtypeStruct((512, 768), F32),
            jax.ShapeDtypeStruct((24, 2304), F32),
            jax.ShapeDtypeStruct((24, 768), F32),
            jax.ShapeDtypeStruct((24, 3072), F32),
            jax.ShapeDtypeStruct((96, 768), F32),
            jax.ShapeDtypeStruct((6, 24), F32),
            jax.ShapeDtypeStruct((1, 96), F32),
            jax.ShapeDtypeStruct((2, 24), F32),
        ],
        in_specs=[inside] * 3 + [anywhere] + [inside] * 3 + [anywhere] + [inside] * 2 + [anywhere],
        out_specs=[anywhere, inside, anywhere] + [inside] * 2 + [anywhere] * 2 + [inside] * 3,
        scratch_shapes=[
            vm(768, PW), vm(768, 3072), vm(3072, 768),
            vm(4, 2, 2, 16, WIDE + SW), vm(4, 2, 2, 16, WIDE), vm(4, 2, 2, 16, WIDE),
            vm(8, 4, 16, 768), vm(8, 4, 16, 768), vm(8, 4, 16, 1536), vm(8, 4, 16, 768),
            vm(8, 4, 16, SW), vf(16, SW), vf(16, 3328),
            pltpu.VMEM((2, 512, 768), jnp.int32), vm(512, 2304), vf(512, 512), vm(512, 768),
            vf(2, 512, 768), vm(1024, 768), vm(1024, 3072),
            vf(120, 768), vf(8, 512), vm(8, 512), vf(16, 3072), vm(16, 3200), vf(96, 512),
            vm(208, 512), vm(208, 768), vf(128, 768), vf(768, 128), vf(256, 768), vf(256, 768), vf(16, 3328),
            vm(32, 32, 128), vm(32, 32, 128), vm(32, 32, 128), vm(32, 32, 128), vm(32, 16, 256),
            vf(512, 768), vm(768, 512), vm(512, 256),
            vm(512, 32), vm(512, 32), vm(512, 32), vf(32, 128), vm(512, 1536), vm(512, 32), vf(32, 1536), vf(32, 1536),
            vm(512, 768), vm(96, 768), vf(24, 3072), vf(96, 768),
        ] + engine + engine + [one] * 6 + [sems(2), sems(4)] + [one] * 5 + [sems(4)],
        compiler_params=pltpu.CompilerParams(
            collective_id=0, has_side_effects=True, vmem_limit_bytes=63 * 2**20
        ),
    )(
        qkv_weight, proj_weight, ffn_in_weight, ffn_out_weight, bias_rows, norm_gains,
        ffn_bias[None], tokens, buckets, padding[None], dropout,
    )
    out = pl.pallas_call(
        hand_over,
        name="hand_over",
        out_shape=[jax.ShapeDtypeStruct(o.shape, o.dtype) for o in out],
        in_specs=[anywhere] * 10,
        out_specs=[anywhere] * 10,
        scratch_shapes=[pltpu.VMEM(o.shape, o.dtype) for o in out] + [sems(16), sems(16)],
        compiler_params=pltpu.CompilerParams(vmem_limit_bytes=60 * 2**20),
    )(*out)
    hidden, loss, gtok, g_qkv, g_proj, g_in, g_out, g_bias, g_fbias, g_gain = out
    return (hidden, loss[0, 0], gtok, g_qkv, g_proj, g_in, g_out, g_bias, g_fbias[0], g_gain)


def solution(mesh):
    in_specs = (
        P(AXES, None),
        P(AXES, None),
        P(AXES, None),
        P(AXES, None),
        P(AXES, None),
        P(None, AXES),
        P(AXES),
        P(None, AXES),
        P(AXES, None),
        P(AXES),
        P(None, None, AXES, None),
    )
    out_specs = (
        P(None, AXES, None),
        P(),
        P(AXES, None),
        P(AXES, None),
        P(AXES, None),
        P(AXES, None),
        P(AXES, None),
        P(None, AXES),
        P(AXES),
        P(None, AXES),
    )
    grid_fits = mesh.shape["dp"] == 8 and mesh.shape["fsdp"] == 4
    return jax.shard_map(
        encoder_step if grid_fits else with_collectives, mesh=mesh, in_specs=in_specs, out_specs=out_specs, check_vma=False
    )
```
